32 devices in a mesh: dp: 16 (over z, x, core), tensor: 2 (over y).
Axes of the slice: x: 2, y: 2, z: 4, core: 2. Of those that a mesh axis runs over, the one named last changes fastest.
Arguments:
- block_input: bfloat16 [32, 3136, 256], P('dp', 'tensor'), may hold values from -6 to 6
- heights: int32 [32], P('dp'), may hold values from 7 to 56, as said below
- widths: int32 [32], P('dp'), may hold values from 7 to 56, as said below
- norm1_gain: float32 [256], replicated, may hold values from 0.25 to 1.75
- norm1_bias: float32 [256], replicated, may hold values from -1.75 to 1.75
- qkv_weight: bfloat16 [256, 3, 2, 128], P(None, None, None, 'tensor'), may hold values from -0.375 to 0.375
- lepe_weight: bfloat16 [2, 9, 128], P(None, None, 'tensor'), may hold values from -1.75 to 1.75
- lepe_bias: bfloat16 [2, 128], P(None, 'tensor'), may hold values from -1.75 to 1.75
- proj_weight: bfloat16 [2, 128, 256], P(None, 'tensor'), may hold values from -0.5 to 0.5
- proj_bias: bfloat16 [256], replicated, may hold values from -1.75 to 1.75
- norm2_gain: float32 [256], replicated, may hold values from 0.25 to 1.75
- norm2_bias: float32 [256], replicated, may hold values from -1.75 to 1.75
- fc1_weight: bfloat16 [256, 1024], P(None, 'tensor'), may hold values from -0.375 to 0.375
- fc1_bias: bfloat16 [1024], P('tensor'), may hold values from -1.75 to 1.75
- fc2_weight: bfloat16 [1024, 256], P('tensor'), may hold values from -0.1875 to 0.1875
- fc2_bias: bfloat16 [256], replicated, may hold values from -1.75 to 1.75
- cotangent: bfloat16 [32, 3136, 256], P('dp', 'tensor'), may hold values from -6 to 6
Outputs:
- output: bfloat16 [32, 3136, 256], P('dp', 'tensor')
- input_grad: bfloat16 [32, 3136, 256], P('dp', 'tensor')
- grad_norm1_gain: float32 [256], replicated
- grad_norm1_bias: float32 [256], replicated
- grad_qkv_weight: float32 [256, 3, 2, 128], P(None, None, None, 'tensor')
- grad_lepe_weight: float32 [2, 9, 128], P(None, None, 'tensor')
- grad_lepe_bias: float32 [2, 128], P(None, 'tensor')
- grad_proj_weight: float32 [2, 128, 256], P(None, 'tensor')
- grad_proj_bias: float32 [256], replicated
- grad_norm2_gain: float32 [256], replicated
- grad_norm2_bias: float32 [256], replicated
- grad_fc1_weight: float32 [256, 1024], P(None, 'tensor')
- grad_fc1_bias: float32 [1024], P('tensor')
- grad_fc2_weight: float32 [1024, 256], P('tensor')
- grad_fc2_bias: float32 [256], replicated
The draws below stay inside these ranges and needn't reach their ends.
Inputs may be any that keep to these rules, and one draw needn't show every extreme that they name: `heights`: in every aligned block of 2 images one image has height 56. `widths`: in every aligned block of 2 images one image has width 56.
All inputs are finite; a program needn't handle non-finite values.
Results may differ from the reference program's by a relative error of at most 0.015.
Values may be sent and summed in bfloat16 or wider, within the bound.
No kernel may reach another device: no remote copies, remote signals or barrier semaphores. Data moves between devices by JAX's collectives and lax.ppermute only.
A program may use at most 256 MiB of HBM per device.

```python
import jax
import jax.numpy as jnp
from jax import lax

D = 256
FF = 1024
HEAD_DIM = 32
STRIPE = 7
PH = 56
PW = 56
IMG_DEV = 2
BR = 128
CELLS = 3136
IMAGES = 32


def draw_side(key, side_limit):
    first_key, second_key = jax.random.split(key)
    side_cells = jax.random.randint(first_key, (IMAGES,), STRIPE, side_limit + 1)
    chosen = jax.random.randint(second_key, (IMAGES // IMG_DEV,), 0, IMG_DEV)
    places = jnp.arange(IMAGES // IMG_DEV, dtype=jnp.int32) * IMG_DEV + chosen
    return side_cells.at[places].set(side_limit).astype(jnp.int32)


def draw_heights(key, part):
    key = jax.random.fold_in(key, 5)
    return draw_side(key, PH)


def draw_widths(key, part):
    key = jax.random.fold_in(key, 9)
    return draw_side(key, PW)


def level_of(key, extent, cuts, low, top_value):
    factor_of, own = 1.0, jax.random.fold_in(key, 6)
    for position, parts in cuts:
        steps = jnp.exp(jax.random.uniform(jax.random.fold_in(own, position), (parts,), jnp.float32, low / len(cuts), top_value / len(cuts)))
        factor_of = factor_of * jnp.repeat(steps, extent[position] // parts).reshape([-1 if axis == position else 1 for axis in range(len(extent))])
    return factor_of


def scatter_about(rng, extent, width, most, cuts=(), kind=jnp.bfloat16):
    entries = jax.random.normal(rng, extent, jnp.float32) * width
    if len(cuts) > 0:
        entries = level_of(rng, extent, cuts, -0.22, 0.18) * entries
    return jnp.clip(entries, min=-most, max=most).astype(kind)


def setup_inputs(seed: int = 0) -> dict:
    seeds = jax.random.split(jax.random.key(seed), 18)
    return {
        "block_input": scatter_about(seeds[0], (IMAGES, CELLS, D), 1.0, 6.0, ((0, 16), (1, 2))),
        "heights": draw_heights(jax.random.fold_in(seeds[17], 71), 0),
        "widths": draw_widths(jax.random.fold_in(seeds[17], 71), 0),
        "norm1_gain": jnp.clip(1.0 + 0.15 * jax.random.normal(seeds[3], (D,), jnp.float32), 0.25, 1.75),
        "norm1_bias": scatter_about(seeds[4], (D,), 0.3, 1.75, (), jnp.float32),
        "qkv_weight": scatter_about(seeds[5], (D, 3, 2, BR), D ** -0.5, 0.375, ((3, 2),)),
        "lepe_weight": scatter_about(seeds[6], (2, 9, BR), 0.3, 1.75, ((2, 2),)),
        "lepe_bias": scatter_about(seeds[7], (2, BR), 0.3, 1.75, ((1, 2),)),
        "proj_weight": scatter_about(seeds[8], (2, BR, D), (D // 2) ** -0.5, 0.5, ((1, 2),)),
        "proj_bias": scatter_about(seeds[9], (D,), 0.3, 1.75),
        "norm2_gain": jnp.clip(1.0 + 0.15 * jax.random.normal(seeds[10], (D,), jnp.float32), 0.25, 1.75),
        "norm2_bias": scatter_about(seeds[11], (D,), 0.3, 1.75, (), jnp.float32),
        "fc1_weight": scatter_about(seeds[12], (D, FF), D ** -0.5, 0.375, ((1, 2),)),
        "fc1_bias": scatter_about(seeds[13], (FF,), 0.3, 1.75, ((0, 2),)),
        "fc2_weight": scatter_about(seeds[14], (FF, D), FF ** -0.5, 0.1875, ((0, 2),)),
        "fc2_bias": scatter_about(seeds[15], (D,), 0.3, 1.75),
        "cotangent": scatter_about(seeds[16], (IMAGES, CELLS, D), 1.0, 6.0, ((0, 16), (1, 2))),
    }


MASKED = -30.0
EPSILON = 1e-05
HIGHEST = lax.Precision.HIGHEST

@jax.custom_vjp
def low(v):
    return lax.optimization_barrier(v.astype(jnp.bfloat16)).astype(jnp.float32)

@jax.custom_vjp
def low_back(v):
    return v

def low_keep(v):
    return (low(v), None)

def low_pass(kept, grad):
    return (grad,)

def back_keep(v):
    return (v, None)

def back_low(kept, grad):
    return (low(grad),)
low.defvjp(low_keep, low_pass)
low_back.defvjp(back_keep, back_low)

def image_masks(heights, widths):
    cell_index = jnp.arange(PH * PW, dtype=jnp.int32)
    inside = ((cell_index // PW)[None, :] < heights[:, None]) & ((cell_index % PW)[None, :] < widths[:, None])
    return inside.astype(jnp.float32)

def layer_norm(values, gain, shift):
    centred = values - lax.optimization_barrier(jnp.mean(values, -1, keepdims=True))
    inverse = lax.rsqrt(lax.optimization_barrier(jnp.mean(centred * centred, -1, keepdims=True)) + EPSILON)
    return centred * inverse * gain + shift

def window_shape(across):
    if across:
        return (STRIPE, PW)
    return (PH, STRIPE)

def to_windows(values, across):
    leading = values.shape[0]
    trailing = values.shape[2:]
    if across:
        return values.reshape((leading, PH // STRIPE, STRIPE * PW) + trailing)
    layout = values.reshape((leading, PH, PW // STRIPE, STRIPE) + trailing)
    permuted = (0, 2, 1, 3) + tuple(range(4, layout.ndim))
    return layout.transpose(permuted).reshape((leading, PW // STRIPE, PH * STRIPE) + trailing)

def from_windows(values, across):
    leading = values.shape[0]
    trailing = values.shape[3:]
    if across:
        return values.reshape((leading, PH * PW) + trailing)
    layout = values.reshape((leading, PW // STRIPE, PH, STRIPE) + trailing)
    permuted = (0, 2, 1, 3) + tuple(range(4, layout.ndim))
    return layout.transpose(permuted).reshape((leading, PH * PW) + trailing)

def split_heads(values, head_count):
    return values.reshape(values.shape[:-1] + (head_count, HEAD_DIM))

def lepe_apply(values, lepe_taps, win_h, win_w):
    leading = values.shape[:2]
    channels = values.shape[-1]
    spatial = values.reshape(leading + (win_h, win_w, channels))
    padded = jnp.pad(spatial, ((0, 0), (0, 0), (1, 1), (1, 1), (0, 0)))
    result = jnp.zeros_like(spatial)
    for shift_y in range(3):
        for shift_x in range(3):
            result = result + lepe_taps[shift_y * 3 + shift_x] * padded[:, :, shift_y:shift_y + win_h, shift_x:shift_x + win_w]
    return result.reshape(values.shape)

def branch_mix(queries, key_rows, value_rows, valid_keys, lepe_taps, lepe_shift, across):
    head_count = queries.shape[-1] // HEAD_DIM
    win_h, win_w = window_shape(across)
    query_win = split_heads(to_windows(queries, across), head_count)
    key_win = split_heads(to_windows(key_rows, across), head_count)
    value_win = to_windows(value_rows, across)
    valid_win = to_windows(valid_keys, across)
    scores = jnp.einsum('islhd,ismhd->ishlm', query_win, key_win, precision=HIGHEST)
    scores = low_back(jnp.where(valid_win[:, :, None, None, :], scores, MASKED))
    weights = low(jax.nn.softmax(scores, axis=-1))
    attended = jnp.einsum('ishlm,ismhd->islhd', weights, split_heads(value_win, head_count), precision=HIGHEST)
    mixed_win = attended.reshape(value_win.shape) + lepe_apply(value_win, lepe_taps, win_h, win_w) + lepe_shift
    return from_windows(mixed_win, across)

def forward(param_set, inputs, masks):
    gain1, shift1, qkv_w, lepe_w, lepe_b, proj_w, proj_b, gain2, shift2, fc1_w, fc1_b, fc2_w, fc2_b = param_set
    group_size = inputs.shape[0]
    branch_width = qkv_w.shape[3]
    mask_rows = masks[..., None]
    x_in = inputs * mask_rows
    normed1 = low(layer_norm(x_in, gain1, shift1))
    projected = jnp.einsum('gcd,de->gce', normed1, qkv_w.reshape(D, 6 * branch_width), precision=HIGHEST)
    projected = low_back(projected).reshape(group_size, PH * PW, 3, 2, branch_width)
    queries = low(projected[:, :, 0] * HEAD_DIM ** (-0.5))
    key_rows = low(projected[:, :, 1])
    value_rows = low(projected[:, :, 2])
    valid_keys = masks > 0.5
    mixed_rows = jnp.stack([branch_mix(queries[:, :, branch], key_rows[:, :, branch], value_rows[:, :, branch], valid_keys, lepe_w[branch], lepe_b[branch], branch == 0) for branch in range(2)], 2)
    mixed_low = low(low_back(mixed_rows))
    attn_out = low_back(jnp.einsum('gcbe,bed->gcd', mixed_low, proj_w, precision=HIGHEST)) + proj_b
    x_mid = x_in + attn_out
    normed2 = low(layer_norm(x_mid, gain2, shift2))
    hidden_pre = low_back(jnp.einsum('gcd,df->gcf', normed2, fc1_w, precision=HIGHEST) + fc1_b)
    hidden_low = low(jax.nn.gelu(hidden_pre, approximate=False))
    mlp_out = low_back(jnp.einsum('gcf,fd->gcd', hidden_low, fc2_w, precision=HIGHEST)) + fc2_b
    return mask_rows * (x_mid + mlp_out)

def reference(block_input, heights, widths, norm1_gain, norm1_bias, qkv_weight, lepe_weight, lepe_bias, proj_weight, proj_bias, norm2_gain, norm2_bias, fc1_weight, fc1_bias, fc2_weight, fc2_bias, cotangent):
    params = tuple((weight_item.astype(jnp.float32) for weight_item in (norm1_gain, norm1_bias, qkv_weight, lepe_weight, lepe_bias, proj_weight, proj_bias, norm2_gain, norm2_bias, fc1_weight, fc1_bias, fc2_weight, fc2_bias)))
    masks = image_masks(heights, widths)
    group_size = 1
    blocks = IMAGES // group_size
    inputs = block_input.astype(jnp.float32).reshape(blocks, group_size, PH * PW, D)
    cotangents = cotangent.astype(jnp.float32).reshape(blocks, group_size, PH * PW, D)
    block_masks = masks.reshape(blocks, group_size, PH * PW)

    def one_block(totals, block_items):
        block_x, block_cot, block_mask = block_items

        def closed(param_set, inputs_now):
            return forward(param_set, inputs_now, block_mask)
        result, pullback = jax.vjp(closed, params, block_x)
        grad_params, grad_x = pullback(block_cot)
        totals = jax.tree.map(lambda left_sum, right_sum: left_sum + right_sum, totals, grad_params)
        return (totals, (result.astype(jnp.bfloat16), grad_x.astype(jnp.bfloat16)))
    zeros = tuple((jnp.zeros_like(weight_item) for weight_item in params))
    totals, (results, grad_inputs) = lax.scan(one_block, zeros, (inputs, cotangents, block_masks))
    grad_gain1, grad_shift1, grad_qkv, grad_lepe_w, grad_lepe_b, grad_proj, grad_proj_b, grad_gain2, grad_shift2, grad_fc1, grad_fc1_b, grad_fc2, grad_fc2_b = totals
    output = results.reshape(IMAGES, PH * PW, D)
    input_grad = grad_inputs.reshape(IMAGES, PH * PW, D)
    return (output, input_grad, grad_gain1, grad_shift1, grad_qkv, grad_lepe_w, grad_lepe_b, grad_proj, grad_proj_b, grad_gain2, grad_shift2, grad_fc1, grad_fc1_b, grad_fc2, grad_fc2_b)
```

```python
from functools import partial

import jax
import jax.numpy as jnp
from jax import lax
from jax.experimental import pallas as pl
from jax.experimental.pallas import tpu as pltpu
from jax.sharding import PartitionSpec as P

HEAD_DIM = 32
STRIPE = 7
PH = 56
PW = 56
HEADS = 4
BR = HEADS * HEAD_DIM
WIN = STRIPE * PW
WIDE = HEADS * WIN
MAIN = WIN // 128 * 128
REST = WIN - MAIN
HALF = 28
PAIR = 2 * WIN
CHUNK = 256
CHUNKS = [(lo, min(lo + CHUNK, WIDE)) for lo in range(0, WIDE, CHUNK)]

MASKED = -30.0
EPSILON = 1e-05
LOG2E = 1.4426950408889634
LN2 = 0.6931471805599453
DENSITY = 0.3989422804014327
DEN_LOW = 2.0**-60
DEN_HIGH = 2.0**100

F32 = jnp.float32
BF16 = jnp.bfloat16
VMEM_LIMIT = 56 * 2**20


def dot(a, b):
    return jnp.dot(a, b, preferred_element_type=F32)


def dot_nt(a, b):
    return lax.dot_general(a, b, (((1,), (1,)), ((), ())), preferred_element_type=F32)


def dot_tn(a, b):
    return lax.dot_general(a, b, (((0,), (0,)), ((), ())), preferred_element_type=F32)


def split_index(count, width, lanes, axis=0):
    shape = (count, lanes) if axis == 0 else (lanes, count)
    index = lax.broadcasted_iota(jnp.int32, shape, axis)
    step = -(-65536 // width)
    major = lax.shift_right_logical(index * step, 16)
    return major, index - major * width


def inside(parts, base_major, base_minor, lim_major, lim_minor):
    major, minor = parts
    return (major < lim_major - base_major) & (minor < lim_minor - base_minor)


def as_float(flag):
    return jnp.where(flag, 1.0, 0.0).astype(F32)


def twice(values):
    return jnp.concatenate([values, values], axis=1)


def head_lane(head):
    lane = lax.broadcasted_iota(jnp.int32, (1, BR), 1)
    return as_float((lane >= head * HEAD_DIM) & (lane < (head + 1) * HEAD_DIM))


def head_blocks(values):
    lanes = [head_lane(head) for head in range(HEADS)]
    top = [values[:MAIN] * lane for lane in lanes]
    rest = [values[MAIN:] * lane for lane in lanes]
    return jnp.concatenate(top + rest, axis=0)


def from_wide(values):
    rows = []
    for head in range(HEADS):
        own = values[head * HEAD_DIM : (head + 1) * HEAD_DIM]
        rest = HEADS * MAIN + head * REST
        rows.append(
            jnp.concatenate(
                [own[:, head * MAIN : (head + 1) * MAIN], own[:, rest : rest + REST]], axis=1
            )
        )
    return jnp.concatenate(rows, axis=0)


def norm_parts(values):
    centred = values - jnp.mean(values, -1, keepdims=True)
    inverse = lax.rsqrt(jnp.mean(centred * centred, -1, keepdims=True) + EPSILON)
    return centred * inverse, inverse


def norm_back(grad_rows, unit_rows, inverse, gain):
    scaled = grad_rows * gain
    return inverse * (
        scaled
        - jnp.mean(scaled, -1, keepdims=True)
        - unit_rows * jnp.mean(scaled * unit_rows, -1, keepdims=True)
    )


def neighbours(values):
    _, minor = split_index(WIN, PW, BR)
    before = jnp.where(minor == 0, 0.0, pltpu.roll(values, 1, 0))
    after = jnp.where(minor == PW - 1, 0.0, pltpu.roll(values, WIN - 1, 0))
    return before, after


def add_rows(low, mid, high):
    gap = jnp.zeros((PW, mid.shape[1]), F32)
    return (
        mid
        + jnp.concatenate([gap, low[: WIN - PW]], axis=0)
        + jnp.concatenate([high[PW:], gap], axis=0)
    )


def lepe_apply(values, taps):
    before, after = neighbours(values)
    rows = [
        taps[3 * a : 3 * a + 1] * before
        + taps[3 * a + 1 : 3 * a + 2] * values
        + taps[3 * a + 2 : 3 * a + 3] * after
        for a in range(3)
    ]
    return add_rows(rows[0], rows[1], rows[2])


def lepe_back(grads, values, taps):
    before, after = neighbours(grads)
    rows = [
        taps[3 * a : 3 * a + 1] * after
        + taps[3 * a + 1 : 3 * a + 2] * grads
        + taps[3 * a + 2 : 3 * a + 3] * before
        for a in range(3)
    ]
    back = add_rows(rows[2], rows[1], rows[0])
    value_before, value_after = neighbours(values)
    tap_rows = []
    for a in range(3):
        for item in (value_before, values, value_after):
            if a == 0:
                product = grads[PW:] * item[: WIN - PW]
            elif a == 1:
                product = grads * item
            else:
                product = grads[: WIN - PW] * item[PW:]
            tap_rows.append(jnp.sum(product, 0, keepdims=True))
    tap_rows.append(jnp.sum(grads, 0, keepdims=True))
    return back, tap_rows


def window_valid(window_base, lim_major, lim_minor):
    return inside(split_index(WIN, PW, BR), window_base, 0, lim_major, lim_minor)


def window_forward(projected, valid, taps, shift, k, refs):
    p_ref, q_ref, k_ref, v_ref, o_ref, rl_ref, kb_ref, vb_ref, lepe_ref, mixed_ref = refs
    queries = (projected[:, :BR] * (HEAD_DIM**-0.5 * LOG2E)).astype(BF16)
    key_rows = projected[:, BR : 2 * BR]
    values = projected[:, 2 * BR :].astype(BF16).astype(F32)
    valid_float = as_float(valid)
    weight = jnp.where(valid, 1.0, jnp.exp(jnp.full((WIN, BR), MASKED, F32)))
    q_ref[k] = queries
    k_ref[k] = (key_rows * valid_float).astype(BF16)
    v_ref[k] = values.astype(BF16)
    kb_ref[k] = head_blocks(key_rows * valid_float).astype(BF16)
    vb_ref[k, :, :BR] = head_blocks(values * weight).astype(BF16)
    vb_ref[k, :, BR:] = head_blocks(weight).astype(BF16)
    for lo, hi in CHUNKS:
        p_ref[k, :, lo:hi] = jnp.exp2(dot_nt(queries, kb_ref[k, lo:hi])).astype(BF16)
    sums = dot(p_ref[k], vb_ref[k])
    totals = sums[:, BR:]
    inverse = 1.0 / totals
    attended = sums[:, :BR] * inverse
    o_ref[k] = attended.astype(BF16)
    rl_ref[k] = inverse
    lepe = lepe_apply(values, taps) + shift
    lepe_ref[k] = lepe
    mixed_ref[k] = attended + lepe
    safe = (totals > DEN_LOW) & (totals < DEN_HIGH)
    return jnp.max(jnp.where(safe, 0.0, 1.0))


def window_forward_safe(k, refs, s_ref):
    p_ref, q_ref, k_ref, v_ref, o_ref, rl_ref, kb_ref, vb_ref, lepe_ref, mixed_ref = refs
    s_ref[...] = dot_nt(q_ref[k], kb_ref[k])
    for head in range(HEADS):
        cut = slice(head * MAIN, (head + 1) * MAIN)
        rest = HEADS * MAIN + head * REST
        left = s_ref[:, cut]
        right = s_ref[:, rest : rest + REST]
        peak = jnp.maximum(jnp.max(left, -1, keepdims=True), jnp.max(right, -1, keepdims=True))
        s_ref[:, cut] = left - peak
        s_ref[:, rest : rest + REST] = right - peak
    for lo, hi in CHUNKS:
        p_ref[k, :, lo:hi] = jnp.exp2(s_ref[:, lo:hi]).astype(BF16)
    sums = dot(p_ref[k], vb_ref[k])
    inverse = 1.0 / sums[:, BR:]
    attended = sums[:, :BR] * inverse
    o_ref[k] = attended.astype(BF16)
    rl_ref[k] = inverse
    mixed_ref[k] = attended + lepe_ref[k]


def window_backward(grads, valid, base, lim_major, lim_minor, taps, k, refs):
    p_ref, q_ref, k_ref, v_ref, o_ref, rl_ref, kb_ref, vb_ref, ds_ref = refs
    lane = lax.broadcasted_iota(jnp.int32, (WIN, BR), 1)
    scaled = (grads * rl_ref[k]).astype(BF16)
    product = scaled.astype(F32) * o_ref[k].astype(F32)
    high = product.astype(BF16)
    low = (product - high.astype(F32)).astype(BF16)
    row = lax.broadcasted_iota(jnp.int32, (2 * BR, BR), 0)
    col = lax.broadcasted_iota(jnp.int32, (2 * BR, BR), 1)
    head_of = lax.shift_right_logical(row & (BR - 1), 5)
    picks = as_float((col < 2 * HEADS) & (head_of == (col & (HEADS - 1)))).astype(BF16)
    inner = dot(jnp.concatenate([high, low], axis=1), picks)
    inner_high = inner.astype(BF16).astype(F32)
    extra = jnp.where(lane < HEADS, inner_high, inner - inner_high).astype(BF16)
    left = jnp.concatenate([scaled, extra], axis=1)
    values = v_ref[k].astype(F32)
    vb_ref[k, :, :BR] = head_blocks(values).astype(BF16)
    kb_ref[k] = head_blocks(k_ref[k].astype(F32)).astype(BF16)
    for lo, hi in CHUNKS:
        grad_probs = dot_nt(left, vb_ref[k, lo:hi])
        ds_ref[k, :, lo:hi] = grad_probs.astype(BF16) * p_ref[k, :, lo:hi]
    grad_query = dot(ds_ref[k], kb_ref[k]) * (HEAD_DIM**-0.5)
    query_t = q_ref[k].astype(F32).T.astype(BF16)
    scaled_t = scaled.astype(F32).T.astype(BF16)
    valid_t = inside(split_index(WIN, PW, BR, 1), base, 0, lim_major, lim_minor)
    weight_t = jnp.where(valid_t, 1.0, jnp.exp(jnp.full((BR, WIN), MASKED, F32)))
    grad_key = (from_wide(dot(query_t, ds_ref[k])) * jnp.where(valid_t, LN2, 0.0)).T
    grad_value = (from_wide(dot(scaled_t, p_ref[k])) * weight_t).T
    back, tap_rows = lepe_back(grads, values, taps)
    out = jnp.concatenate([grad_query, grad_key, grad_value + back], axis=1)
    return out.astype(BF16), tap_rows


def set_indicator(vb_ref):
    row = lax.broadcasted_iota(jnp.int32, (WIDE, BR), 0)
    col = lax.broadcasted_iota(jnp.int32, (WIDE, BR), 1)
    head = jnp.zeros((WIDE, BR), jnp.int32)
    for cut in range(1, HEADS):
        head = head + jnp.where(row >= cut * MAIN, 1, 0)
    tail = lax.shift_right_logical(row - HEADS * MAIN, 3)
    head = jnp.where(row >= HEADS * MAIN, tail, head)
    hit = (col < 2 * HEADS) & ((col & (HEADS - 1)) == head)
    for k in range(2):
        vb_ref[k, :, BR:] = jnp.where(hit, -1.0, 0.0).astype(BF16)


def split_columns(source, left, right):
    for row in range(STRIPE * 2):
        left[row * HALF : (row + 1) * HALF] = source[row * PW : row * PW + HALF]
        right[row * HALF : (row + 1) * HALF] = source[row * PW + HALF : (row + 1) * PW]


def merge_columns(left, right, target):
    for row in range(STRIPE * 2):
        target[row * PW : row * PW + HALF] = left[row * HALF : (row + 1) * HALF]
        target[row * PW + HALF : (row + 1) * PW] = right[row * HALF : (row + 1) * HALF]


def quadrant_kernel(sc, x_ref, own_ref, send_ref, whole, left, right):
    whole[...] = x_ref[0].astype(F32)
    split_columns(whole, left, right)
    first = sc[0] == 0
    own_ref[0] = jnp.where(first, left[...], right[...]).astype(BF16)
    send_ref[0] = jnp.where(first, right[...], left[...]).astype(BF16)


def rows_forward_kernel(
    sc, x_ref, gain_ref, bias_ref, w_ref, taps_ref, shift_ref,
    p_ref, q_ref, k_ref, v_ref, o_ref, rl_ref, m_ref,
    kb_ref, vb_ref, lepe_ref, mixed_ref, s_ref,
):
    step = pl.program_id(0)
    image, part = step // 2, step % 2
    height, width = sc[1 + 2 * image], sc[2 + 2 * image]
    row_base = sc[0] * HALF + part * 2 * STRIPE
    mask = as_float(inside(split_index(PAIR, PW, BR), row_base, 0, height, width))
    unit, _ = norm_parts(x_ref[0].astype(F32) * twice(mask))
    normed = (unit * gain_ref[...] + bias_ref[...]).astype(BF16)
    projected = dot(normed, w_ref[...])
    refs = (p_ref, q_ref, k_ref, v_ref, o_ref, rl_ref, kb_ref, vb_ref, lepe_ref, mixed_ref)
    bad = jnp.float32(0)
    for k in range(2):
        valid = window_valid(row_base + k * STRIPE, height, width)
        rows = projected[k * WIN : (k + 1) * WIN]
        bad = jnp.maximum(
            bad, window_forward(rows, valid, taps_ref[...], shift_ref[...], k, refs)
        )

    @pl.when(bad > 0.0)
    def _():
        for k in range(2):
            window_forward_safe(k, refs, s_ref)

    for k in range(2):
        m_ref[k] = mixed_ref[k].astype(BF16)


def columns_forward_kernel(
    image, sc, own_ref, other_ref, gain_ref, bias_ref, w_ref, taps_ref, shift_ref,
    p_ref, q_ref, k_ref, v_ref, o_ref, rl_ref, n_ref, keep_ref, send_ref,
    normed_ref, out_ref, kb_ref, vb_ref, lepe_ref, mixed_ref, s_ref,
):
    step = pl.program_id(0)
    place = sc[0]
    height, width = sc[1 + 2 * image], sc[2 + 2 * image]
    column_base = place * HALF

    @pl.when(step == 0)
    def _():
        for source, side in ((own_ref, place), (other_ref, 1 - place)):
            for s in range(2):
                flag = inside(
                    split_index(WIN, HALF, BR), side * HALF + s * 2 * STRIPE, column_base,
                    height, width,
                )
                unit, _ = norm_parts(source[s].astype(F32) * twice(as_float(flag)))
                start = pl.multiple_of(side * PAIR + s * WIN, 8)
                normed = unit * gain_ref[...] + bias_ref[...]
                normed_ref[0, pl.ds(start, WIN)] = normed[:, :BR]
                normed_ref[1, pl.ds(start, WIN)] = normed[:, BR:]

    refs = (p_ref, q_ref, k_ref, v_ref, o_ref, rl_ref, kb_ref, vb_ref, lepe_ref, mixed_ref)
    bad = jnp.float32(0)
    for k in range(2):
        column = (2 * step + k) * STRIPE
        halves = [
            jnp.concatenate(
                [normed_ref[j, pl.ds(column + q, PH, stride=HALF)] for q in range(STRIPE)], axis=0
            )
            for j in range(2)
        ]
        normed = jnp.concatenate(halves, axis=1).astype(BF16)
        n_ref[k] = normed
        valid = window_valid(column_base + column, width, height)
        rows = dot(normed, w_ref[...])
        bad = jnp.maximum(
            bad, window_forward(rows, valid, taps_ref[...], shift_ref[...], k, refs)
        )

    @pl.when(bad > 0.0)
    def _():
        for k in range(2):
            window_forward_safe(k, refs, s_ref)

    for k in range(2):
        column = (2 * step + k) * STRIPE
        mixed = mixed_ref[k]
        for q in range(STRIPE):
            out_ref[pl.ds(column + q, PH, stride=HALF)] = mixed[q * PH : (q + 1) * PH]

    @pl.when(step == 1)
    def _():
        for s in range(2):
            keep = pl.multiple_of(place * PAIR + s * WIN, 8)
            send = pl.multiple_of((1 - place) * PAIR + s * WIN, 8)
            keep_ref[s] = out_ref[pl.ds(keep, WIN)].astype(BF16)
            send_ref[s] = out_ref[pl.ds(send, WIN)].astype(BF16)


def mlp_kernel(
    image, first, sc, x_ref, cot_ref, mh_ref, mo_ref, mr_ref, *rest
):
    (
        pw_ref, pwt_ref, pb_ref, gain_ref, bias_ref, w1_ref, w1t_ref, b1_ref, w2_ref, w2t_ref, b2_ref,
    ) = rest[:11]
    rest = rest[11:]
    if not first:
        old1_ref, old2_ref, oldp_ref, olds_ref, oldb_ref = rest[:5]
        rest = rest[6:]
    (
        out_ref, gmid_ref, gh_ref, gk_ref, gs_ref, g1_ref, g2_ref, gp_ref, small_ref, gb1_ref,
        whole, left, right,
    ) = rest
    step = pl.program_id(0)
    place = sc[0]
    height, width = sc[1 + 2 * image], sc[2 + 2 * image]
    row_base = place * HALF + step * 2 * STRIPE

    @pl.when(step == 0)
    def _():
        if first:
            g1_ref[...] = jnp.zeros_like(g1_ref)
            g2_ref[...] = jnp.zeros_like(g2_ref)
            gp_ref[...] = jnp.zeros_like(gp_ref)
            small_ref[...] = jnp.zeros_like(small_ref)
            gb1_ref[...] = jnp.zeros_like(gb1_ref)
        else:
            g1_ref[...] = old1_ref[...]
            g2_ref[...] = old2_ref[...]
            gp_ref[...] = oldp_ref[...]
            small_ref[...] = olds_ref[...]
            gb1_ref[...] = oldb_ref[...]

    mask = twice(as_float(inside(split_index(PAIR, PW, BR), row_base, 0, height, width)))
    first_half = place == 0
    own = mo_ref[0].astype(F32)
    other = mr_ref[0].astype(F32)
    left[...] = jnp.where(first_half, own, other)
    right[...] = jnp.where(first_half, other, own)
    merge_columns(left, right, whole)
    rows_part = jnp.concatenate([mh_ref[0].astype(F32), mh_ref[1].astype(F32)], axis=0)
    mixed = jnp.concatenate([rows_part, whole[...]], axis=1).astype(BF16)
    x_in = x_ref[0].astype(F32) * mask
    x_mid = x_in + dot(mixed, pw_ref[...]) + pb_ref[...]
    unit, inverse = norm_parts(x_mid)
    normed = (unit * gain_ref[...] + bias_ref[...]).astype(BF16)
    grad_result = cot_ref[0].astype(F32) * mask
    grad_low = grad_result.astype(BF16)
    normed_t = normed.astype(F32).T.astype(BF16)
    grad_t = grad_result.T.astype(BF16)
    total = x_mid + b2_ref[...]
    grad_normed = jnp.zeros_like(total)
    for j in range(w1_ref.shape[0]):
        pre = dot(normed, w1_ref[j]) + b1_ref[j]
        bell = jnp.exp2(pre * pre * (-0.5 * LOG2E))
        near = 1.0 / (1.0 + 0.23164189 * jnp.abs(pre))
        series = 0.5 * 1.061405429 * near - 0.5 * 1.453152027
        series = series * near + 0.5 * 1.421413741
        series = series * near - 0.5 * 0.284496736
        series = series * near + 0.5 * 0.254829592
        tail = series * near * bell
        below = jnp.where(pre < 0.0, tail, 1.0 - tail)
        hidden = (pre * below).astype(BF16)
        slope = below + pre * bell * DENSITY
        grad_pre = (dot(grad_low, w2t_ref[j]) * slope).astype(BF16)
        total = total + dot(hidden, w2_ref[j])
        grad_normed = grad_normed + dot(grad_pre, w1t_ref[j])
        g2_ref[j] += dot(grad_t, hidden)
        g1_ref[j] += dot(normed_t, grad_pre)
        gb1_ref[j] += jnp.sum(grad_pre.astype(F32), 0, keepdims=True)
    out_ref[0] = (mask * total).astype(BF16)
    grad_mid = grad_result + norm_back(grad_normed, unit, inverse, gain_ref[...])
    gmid_ref[0] = grad_mid
    small_ref[0:1] += jnp.sum(grad_normed * unit, 0, keepdims=True)
    small_ref[1:2] += jnp.sum(grad_normed, 0, keepdims=True)
    small_ref[2:3] += jnp.sum(grad_mid, 0, keepdims=True)
    small_ref[3:4] += jnp.sum(grad_result, 0, keepdims=True)
    mid_low = grad_mid.astype(BF16)
    gp_ref[...] += dot_tn(mixed, mid_low)
    grad_mixed = dot(mid_low, pwt_ref[...])
    gh_ref[0] = grad_mixed[:WIN, :BR].astype(BF16)
    gh_ref[1] = grad_mixed[WIN:, :BR].astype(BF16)
    whole[...] = grad_mixed[:, BR:]
    split_columns(whole, left, right)
    gk_ref[0] = jnp.where(first_half, left[...], right[...]).astype(BF16)
    gs_ref[0] = jnp.where(first_half, right[...], left[...]).astype(BF16)


def columns_backward_kernel(
    image, sc, gk_ref, gr_ref, p_ref, q_ref, k_ref, v_ref, o_ref, rl_ref, n_ref, wt_ref, taps_ref,
    gq_ref, lepe_ref, keep_ref, send_ref,
    grad_ref, out_ref, acc_ref, kb_ref, vb_ref, ds_ref,
):
    step = pl.program_id(0)
    place = sc[0]
    height, width = sc[1 + 2 * image], sc[2 + 2 * image]

    @pl.when(step == 0)
    def _():
        set_indicator(vb_ref)
        acc_ref[...] = jnp.zeros_like(acc_ref)
        lepe_ref[...] = jnp.zeros_like(lepe_ref)
        for source, side in ((gk_ref, place), (gr_ref, 1 - place)):
            for s in range(2):
                start = pl.multiple_of(side * PAIR + s * WIN, 8)
                grad_ref[pl.ds(start, WIN)] = source[s].astype(F32)

    refs = (p_ref, q_ref, k_ref, v_ref, o_ref, rl_ref, kb_ref, vb_ref, ds_ref)
    for k in range(2):
        column = (2 * step + k) * STRIPE
        grads = jnp.concatenate(
            [grad_ref[pl.ds(column + q, PH, stride=HALF)] for q in range(STRIPE)], axis=0
        )
        base = place * HALF + column
        valid = window_valid(base, width, height)
        rows, tap_rows = window_backward(
            grads, valid, base, width, height, taps_ref[...], k, refs
        )
        for index, item in enumerate(tap_rows):
            lepe_ref[index : index + 1] += item
        acc_ref[...] += dot_tn(n_ref[k], rows)
        back = dot(rows, wt_ref[...])
        for q in range(STRIPE):
            cut = slice(q * PH, (q + 1) * PH)
            out_ref[0, pl.ds(column + q, PH, stride=HALF)] = back[cut, :BR]
            out_ref[1, pl.ds(column + q, PH, stride=HALF)] = back[cut, BR:]

    @pl.when(step == 1)
    def _():
        gq_ref[...] = acc_ref[...].T
        for s in range(2):
            keep = pl.multiple_of(place * PAIR + s * WIN, 8)
            send = pl.multiple_of((1 - place) * PAIR + s * WIN, 8)
            for j in range(2):
                lanes = slice(j * BR, (j + 1) * BR)
                keep_ref[s, :, lanes] = out_ref[j, pl.ds(keep, WIN)].astype(BF16)
                send_ref[s, :, lanes] = out_ref[j, pl.ds(send, WIN)].astype(BF16)


def rows_backward_kernel(
    image, first, sc, x_ref, gm_ref, gmid_ref, vk_ref, vr_ref,
    p_ref, q_ref, k_ref, v_ref, o_ref, rl_ref, wt_ref, taps_ref, gain_ref, bias_ref, *rest
):
    if not first:
        rest = rest[1:]
    (
        out_ref, gq_ref, lepe_ref, small_ref,
        acc_ref, whole, left, right, kb_ref, vb_ref, ds_ref,
    ) = rest
    step = pl.program_id(0)
    place = sc[0]
    height, width = sc[1 + 2 * image], sc[2 + 2 * image]
    row_base = place * HALF + step * 2 * STRIPE

    @pl.when(step == 0)
    def _():
        set_indicator(vb_ref)
        acc_ref[...] = jnp.zeros_like(acc_ref)
        lepe_ref[...] = jnp.zeros_like(lepe_ref)
        small_ref[...] = jnp.zeros_like(small_ref)

    mask = twice(as_float(inside(split_index(PAIR, PW, BR), row_base, 0, height, width)))
    unit, inverse = norm_parts(x_ref[0].astype(F32) * mask)
    normed = (unit * gain_ref[...] + bias_ref[...])
    first_half = place == 0
    own = vk_ref[0].astype(F32)
    other = vr_ref[0].astype(F32)
    left[...] = jnp.where(first_half, own, other)
    right[...] = jnp.where(first_half, other, own)
    merge_columns(left, right, whole)
    refs = (p_ref, q_ref, k_ref, v_ref, o_ref, rl_ref, kb_ref, vb_ref, ds_ref)
    parts = []
    for k in range(2):
        base = row_base + k * STRIPE
        valid = window_valid(base, height, width)
        rows, tap_rows = window_backward(
            gm_ref[k].astype(F32), valid, base, height, width, taps_ref[...], k, refs
        )
        for index, item in enumerate(tap_rows):
            lepe_ref[index : index + 1] += item
        acc_ref[...] += dot_tn(normed[k * WIN : (k + 1) * WIN].astype(BF16), rows)
        parts.append(dot(rows, wt_ref[...]))
    grad_normed = jnp.concatenate(parts, axis=0) + whole[...]
    small_ref[0:1] += jnp.sum(grad_normed * unit, 0, keepdims=True)
    small_ref[1:2] += jnp.sum(grad_normed, 0, keepdims=True)
    back = norm_back(grad_normed, unit, inverse, gain_ref[...])
    out_ref[0] = (mask * (gmid_ref[0] + back)).astype(BF16)

    @pl.when(step == 1)
    def _():
        gq_ref[...] = acc_ref[...].T


def spec(shape, index=None):
    if index is None:
        return pl.BlockSpec(shape, lambda i: (0,) * len(shape))
    return pl.BlockSpec(shape, index)


def shaped(shape, dtype):
    return jax.ShapeDtypeStruct(shape, dtype)


SCALARS = pl.BlockSpec(memory_space=pltpu.SMEM)


def call(kernel, name, grid, in_specs, out_specs, out_shape, scratch, flops, moved, aliases=None):
    return pl.pallas_call(
        kernel,
        name=name,
        grid=(grid,),
        in_specs=in_specs,
        out_specs=out_specs,
        out_shape=out_shape,
        scratch_shapes=scratch,
        input_output_aliases=aliases or {},
        cost_estimate=pl.CostEstimate(flops=flops, bytes_accessed=moved, transcendentals=0),
        compiler_params=pltpu.CompilerParams(
            vmem_limit_bytes=VMEM_LIMIT, dimension_semantics=("arbitrary",)
        ),
    )


def window_shapes(count):
    return [
        shaped((count, WIN, WIDE), BF16),
        shaped((count, WIN, BR), BF16),
        shaped((count, WIN, BR), BF16),
        shaped((count, WIN, BR), BF16),
        shaped((count, WIN, BR), BF16),
        shaped((count, WIN, BR), F32),
    ]


def window_specs(offset=0):
    index = lambda i: (i + offset, 0, 0)
    return [spec((2, WIN, WIDE), index)] + [spec((2, WIN, BR), index)] * 5


def forward_scratch():
    return [
        pltpu.VMEM((2, WIDE, BR), BF16),
        pltpu.VMEM((2, WIDE, 2 * BR), BF16),
        pltpu.VMEM((2, WIN, BR), F32),
        pltpu.VMEM((2, WIN, BR), F32),
        pltpu.VMEM((WIN, WIDE), F32),
    ]


def backward_scratch():
    return [
        pltpu.VMEM((2, WIDE, BR), BF16),
        pltpu.VMEM((2, WIDE, 2 * BR), BF16),
        pltpu.VMEM((2, WIN, WIDE), BF16),
    ]


WINDOW_FLOPS = 2 * WIN * WIDE * 256


def split_quadrants(scalars, x_pairs):
    count, _, width = x_pairs.shape
    block = spec((1, WIN, width), lambda i: (i, 0, 0))
    return call(
        quadrant_kernel, "quadrants", count,
        [SCALARS, spec((1, PAIR, width), lambda i: (i, 0, 0))],
        [block, block],
        [shaped((count, WIN, width), BF16)] * 2,
        [pltpu.VMEM((PAIR, width), F32), pltpu.VMEM((WIN, width), F32), pltpu.VMEM((WIN, width), F32)],
        0, 4 * x_pairs.size,
    )(scalars, x_pairs)


def rows_forward(scalars, x_pairs, gain, bias, weight, taps, shift):
    count, _, width = x_pairs.shape
    windows = 2 * count
    return call(
        rows_forward_kernel, "rows_forward", count,
        [
            SCALARS, spec((1, PAIR, width), lambda i: (i, 0, 0)), spec((1, width)), spec((1, width)),
            spec((width, 3 * BR)), spec((9, BR)), spec((1, BR)),
        ],
        window_specs() + [spec((2, WIN, BR), lambda i: (i, 0, 0))],
        window_shapes(windows) + [shaped((windows, WIN, BR), BF16)],
        forward_scratch(),
        windows * 2 * WINDOW_FLOPS, windows * 2 * WIN * WIDE,
    )(scalars, x_pairs, gain, bias, weight, taps, shift)


def columns_forward(image, scalars, own, other, gain, bias, weight, taps, shift):
    width = own.shape[2]
    pick = lambda i: (image, 0, 0)
    fixed = spec((2, WIN, BR), lambda i: (0, 0, 0))
    return call(
        partial(columns_forward_kernel, image), "columns_forward", 2,
        [
            SCALARS, spec((2, WIN, width), pick), spec((2, WIN, width), pick), spec((1, width)),
            spec((1, width)), spec((width, 3 * BR)), spec((9, BR)), spec((1, BR)),
        ],
        window_specs() + [spec((2, WIN, width), lambda i: (i, 0, 0)), fixed, fixed],
        window_shapes(4) + [shaped((4, WIN, width), BF16)] + [shaped((2, WIN, BR), BF16)] * 2,
        [pltpu.VMEM((2, 2 * PAIR, BR), F32), pltpu.VMEM((2 * PAIR, BR), F32)] + forward_scratch(),
        4 * 2 * WINDOW_FLOPS, 4 * 2 * WIN * WIDE,
    )(scalars, own, other, gain, bias, weight, taps, shift)


def mlp(image, scalars, x_pairs, cot_pairs, mixed_rows, mixed_own, mixed_other, params, previous):
    count, _, width = x_pairs.shape
    proj, proj_t, proj_b, gain, bias, w1, w1_t, b1, w2, w2_t, b2 = params
    chunks = w1.shape[0]
    pair = spec((1, PAIR, width), lambda i: (2 * image + i, 0, 0))
    part = spec((1, WIN, BR), lambda i: (i, 0, 0))
    square = spec((chunks, width, CHUNK))
    row = spec((1, width))
    sums = [square, square, spec((2 * BR, width)), spec((8, width)), spec((chunks, 1, CHUNK))]
    sum_shapes = [
        shaped((chunks, width, CHUNK), F32), shaped((chunks, width, CHUNK), F32),
        shaped((2 * BR, width), F32), shaped((8, width), F32), shaped((chunks, 1, CHUNK), F32),
    ]
    in_specs = [
        SCALARS, pair, pair, spec((2, WIN, BR), lambda i: (2 * image + i, 0, 0)), part, part,
        spec((2 * BR, width)), spec((width, 2 * BR)), row, row, row,
        square, spec((chunks, CHUNK, width)), spec((chunks, 1, CHUNK)),
        spec((chunks, CHUNK, width)), square, row,
    ]
    operands = [
        scalars, x_pairs, cot_pairs, mixed_rows, mixed_own, mixed_other,
        proj, proj_t, proj_b, gain, bias, w1, w1_t, b1, w2, w2_t, b2,
    ]
    aliases = {}
    first = previous is None
    if not first:
        old_sums, old_out = previous
        in_specs += sums + [pl.BlockSpec(memory_space=pl.ANY)]
        operands += list(old_sums) + [old_out]
        aliases = {len(operands) - 1: 0}
    fixed = spec((1, PAIR, width), lambda i: (i, 0, 0))
    return call(
        partial(mlp_kernel, image, first), "feed_forward", 2,
        in_specs,
        [pair, fixed, spec((2, WIN, BR), lambda i: (i, 0, 0)), part, part] + sums,
        [
            shaped(x_pairs.shape, BF16), shaped((2, PAIR, width), F32),
            shaped((4, WIN, BR), BF16), shaped((2, WIN, BR), BF16), shaped((2, WIN, BR), BF16),
        ] + sum_shapes,
        [pltpu.VMEM((PAIR, BR), F32), pltpu.VMEM((WIN, BR), F32), pltpu.VMEM((WIN, BR), F32)],
        2 * 12 * PAIR * width * CHUNK * chunks, 2 * 10 * PAIR * width, aliases,
    )(*operands)


def columns_backward(image, scalars, grad_own, grad_other, kept, normed, weight_t, taps):
    width = weight_t.shape[1]
    fixed = spec((2, WIN, width), lambda i: (0, 0, 0))
    grads = spec((2, WIN, BR), lambda i: (0, 0, 0))
    return call(
        partial(columns_backward_kernel, image), "columns_backward", 2,
        [SCALARS, grads, grads] + window_specs()
        + [spec((2, WIN, width), lambda i: (i, 0, 0)), spec((3 * BR, width)), spec((9, BR))],
        [spec((3 * BR, width)), spec((16, BR)), fixed, fixed],
        [shaped((3 * BR, width), F32), shaped((16, BR), F32)] + [shaped((2, WIN, width), BF16)] * 2,
        [pltpu.VMEM((2 * PAIR, BR), F32), pltpu.VMEM((2, 2 * PAIR, BR), F32), pltpu.VMEM((width, 3 * BR), F32)]
        + backward_scratch(),
        4 * 4 * WINDOW_FLOPS, 4 * 2 * WIN * WIDE,
    )(scalars, grad_own, grad_other, *kept, normed, weight_t, taps)


def rows_backward(
    image, scalars, x_pairs, grad_mixed, grad_mid, back_own, back_other, kept, weight_t, taps, gain,
    bias, previous,
):
    width = weight_t.shape[1]
    pair = spec((1, PAIR, width), lambda i: (2 * image + i, 0, 0))
    part = spec((1, WIN, width), lambda i: (i, 0, 0))
    in_specs = [
        SCALARS, pair, spec((2, WIN, BR), lambda i: (i, 0, 0)),
        spec((1, PAIR, width), lambda i: (i, 0, 0)), part, part,
    ] + window_specs(2 * image) + [
        spec((3 * BR, width)), spec((9, BR)), spec((1, width)), spec((1, width)),
    ]
    operands = [
        scalars, x_pairs, grad_mixed, grad_mid, back_own, back_other, *kept, weight_t, taps, gain, bias,
    ]
    aliases = {}
    first = previous is None
    if not first:
        in_specs.append(pl.BlockSpec(memory_space=pl.ANY))
        operands.append(previous)
        aliases = {len(operands) - 1: 0}
    return call(
        partial(rows_backward_kernel, image, first), "rows_backward", 2,
        in_specs,
        [pair, spec((3 * BR, width)), spec((16, BR)), spec((8, width))],
        [
            shaped(x_pairs.shape, BF16), shaped((3 * BR, width), F32), shaped((16, BR), F32),
            shaped((8, width), F32),
        ],
        [
            pltpu.VMEM((width, 3 * BR), F32), pltpu.VMEM((PAIR, width), F32),
            pltpu.VMEM((WIN, width), F32), pltpu.VMEM((WIN, width), F32),
        ] + backward_scratch(),
        4 * 5 * WINDOW_FLOPS, 4 * 2 * WIN * WIDE, aliases,
    )(*operands)


def swap_tensor(values):
    return lax.ppermute(values, "tensor", [(0, 1), (1, 0)])


def swap_dp(values, size, bit):
    return lax.ppermute(values, "dp", [(i, i ^ (1 << bit)) for i in range(size)])


def reduce_packed(packed, size):
    place = lax.axis_index("tensor")
    index = lax.axis_index("dp")
    rows = packed.shape[1]
    bits = size.bit_length() - 1
    low = packed.astype(BF16)
    core = index & 1
    half = rows // 2
    sent = lax.dynamic_slice_in_dim(low, (1 - core) * half, half, 1)
    kept = lax.dynamic_slice_in_dim(low, core * half, half, 1)
    low = (kept.astype(F32) + swap_dp(sent, size, 0).astype(F32)).astype(BF16)
    sent = lax.dynamic_index_in_dim(low, 1 - place, 0, False)
    kept = lax.dynamic_index_in_dim(low, place, 0, False)
    low = (kept.astype(F32) + swap_tensor(sent).astype(F32)).astype(BF16)
    for bit in range(1, bits):
        low = (low.astype(F32) + swap_dp(low, size, bit).astype(F32)).astype(BF16)
    other = swap_dp(low, size, 0)
    first = jnp.where(core == 0, low, other)
    second = jnp.where(core == 0, other, low)
    return jnp.concatenate([first, second], axis=0)


def per_device(
    size, block_input, heights, widths, norm1_gain, norm1_bias, qkv_weight, lepe_weight, lepe_bias,
    proj_weight, proj_bias, norm2_gain, norm2_bias, fc1_weight, fc1_bias, fc2_weight, fc2_bias,
    cotangent,
):
    place = lax.axis_index("tensor")
    images, local_cells, width = block_input.shape
    sides = jnp.stack([heights, widths], 1).reshape(-1)
    scalars = jnp.concatenate([place[None].astype(jnp.int32), sides])
    x_pairs = block_input.reshape(2 * images, PAIR, width)
    cot_pairs = cotangent.reshape(2 * images, PAIR, width)

    def both(own, axis):
        other = swap_tensor(own)
        return jnp.concatenate(
            [jnp.where(place == 0, own, other), jnp.where(place == 0, other, own)], axis
        )

    gain1, bias1 = norm1_gain[None], norm1_bias[None]
    qkv = [both(qkv_weight[:, :, b], 2).reshape(width, 3 * BR) for b in range(2)]
    quad_own, quad_send = split_quadrants(scalars, x_pairs)
    quad_other = swap_tensor(quad_send)
    lepe_all = both(jnp.concatenate([lepe_weight, lepe_bias[:, None]], 1), 2).astype(F32)
    proj = both(proj_weight, 1).reshape(2 * BR, width)
    w1 = both(fc1_weight, 1)
    b1 = both(fc1_bias[None], 1).astype(F32)
    w2 = both(fc2_weight, 0)
    hidden = w1.shape[1]
    chunks = hidden // CHUNK
    w1_chunks = w1.reshape(width, chunks, CHUNK).transpose(1, 0, 2)
    w1_t = w1.T.reshape(chunks, CHUNK, width)
    w2_chunks = w2.reshape(chunks, CHUNK, width)
    w2_t = w2_chunks.transpose(0, 2, 1)
    params = (
        proj, proj.T, proj_bias.astype(F32)[None], norm2_gain[None], norm2_bias[None],
        w1_chunks, w1_t, b1.reshape(chunks, 1, CHUNK), w2_chunks, w2_t, fc2_bias.astype(F32)[None],
    )
    taps = [lepe_all[0, :9], lepe_all[1, :9].reshape(3, 3, BR).transpose(1, 0, 2).reshape(9, BR)]
    shifts = [lepe_all[b, 9:10] for b in range(2)]

    *kept_rows, mixed_rows = rows_forward(
        scalars, x_pairs, gain1, bias1, qkv[0], taps[0], shifts[0]
    )
    columns = []
    for image in range(images):
        *kept, normed, keep, send = columns_forward(
            image, scalars, quad_own, quad_other, gain1, bias1, qkv[1], taps[1], shifts[1]
        )
        columns.append((kept, normed, keep, swap_tensor(send)))
    previous = None
    middle = []
    for image in range(images):
        _, _, keep, other = columns[image]
        output, grad_mid, grad_rows, grad_keep, grad_send, *sums = mlp(
            image, scalars, x_pairs, cot_pairs, mixed_rows, keep, other, params, previous
        )
        previous = (sums, output)
        middle.append((grad_mid, grad_rows, grad_keep, swap_tensor(grad_send)))
    g1, g2, gp, small2, gb1 = sums
    column_back = []
    for image in range(images):
        kept, normed, _, _ = columns[image]
        _, _, grad_keep, grad_other = middle[image]
        gq, lepe_grad, back_keep, back_send = columns_backward(
            image, scalars, grad_keep, grad_other, kept, normed, qkv[1].T, taps[1]
        )
        column_back.append((gq, lepe_grad, back_keep, swap_tensor(back_send)))
    input_grad = None
    row_back = []
    for image in range(images):
        grad_mid, grad_rows, _, _ = middle[image]
        _, _, back_keep, back_other = column_back[image]
        input_grad, gq, lepe_grad, small1 = rows_backward(
            image, scalars, x_pairs, grad_rows, grad_mid, back_keep, back_other, kept_rows,
            qkv[0].T, taps[0], gain1, bias1, input_grad,
        )
        row_back.append((gq, lepe_grad, small1))

    def halves(rows):
        count = rows.shape[0] // BR
        return (
            rows.reshape(count, 2, BR // 2, width).transpose(1, 0, 2, 3).reshape(2, -1, width)
        )

    gqs = [sum(item[0] for item in row_back), sum(item[0] for item in column_back)]
    lepe_grads = jnp.concatenate(
        [sum(item[1] for item in row_back), sum(item[1] for item in column_back)], 1
    )[:10]
    small1 = sum(item[2] for item in row_back)[:2]
    shared = jnp.concatenate([small1, small2[:4], gb1.reshape(-1, width), lepe_grads], 0)
    shared = jnp.broadcast_to(shared[None], (2,) + shared.shape)
    split = chunks // 2
    packed = jnp.concatenate(
        [
            g1.reshape(2, split * width, CHUNK), g2.reshape(2, split * width, CHUNK), halves(gp),
            halves(gqs[0]), halves(gqs[1]), shared,
        ],
        1,
    )
    rows = packed.shape[1]
    padding = -rows % 16
    packed = jnp.pad(packed, ((0, 0), (0, padding), (0, 0)))
    total = reduce_packed(packed, size).astype(F32)
    at = 0
    pieces = []
    for count in (split * width, split * width, BR, 3 * BR // 2, 3 * BR // 2, 2, 4, hidden // width, 10):
        pieces.append(total[at : at + count])
        at += count
    t1, t2, tp, tq0, tq1, ts1, ts2, tb1, tl = pieces
    grad_fc1 = t1.reshape(split, width, CHUNK).transpose(1, 0, 2).reshape(width, split * CHUNK)
    grad_fc2 = t2.reshape(split, width, CHUNK).transpose(0, 2, 1).reshape(split * CHUNK, width)
    grad_proj = tp.reshape(2, BR // 2, width)
    grad_qkv = jnp.stack([tq0.reshape(3, BR // 2, width), tq1.reshape(3, BR // 2, width)], 1)
    grad_qkv = grad_qkv.transpose(3, 0, 1, 2)
    lepe_both = jnp.stack([tl[:, :BR], tl[:, BR:]], 0)
    lepe_own = lax.dynamic_slice_in_dim(lepe_both, place * (BR // 2), BR // 2, 2)
    taps_rows = lepe_own[0, :9]
    taps_columns = lepe_own[1, :9].reshape(3, 3, -1).transpose(1, 0, 2).reshape(9, -1)
    grad_lepe = jnp.stack([taps_rows, taps_columns], 0)
    grad_shift = lepe_own[:, 9]
    grad_b1 = lax.dynamic_slice_in_dim(tb1.reshape(-1), place * (hidden // 2), hidden // 2, 0)
    return (
        output.reshape(block_input.shape), input_grad.reshape(block_input.shape),
        ts1[0], ts1[1], grad_qkv, grad_lepe, grad_shift, grad_proj, ts2[2], ts2[0], ts2[1],
        grad_fc1, grad_b1, grad_fc2, ts2[3],
    )


def solution(mesh):
    placed = (
        P("dp", "tensor", None),
        P("dp"),
        P("dp"),
        P(),
        P(),
        P(None, None, None, "tensor"),
        P(None, None, "tensor"),
        P(None, "tensor"),
        P(None, "tensor", None),
        P(),
        P(),
        P(),
        P(None, "tensor"),
        P("tensor"),
        P("tensor", None),
        P(),
        P("dp", "tensor", None),
    )
    return jax.shard_map(
        partial(per_device, mesh.shape["dp"]),
        mesh=mesh,
        in_specs=placed,
        out_specs=(
            P("dp", "tensor", None),
            P("dp", "tensor", None),
            P(),
            P(),
            P(None, None, None, "tensor"),
            P(None, None, "tensor"),
            P(None, "tensor"),
            P(None, "tensor", None),
            P(),
            P(),
            P(),
            P(None, "tensor"),
            P("tensor"),
            P("tensor", None),
            P(),
        ),
        check_vma=False,
    )
```

```python
from functools import partial

import jax
import jax.numpy as jnp
from jax import lax
from jax.experimental import pallas as pl
from jax.experimental.pallas import tpu as pltpu
from jax.sharding import PartitionSpec as P

HEAD_DIM = 32
STRIPE = 7
PH = 56
PW = 56
HEADS = 4
BR = HEADS * HEAD_DIM
WIN = STRIPE * PW
WIDE = HEADS * WIN
MAIN = WIN // 128 * 128
REST = WIN - MAIN
HALF = 28
PAIR = 2 * WIN
CHUNK = 256
CHUNKS = [(lo, min(lo + CHUNK, WIDE)) for lo in range(0, WIDE, CHUNK)]

MASKED = -30.0
EPSILON = 1e-05
LOG2E = 1.4426950408889634
LN2 = 0.6931471805599453
DENSITY = 0.3989422804014327
DEN_LOW = 2.0**-60
DEN_HIGH = 2.0**100

F32 = jnp.float32
BF16 = jnp.bfloat16
MIB = 2**20
GRAD_ROWS = 1152
LAST_ROWS = 416
SMALL_AT = 3 * BR
FIRST_HALF = 208
LATE = 304


def dot(a, b):
    return jnp.dot(a, b, preferred_element_type=F32)


def dot_nt(a, b):
    return lax.dot_general(a, b, (((1,), (1,)), ((), ())), preferred_element_type=F32)


def dot_tn(a, b):
    return lax.dot_general(a, b, (((0,), (0,)), ((), ())), preferred_element_type=F32)


def split_index(count, width, lanes, axis=0):
    shape = (count, lanes) if axis == 0 else (lanes, count)
    index = lax.broadcasted_iota(jnp.int32, shape, axis)
    step = -(-65536 // width)
    major = lax.shift_right_logical(index * step, 16)
    return major, index - major * width


def inside(parts, base_major, base_minor, lim_major, lim_minor):
    major, minor = parts
    return (major < lim_major - base_major) & (minor < lim_minor - base_minor)


def as_float(flag):
    return jnp.where(flag, 1.0, 0.0).astype(F32)


def twice(values):
    return jnp.concatenate([values, values], axis=1)


def head_lane(head):
    lane = lax.broadcasted_iota(jnp.int32, (1, BR), 1)
    return as_float((lane >= head * HEAD_DIM) & (lane < (head + 1) * HEAD_DIM))


def head_blocks(values):
    lanes = [head_lane(head) for head in range(HEADS)]
    top = [values[:MAIN] * lane for lane in lanes]
    rest = [values[MAIN:] * lane for lane in lanes]
    return jnp.concatenate(top + rest, axis=0)


def from_wide(values):
    rows = []
    for head in range(HEADS):
        own = values[head * HEAD_DIM : (head + 1) * HEAD_DIM]
        rest = HEADS * MAIN + head * REST
        rows.append(
            jnp.concatenate(
                [own[:, head * MAIN : (head + 1) * MAIN], own[:, rest : rest + REST]], axis=1
            )
        )
    return jnp.concatenate(rows, axis=0)


def norm_parts(values):
    centred = values - jnp.mean(values, -1, keepdims=True)
    inverse = lax.rsqrt(jnp.mean(centred * centred, -1, keepdims=True) + EPSILON)
    return centred * inverse, inverse


def norm_back(grad_rows, unit_rows, inverse, gain):
    scaled = grad_rows * gain
    return inverse * (
        scaled
        - jnp.mean(scaled, -1, keepdims=True)
        - unit_rows * jnp.mean(scaled * unit_rows, -1, keepdims=True)
    )


def neighbours(values):
    _, minor = split_index(WIN, PW, BR)
    before = jnp.where(minor == 0, 0.0, pltpu.roll(values, 1, 0))
    after = jnp.where(minor == PW - 1, 0.0, pltpu.roll(values, WIN - 1, 0))
    return before, after


def add_rows(low, mid, high):
    gap = jnp.zeros((PW, mid.shape[1]), F32)
    return (
        mid
        + jnp.concatenate([gap, low[: WIN - PW]], axis=0)
        + jnp.concatenate([high[PW:], gap], axis=0)
    )


def lepe_apply(values, taps):
    before, after = neighbours(values)
    rows = [
        taps[3 * a : 3 * a + 1] * before
        + taps[3 * a + 1 : 3 * a + 2] * values
        + taps[3 * a + 2 : 3 * a + 3] * after
        for a in range(3)
    ]
    return add_rows(rows[0], rows[1], rows[2])


def lepe_back(grads, values, taps):
    before, after = neighbours(grads)
    rows = [
        taps[3 * a : 3 * a + 1] * after
        + taps[3 * a + 1 : 3 * a + 2] * grads
        + taps[3 * a + 2 : 3 * a + 3] * before
        for a in range(3)
    ]
    back = add_rows(rows[2], rows[1], rows[0])
    value_before, value_after = neighbours(values)
    tap_rows = []
    for a in range(3):
        for item in (value_before, values, value_after):
            if a == 0:
                product = grads[PW:] * item[: WIN - PW]
            elif a == 1:
                product = grads * item
            else:
                product = grads[: WIN - PW] * item[PW:]
            tap_rows.append(jnp.sum(product, 0, keepdims=True))
    tap_rows.append(jnp.sum(grads, 0, keepdims=True))
    return back, tap_rows


def window_valid(window_base, lim_major, lim_minor):
    return inside(split_index(WIN, PW, BR), window_base, 0, lim_major, lim_minor)


def window_forward(projected, valid, taps, shift, first, k, refs):
    p_ref, q_ref, k_ref, v_ref, o_ref, rl_ref, kb_ref, vb_ref, lepe_ref, mixed_ref = refs
    queries = (projected[:, :BR] * (HEAD_DIM**-0.5 * LOG2E)).astype(BF16)
    key_rows = projected[:, BR : 2 * BR]
    values = projected[:, 2 * BR :].astype(BF16).astype(F32)
    valid_float = as_float(valid)
    weight = jnp.where(valid, 1.0, jnp.exp(jnp.full((WIN, BR), MASKED, F32)))
    q_ref[first + k] = queries
    k_ref[first + k] = (key_rows * valid_float).astype(BF16)
    v_ref[first + k] = values.astype(BF16)
    kb_ref[k] = head_blocks(key_rows * valid_float).astype(BF16)
    vb_ref[k, :, :BR] = head_blocks(values * weight).astype(BF16)
    vb_ref[k, :, BR:] = head_blocks(weight).astype(BF16)
    for lo, hi in CHUNKS:
        p_ref[first + k, :, lo:hi] = jnp.exp2(dot_nt(queries, kb_ref[k, lo:hi])).astype(BF16)
    sums = dot(p_ref[first + k], vb_ref[k])
    totals = sums[:, BR:]
    inverse = 1.0 / totals
    attended = sums[:, :BR] * inverse
    o_ref[first + k] = attended.astype(BF16)
    rl_ref[first + k] = inverse
    lepe = lepe_apply(values, taps) + shift
    lepe_ref[k] = lepe
    mixed_ref[k] = attended + lepe
    safe = (totals > DEN_LOW) & (totals < DEN_HIGH)
    return jnp.max(jnp.where(safe, 0.0, 1.0))


def window_forward_safe(first, k, refs, s_ref):
    p_ref, q_ref, k_ref, v_ref, o_ref, rl_ref, kb_ref, vb_ref, lepe_ref, mixed_ref = refs
    s_ref[...] = dot_nt(q_ref[first + k], kb_ref[k])
    for head in range(HEADS):
        cut = slice(head * MAIN, (head + 1) * MAIN)
        rest = HEADS * MAIN + head * REST
        left = s_ref[:, cut]
        right = s_ref[:, rest : rest + REST]
        peak = jnp.maximum(jnp.max(left, -1, keepdims=True), jnp.max(right, -1, keepdims=True))
        s_ref[:, cut] = left - peak
        s_ref[:, rest : rest + REST] = right - peak
    for lo, hi in CHUNKS:
        p_ref[first + k, :, lo:hi] = jnp.exp2(s_ref[:, lo:hi]).astype(BF16)
    sums = dot(p_ref[first + k], vb_ref[k])
    inverse = 1.0 / sums[:, BR:]
    attended = sums[:, :BR] * inverse
    o_ref[first + k] = attended.astype(BF16)
    rl_ref[first + k] = inverse
    mixed_ref[k] = attended + lepe_ref[k]


def window_backward(grads, base, lim_major, lim_minor, taps, first, k, refs):
    p_ref, q_ref, k_ref, v_ref, o_ref, rl_ref, kb_ref, vb_ref, ds_ref = refs
    lane = lax.broadcasted_iota(jnp.int32, (WIN, BR), 1)
    scaled = (grads * rl_ref[first + k]).astype(BF16)
    product = scaled.astype(F32) * o_ref[first + k].astype(F32)
    high = product.astype(BF16)
    low = (product - high.astype(F32)).astype(BF16)
    row = lax.broadcasted_iota(jnp.int32, (2 * BR, BR), 0)
    col = lax.broadcasted_iota(jnp.int32, (2 * BR, BR), 1)
    head_of = lax.shift_right_logical(row & (BR - 1), 5)
    picks = as_float((col < 2 * HEADS) & (head_of == (col & (HEADS - 1)))).astype(BF16)
    inner = dot(jnp.concatenate([high, low], axis=1), picks)
    inner_high = inner.astype(BF16).astype(F32)
    extra = jnp.where(lane < HEADS, inner_high, inner - inner_high).astype(BF16)
    left = jnp.concatenate([scaled, extra], axis=1)
    values = v_ref[first + k].astype(F32)
    vb_ref[k, :, :BR] = head_blocks(values).astype(BF16)
    kb_ref[k] = head_blocks(k_ref[first + k].astype(F32)).astype(BF16)
    for lo, hi in CHUNKS:
        grad_probs = dot_nt(left, vb_ref[k, lo:hi])
        ds_ref[k, :, lo:hi] = grad_probs.astype(BF16) * p_ref[first + k, :, lo:hi]
    grad_query = dot(ds_ref[k], kb_ref[k]) * (HEAD_DIM**-0.5)
    query_t = q_ref[first + k].astype(F32).T.astype(BF16)
    scaled_t = scaled.astype(F32).T.astype(BF16)
    valid_t = inside(split_index(WIN, PW, BR, 1), base, 0, lim_major, lim_minor)
    weight_t = jnp.where(valid_t, 1.0, jnp.exp(jnp.full((BR, WIN), MASKED, F32)))
    grad_key = (from_wide(dot(query_t, ds_ref[k])) * jnp.where(valid_t, LN2, 0.0)).T
    grad_value = (from_wide(dot(scaled_t, p_ref[first + k])) * weight_t).T
    back, tap_rows = lepe_back(grads, values, taps)
    out = jnp.concatenate([grad_query, grad_key, grad_value + back], axis=1)
    return out.astype(BF16), tap_rows


def set_indicator(vb_ref):
    row = lax.broadcasted_iota(jnp.int32, (WIDE, BR), 0)
    col = lax.broadcasted_iota(jnp.int32, (WIDE, BR), 1)
    head = jnp.zeros((WIDE, BR), jnp.int32)
    for cut in range(1, HEADS):
        head = head + jnp.where(row >= cut * MAIN, 1, 0)
    tail = lax.shift_right_logical(row - HEADS * MAIN, 3)
    head = jnp.where(row >= HEADS * MAIN, tail, head)
    hit = (col < 2 * HEADS) & ((col & (HEADS - 1)) == head)
    for k in range(2):
        vb_ref[k, :, BR:] = jnp.where(hit, -1.0, 0.0).astype(BF16)


def split_columns(source, left, right):
    for row in range(STRIPE * 2):
        left[row * HALF : (row + 1) * HALF] = source[row * PW : row * PW + HALF]
        right[row * HALF : (row + 1) * HALF] = source[row * PW + HALF : (row + 1) * PW]


def merge_columns(left, right, target):
    for row in range(STRIPE * 2):
        target[row * PW : row * PW + HALF] = left[row * HALF : (row + 1) * HALF]
        target[row * PW + HALF : (row + 1) * PW] = right[row * HALF : (row + 1) * HALF]


def sides(image, heights, info):
    return heights[image], info[image]


def tensor_place(info):
    return info[info.shape[0] - 3]


def core_place(info):
    return info[info.shape[0] - 2]


def along_place(info):
    return info[info.shape[0] - 1]


def pack_kernel(info, qkv_ref, lepe_ref, shift_ref, out_ref, send_ref):
    for item in range(3):
        for direction in range(2):
            row = (2 * item + direction) * BR // 2
            out_ref[row : row + BR // 2] = qkv_ref[item, direction]
    rows = [
        jnp.concatenate([lepe_ref[tap, 0:1], lepe_ref[tap, 1:2]], axis=1).astype(F32)
        for tap in range(9)
    ]
    rows.append(jnp.concatenate([shift_ref[0:1], shift_ref[1:2]], axis=1).astype(F32))
    rows.append(jnp.zeros((2 * FIRST_HALF - SMALL_AT - 10, BR), F32))
    small = jnp.concatenate(rows, axis=0)
    out_ref[SMALL_AT:] = jnp.concatenate([small, jnp.zeros_like(small)], axis=1).astype(BF16)
    send_ref[...] = out_ref[pl.ds(pl.multiple_of(core_place(info) * FIRST_HALF, 16), FIRST_HALF)]


def late_pack_kernel(info, w1_ref, w2_ref, proj_ref, vectors_ref, out_ref, send_ref):
    for j in range(2):
        out_ref[j * CHUNK : (j + 1) * CHUNK] = w1_ref[:, j * CHUNK : (j + 1) * CHUNK]
    out_ref[2 * CHUNK : 4 * CHUNK] = w2_ref[...]
    for b in range(2):
        at = 4 * CHUNK + b * BR // 2
        out_ref[at : at + BR // 2] = proj_ref[b]
    vectors = vectors_ref[...].astype(F32)
    tail = jnp.concatenate([vectors, jnp.zeros((4 * LATE - GRAD_ROWS - 4, 2 * BR), F32)], axis=0)
    out_ref[GRAD_ROWS:] = tail.astype(BF16)
    part = 2 * core_place(info) + along_place(info)
    send_ref[...] = out_ref[pl.ds(pl.multiple_of(part * LATE, 16), LATE)]


def quadrant_kernel(images, info, x_ref, own_ref, *rest):
    sends, (whole, left, right) = rest[:images], rest[images:]
    step = pl.program_id(0)
    whole[...] = x_ref[0].astype(F32)
    split_columns(whole, left, right)
    first = tensor_place(info) == 0
    own_ref[0] = jnp.where(first, left[...], right[...]).astype(BF16)
    other = jnp.where(first, right[...], left[...]).astype(BF16)
    for image in range(images):

        @pl.when(step // 2 == image)
        def _():
            sends[image][0] = other


def rows_forward_kernel(image, first, *refs):
    heights, info, x_ref, gain_ref, bias_ref = refs[:5]
    if first:
        own_ref, near_ref, far_ref, p_ref, q_ref, k_ref, v_ref, o_ref, rl_ref, m_ref, w_ref, wt_ref, taps_ref = refs[5:18]
        other_ref = refs[-6]
    else:
        w_ref, taps_ref, p_ref, q_ref, k_ref, v_ref, o_ref, rl_ref, m_ref = refs[5:14]
    kb_ref, vb_ref, lepe_ref, mixed_ref, s_ref = refs[-5:]
    step = pl.program_id(0)
    height, width = sides(image, heights, info)
    row_base = tensor_place(info) * HALF + step * 2 * STRIPE

    def unpack_weights():
        core = core_place(info)
        for part, piece in ((core, near_ref), (1 - core, far_ref)):
            other_ref[pl.ds(pl.multiple_of(part * FIRST_HALF, 16), FIRST_HALF)] = piece[...]
        for direction in range(2):
            for item in range(3):
                row = (2 * item + direction) * BR // 2
                at = item * BR
                wt_ref[direction, at : at + BR // 2] = own_ref[row : row + BR // 2]
                wt_ref[direction, at + BR // 2 : at + BR] = other_ref[row : row + BR // 2]
            w_ref[direction] = wt_ref[direction].astype(F32).T.astype(BF16)
        own = own_ref[SMALL_AT : SMALL_AT + 16].astype(F32)
        other = other_ref[SMALL_AT : SMALL_AT + 16].astype(F32)
        half = BR // 2
        for direction in range(2):
            cut = slice(direction * half, (direction + 1) * half)
            both = jnp.concatenate([own[:, cut], other[:, cut]], axis=1)
            if direction == 1:
                order = [3 * (tap % 3) + tap // 3 for tap in range(9)] + list(range(9, 16))
                both = jnp.concatenate([both[tap : tap + 1] for tap in order], axis=0)
            taps_ref[direction] = both

    if first:
        pl.when(step == 0)(unpack_weights)

    mask = as_float(inside(split_index(PAIR, PW, BR), row_base, 0, height, width))
    unit, _ = norm_parts(x_ref[0].astype(F32) * twice(mask))
    normed = (unit * gain_ref[...] + bias_ref[...]).astype(BF16)
    projected = dot(normed, w_ref[0])
    refs = (p_ref, q_ref, k_ref, v_ref, o_ref, rl_ref, kb_ref, vb_ref, lepe_ref, mixed_ref)
    bad = jnp.float32(0)
    for k in range(2):
        valid = window_valid(row_base + k * STRIPE, height, width)
        rows = projected[k * WIN : (k + 1) * WIN]
        bad = jnp.maximum(
            bad,
            window_forward(rows, valid, taps_ref[0, :9], taps_ref[0, 9:10], 2 * step, k, refs),
        )

    @pl.when(bad > 0.0)
    def _():
        def one(k, carry):
            window_forward_safe(2 * step, k, refs, s_ref)
            return carry

        lax.fori_loop(0, 2, one, 0)

    for k in range(2):
        m_ref[2 * step + k] = mixed_ref[k].astype(BF16)


def columns_forward_kernel(
    image, heights, info, own_ref, other_ref, gain_ref, bias_ref, w_ref, taps_ref,
    p_ref, q_ref, k_ref, v_ref, o_ref, rl_ref, n_ref, keep_ref, send_ref,
    unit_ref, out_ref, kb_ref, vb_ref, lepe_ref, mixed_ref, s_ref,
):
    step = pl.program_id(0)
    place = tensor_place(info)
    height, width = sides(image, heights, info)
    column_base = place * HALF

    @pl.when(step == 0)
    def _():
        for source, side in ((own_ref, place), (other_ref, 1 - place)):
            for s in range(2):
                flag = inside(
                    split_index(WIN, HALF, BR), side * HALF + s * 2 * STRIPE, column_base,
                    height, width,
                )
                unit, _ = norm_parts(source[s].astype(F32) * twice(as_float(flag)))
                start = pl.multiple_of(side * PAIR + s * WIN, 8)
                unit_ref[0, pl.ds(start, WIN)] = unit[:, :BR]
                unit_ref[1, pl.ds(start, WIN)] = unit[:, BR:]

    refs = (p_ref, q_ref, k_ref, v_ref, o_ref, rl_ref, kb_ref, vb_ref, lepe_ref, mixed_ref)
    bad = jnp.float32(0)
    for k in range(2):
        column = (2 * step + k) * STRIPE
        halves = [
            jnp.concatenate(
                [unit_ref[j, pl.ds(column + q, PH, stride=HALF)] for q in range(STRIPE)], axis=0
            )
            for j in range(2)
        ]
        unit = jnp.concatenate(halves, axis=1)
        n_ref[2 * step + k] = unit.astype(BF16)
        normed = (unit * gain_ref[...] + bias_ref[...]).astype(BF16)
        valid = window_valid(column_base + column, width, height)
        rows = dot(normed, w_ref[1])
        bad = jnp.maximum(
            bad,
            window_forward(rows, valid, taps_ref[1, :9], taps_ref[1, 9:10], 2 * step, k, refs),
        )

    @pl.when(bad > 0.0)
    def _():
        def one(k, carry):
            window_forward_safe(2 * step, k, refs, s_ref)
            return carry

        lax.fori_loop(0, 2, one, 0)

    for k in range(2):
        column = (2 * step + k) * STRIPE
        mixed = mixed_ref[k]
        for q in range(STRIPE):
            out_ref[pl.ds(column + q, PH, stride=HALF)] = mixed[q * PH : (q + 1) * PH]

    @pl.when(step == 1)
    def _():
        for s in range(2):
            keep = pl.multiple_of(place * PAIR + s * WIN, 8)
            send = pl.multiple_of((1 - place) * PAIR + s * WIN, 8)
            keep_ref[s] = out_ref[pl.ds(keep, WIN)].astype(BF16)
            send_ref[s] = pltpu.roll(out_ref[pl.ds(send, WIN)], BR // 2, 1).astype(BF16)


def mlp_kernel(image, first, last, *refs):
    (
        heights, info, x_ref, cot_ref, mh_ref, mo_ref, mr_ref, gain_ref, bias_ref,
        late_own, *late_parts,
    ) = refs[:14]
    refs = refs[14:]
    if not first:
        refs = refs[3:]
    out_ref, gmid_ref, gh_ref, gk_ref, gs_ref, acc_ref, small_ref = refs[:7]
    refs = refs[7:]
    if last:
        kept_ref, sent_ref = refs[:2]
        refs = refs[2:]
    pw_ref, late_ref, whole, left, right, total_ref, gn_ref, normed_ref, grad_ref, normed_t_ref, grad_t_ref = refs
    step = pl.program_id(0)
    place = tensor_place(info)
    height, width = sides(image, heights, info)
    row_base = place * HALF + step * 2 * STRIPE
    half = BR // 2

    @pl.when(step == 0)
    def _():
        far = 4 * LATE
        late_ref[:far] = late_own[...]
        core, along = core_place(info), along_place(info)
        for at, piece in enumerate(late_parts):
            part = 2 * (core if at < 2 else 1 - core) + (along if at % 2 == 0 else 1 - along)
            late_ref[pl.ds(pl.multiple_of(far + part * LATE, 16), LATE)] = piece[...]
        for b in range(2):
            at = 4 * CHUNK + b * half
            pw_ref[b * BR : b * BR + half] = late_ref[at : at + half]
            pw_ref[b * BR + half : (b + 1) * BR] = late_ref[far + at : far + at + half]
        if first:
            acc_ref[...] = jnp.zeros_like(acc_ref)
            small_ref[...] = jnp.zeros_like(small_ref)

    vectors = late_own[GRAD_ROWS : GRAD_ROWS + 16].astype(F32)
    mask = twice(as_float(inside(split_index(PAIR, PW, BR), row_base, 0, height, width)))
    first_half = place == 0
    own = mo_ref[0].astype(F32)
    other = mr_ref[0].astype(F32)
    left[...] = jnp.where(first_half, own, other)
    right[...] = jnp.where(first_half, other, own)
    merge_columns(left, right, whole)
    rows_part = jnp.concatenate([mh_ref[0].astype(F32), mh_ref[1].astype(F32)], axis=0)
    mixed = jnp.concatenate([rows_part, whole[...]], axis=1).astype(BF16)
    x_in = x_ref[0].astype(F32) * mask
    x_mid = x_in + dot(mixed, pw_ref[...]) + vectors[2:3]
    unit, inverse = norm_parts(x_mid)
    normed = (unit * gain_ref[...] + bias_ref[...]).astype(BF16)
    grad_result = cot_ref[0].astype(F32) * mask
    grad_low = grad_result.astype(BF16)
    normed_t = normed.astype(F32).T.astype(BF16)
    grad_t = grad_result.T.astype(BF16)
    total_ref[...] = x_mid + vectors[3:4]
    gn_ref[...] = jnp.zeros_like(gn_ref)
    normed_ref[...] = normed
    grad_ref[...] = grad_low
    normed_t_ref[...] = normed_t
    grad_t_ref[...] = grad_t

    def holder_chunks(holder, carry):
        base = pl.multiple_of(holder * (4 * LATE), 16)
        rows = late_ref[pl.ds(base + GRAD_ROWS, 16)].astype(F32)
        total, grad_normed = total_ref[...], gn_ref[...]
        for part in range(2):
            cut = part * CHUNK
            w1, w2 = late_ref[pl.ds(base + cut, CHUNK)], late_ref[pl.ds(base + cut + 2 * CHUNK, CHUNK)]
            pre = dot(normed_ref[...], w1) + rows[part : part + 1]
            bell = jnp.exp2(pre * pre * (-0.5 * LOG2E))
            near = 1.0 / (1.0 + 0.23164189 * jnp.abs(pre))
            series = 0.5 * 1.061405429 * near - 0.5 * 1.453152027
            series = series * near + 0.5 * 1.421413741
            series = series * near - 0.5 * 0.284496736
            series = series * near + 0.5 * 0.254829592
            tail = series * near * bell
            below = jnp.where(pre < 0.0, tail, 1.0 - tail)
            hidden = (pre * below).astype(BF16)
            slope = below + pre * bell * DENSITY
            grad_pre = (dot_nt(grad_ref[...], w2) * slope).astype(BF16)
            total = total + dot(hidden, w2)
            grad_normed = grad_normed + dot_nt(grad_pre, w1)
            acc_ref[holder, cut : cut + CHUNK] += dot(normed_t_ref[...], grad_pre)
            acc_ref[holder, cut + 2 * CHUNK : cut + 3 * CHUNK] += dot(grad_t_ref[...], hidden)
            small_ref[pl.ds(4 + 2 * holder + part, 1)] += jnp.sum(grad_pre.astype(F32), 0, keepdims=True)
        total_ref[...] = total
        gn_ref[...] = grad_normed
        return carry

    lax.fori_loop(0, 2, holder_chunks, 0)
    total, grad_normed = total_ref[...], gn_ref[...]
    out_ref[0] = (mask * total).astype(BF16)
    grad_mid = grad_result + norm_back(grad_normed, unit, inverse, gain_ref[...])
    gmid_ref[0] = grad_mid
    small_ref[0:1] += jnp.sum(grad_normed * unit, 0, keepdims=True)
    small_ref[1:2] += jnp.sum(grad_normed, 0, keepdims=True)
    small_ref[2:3] += jnp.sum(grad_mid, 0, keepdims=True)
    small_ref[3:4] += jnp.sum(grad_result, 0, keepdims=True)
    mid_low = grad_mid.astype(BF16)
    grad_proj = dot_tn(mixed, mid_low)
    for b in range(2):
        at = 4 * CHUNK + b * half
        acc_ref[0, at : at + half] += grad_proj[b * BR : b * BR + half]
        acc_ref[1, at : at + half] += grad_proj[b * BR + half : (b + 1) * BR]
    grad_mixed = dot_nt(mid_low, pw_ref[...])
    gh_ref[0] = grad_mixed[:WIN, :BR].astype(BF16)
    gh_ref[1] = grad_mixed[WIN:, :BR].astype(BF16)
    whole[...] = grad_mixed[:, BR:]
    split_columns(whole, left, right)
    gk_ref[0] = jnp.where(first_half, left[...], right[...]).astype(BF16)
    gs_ref[0] = pltpu.roll(jnp.where(first_half, right[...], left[...]), half, 1).astype(BF16)
    if last:

        @pl.when(step == 1)
        def _():
            for s in range(2):
                for j in range(2, 4):
                    cut = slice(j * CHUNK, (j + 1) * CHUNK)
                    acc_ref[s, cut] = acc_ref[s, cut].T
            core, along = core_place(info), along_place(info)
            rows = GRAD_ROWS // 4
            for s in range(2):
                for near in range(2):
                    side = along if near == 0 else 1 - along
                    mine = pl.multiple_of((2 * core + side) * rows, 8)
                    theirs = pl.multiple_of((2 * (1 - core) + side) * rows, 8)
                    kept_ref[s, near] = acc_ref[s, pl.ds(mine, rows)].astype(BF16)
                    sent_ref[s, near] = acc_ref[s, pl.ds(theirs, rows)].astype(BF16)


def backward_sums(rows, unit, acc_ref, sum_ref):
    acc_ref[...] += dot_tn(unit, rows)
    sum_ref[...] += dot(jnp.ones((8, WIN), BF16), rows)


def columns_backward_kernel(
    image, heights, info, gk_ref, gr_ref, p_ref, q_ref, k_ref, v_ref, o_ref, rl_ref, n_ref, wt_ref,
    taps_ref, acc_ref, sum_ref, lepe_ref, keep_ref, send_ref,
    grad_ref, out_ref, kb_ref, vb_ref, ds_ref,
):
    step = pl.program_id(0)
    place = tensor_place(info)
    height, width = sides(image, heights, info)

    @pl.when(step == 0)
    def _():
        set_indicator(vb_ref)
        acc_ref[...] = jnp.zeros_like(acc_ref)
        sum_ref[...] = jnp.zeros_like(sum_ref)
        lepe_ref[...] = jnp.zeros_like(lepe_ref)
        for source, side in ((gk_ref, place), (gr_ref, 1 - place)):
            for s in range(2):
                start = pl.multiple_of(side * PAIR + s * WIN, 8)
                grad_ref[pl.ds(start, WIN)] = source[s].astype(F32)

    refs = (p_ref, q_ref, k_ref, v_ref, o_ref, rl_ref, kb_ref, vb_ref, ds_ref)
    for k in range(2):
        column = (2 * step + k) * STRIPE
        grads = jnp.concatenate(
            [grad_ref[pl.ds(column + q, PH, stride=HALF)] for q in range(STRIPE)], axis=0
        )
        base = place * HALF + column
        rows, tap_rows = window_backward(
            grads, base, width, height, taps_ref[1, :9], 2 * step, k, refs
        )
        for index, item in enumerate(tap_rows):
            lepe_ref[index : index + 1] += item
        backward_sums(rows, n_ref[2 * step + k], acc_ref, sum_ref)
        back = dot(rows, wt_ref[1])
        for q in range(STRIPE):
            cut = slice(q * PH, (q + 1) * PH)
            out_ref[0, pl.ds(column + q, PH, stride=HALF)] = back[cut, :BR]
            out_ref[1, pl.ds(column + q, PH, stride=HALF)] = back[cut, BR:]

    @pl.when(step == 1)
    def _():
        for s in range(2):
            keep = pl.multiple_of(place * PAIR + s * WIN, 8)
            send = pl.multiple_of((1 - place) * PAIR + s * WIN, 8)
            for j in range(2):
                lanes = slice(j * BR, (j + 1) * BR)
                keep_ref[s, :, lanes] = out_ref[j, pl.ds(keep, WIN)].astype(BF16)
                send_ref[s, :, lanes] = out_ref[j, pl.ds(send, WIN)].astype(BF16)


def direction_grads(acc, sums, gain, bias, weight_t):
    moved = acc.T
    shift = sums[0:1]
    high = shift.astype(BF16)
    low = (shift - high.astype(F32)).astype(BF16)
    wide = dot(high, weight_t) + dot(low, weight_t)
    column = sums.T[:, 0:1]
    grad_qkv = moved * gain + column * bias
    grad_gain = jnp.sum(weight_t.astype(F32) * moved, 0, keepdims=True)
    return grad_qkv, grad_gain, wide


def rows_backward_kernel(image, last, others, *refs):
    (
        heights, info, x_ref, gm_ref, p_ref, q_ref, k_ref, v_ref, o_ref, rl_ref, wt_ref, taps_ref,
    ) = refs[:12]
    refs = refs[12:]
    if last:
        gain_ref, bias_ref, small2_ref = refs[:3]
        other_refs = refs[3 : 3 + 3 * others]
        refs = refs[3 + 3 * others :]
        gp_ref, kept_ref, sent_ref = refs[:3]
        acc_ref, sum_ref, lepe_ref, pack_ref, kb_ref, vb_ref, ds_ref = refs[3:]
    else:
        gp_ref, acc_ref, sum_ref, lepe_ref, kb_ref, vb_ref, ds_ref = refs
    step = pl.program_id(0)
    height, width = sides(image, heights, info)
    row_base = tensor_place(info) * HALF + step * 2 * STRIPE

    @pl.when(step == 0)
    def _():
        set_indicator(vb_ref)
        acc_ref[...] = jnp.zeros_like(acc_ref)
        sum_ref[...] = jnp.zeros_like(sum_ref)
        lepe_ref[...] = jnp.zeros_like(lepe_ref)

    mask = twice(as_float(inside(split_index(PAIR, PW, BR), row_base, 0, height, width)))
    unit, _ = norm_parts(x_ref[0].astype(F32) * mask)
    refs = (p_ref, q_ref, k_ref, v_ref, o_ref, rl_ref, kb_ref, vb_ref, ds_ref)
    first_window = 2 * step
    for k in range(2):
        base = row_base + k * STRIPE
        rows, tap_rows = window_backward(
            gm_ref[k].astype(F32), base, height, width, taps_ref[0, :9], first_window, k, refs
        )
        for index, item in enumerate(tap_rows):
            lepe_ref[index : index + 1] += item
        gp_ref[k] = rows
        backward_sums(rows, unit[k * WIN : (k + 1) * WIN].astype(BF16), acc_ref, sum_ref)
    if last:

        @pl.when(step == 1)
        def _():
            row_items = [acc_ref[...], sum_ref[...], lepe_ref[...]]
            column_items = [0.0, 0.0, 0.0]
            for at in range(others):
                kind = other_refs[3 * at : 3 * at + 3]
                if at % 2 == 0:
                    column_items = [old + ref[...] for old, ref in zip(column_items, kind)]
                else:
                    row_items = [old + ref[...] for old, ref in zip(row_items, kind)]
            gain, bias = gain_ref[...], bias_ref[...]
            grad_gain = grad_bias = 0.0
            half = BR // 2
            for direction, items in enumerate((row_items, column_items)):
                grad_qkv, gain_row, bias_row = direction_grads(
                    items[0], items[1], gain, bias, wt_ref[direction]
                )
                grad_gain = grad_gain + gain_row
                grad_bias = grad_bias + bias_row
                for s in range(2):
                    for item in range(3):
                        at = direction * 3 * half + item * half
                        take = item * BR + s * half
                        pack_ref[s, at : at + half] = grad_qkv[take : take + half]
            small2 = small2_ref[...]
            for s in range(2):
                cut = slice(s * half, (s + 1) * half)
                lepe = jnp.concatenate(
                    [row_items[2][:, cut], column_items[2][:, cut], jnp.zeros((16, BR), F32)], axis=1
                )
                head = jnp.concatenate(
                    [grad_gain, grad_bias, small2[:4], small2[4 + 2 * s : 6 + 2 * s]], axis=0
                )
                pack_ref[s, SMALL_AT : SMALL_AT + 8] = head
                pack_ref[s, SMALL_AT + 8 : SMALL_AT + 24] = lepe
                pack_ref[s, SMALL_AT + 24 :] = jnp.zeros((LAST_ROWS - SMALL_AT - 24, 2 * BR), F32)
            core = core_place(info)
            rows = LAST_ROWS // 2
            for s in range(2):
                mine = pl.multiple_of(core * rows, 8)
                theirs = pl.multiple_of((1 - core) * rows, 8)
                kept_ref[s] = pack_ref[s, pl.ds(mine, rows)].astype(BF16)
                sent_ref[s] = pack_ref[s, pl.ds(theirs, rows)].astype(BF16)


def input_kernel(image, first, *refs):
    heights, info, x_ref, gp_ref, gmid_ref, vk_ref, vr_ref, wt_ref, gain_ref = refs[:9]
    refs = refs[9:] if first else refs[10:]
    out_ref, mark_ref, whole, left, right = refs
    mark_ref[...] = jnp.zeros_like(mark_ref)
    step = pl.program_id(0)
    place = tensor_place(info)
    height, width = sides(image, heights, info)
    row_base = place * HALF + step * 2 * STRIPE
    mask = twice(as_float(inside(split_index(PAIR, PW, BR), row_base, 0, height, width)))
    unit, inverse = norm_parts(x_ref[0].astype(F32) * mask)
    first_half = place == 0
    own = vk_ref[0].astype(F32)
    other = vr_ref[0].astype(F32)
    left[...] = jnp.where(first_half, own, other)
    right[...] = jnp.where(first_half, other, own)
    merge_columns(left, right, whole)
    parts = [dot(gp_ref[k], wt_ref[0]) for k in range(2)]
    grad_normed = jnp.concatenate(parts, axis=0) + whole[...]
    back = norm_back(grad_normed, unit, inverse, gain_ref[...])
    out_ref[0] = (mask * (gmid_ref[0] + back)).astype(BF16)


def unpack_kernel(
    info, a_ref, ax_ref, b_ref, bx_ref, c_ref, cx_ref,
    fc1_ref, fc2_ref, proj_ref, qkv_ref, lepe_ref, shift_ref, b1_ref,
    gain1_ref, bias1_ref, gain2_ref, bias2_ref, projb_ref, b2_ref,
):
    core, along = core_place(info) == 0, along_place(info) == 0
    quarters = []
    for c in range(2):
        for side in range(2):
            here = core if c == 0 else jnp.logical_not(core)
            near = along if side == 0 else jnp.logical_not(along)
            mine = jnp.where(near, a_ref[...].astype(F32), ax_ref[...].astype(F32))
            theirs = jnp.where(near, b_ref[...].astype(F32), bx_ref[...].astype(F32))
            quarters.append(jnp.where(here, mine, theirs))
    total = jnp.concatenate(quarters, axis=0)
    fc1_ref[:, :CHUNK] = total[:CHUNK]
    fc1_ref[:, CHUNK:] = total[CHUNK : 2 * CHUNK]
    fc2_ref[...] = total[2 * CHUNK : 4 * CHUNK]
    proj_ref[...] = total[4 * CHUNK :]
    mine, theirs = c_ref[...].astype(F32), cx_ref[...].astype(F32)
    last = jnp.concatenate([jnp.where(core, mine, theirs), jnp.where(core, theirs, mine)], axis=0)
    half = BR // 2
    for direction in range(2):
        for item in range(3):
            at = direction * 3 * half + item * half
            qkv_ref[item, direction] = last[at : at + half]
    small = last[SMALL_AT : SMALL_AT + 24]
    for row, ref in enumerate((gain1_ref, bias1_ref, gain2_ref, bias2_ref, projb_ref, b2_ref)):
        ref[...] = small[row : row + 1]
    b1_ref[...] = small[6:8]
    for tap in range(9):
        turned = 8 + 3 * (tap % 3) + tap // 3
        lepe_ref[tap, 0:1] = small[8 + tap : 9 + tap, :half]
        lepe_ref[tap, 1:2] = small[turned : turned + 1, half : 2 * half]
    shift_ref[0:1] = small[17:18, :half]
    shift_ref[1:2] = small[17:18, half : 2 * half]


def spec(shape, index=None):
    if index is None:
        return pl.BlockSpec(shape, lambda i: (0,) * len(shape))
    return pl.BlockSpec(shape, index)


def shaped(shape, dtype):
    return jax.ShapeDtypeStruct(shape, dtype)


SCALARS = pl.BlockSpec(memory_space=pltpu.SMEM)
RESIDENT = pl.BlockSpec(memory_space=pltpu.VMEM)


def call(
    kernel, name, grid, in_specs, out_specs, out_shape, scratch, micros, limit, aliases=None
):
    return pl.pallas_call(
        kernel,
        name=name,
        grid=(grid,),
        in_specs=in_specs,
        out_specs=out_specs,
        out_shape=out_shape,
        scratch_shapes=scratch,
        input_output_aliases=aliases or {},
        cost_estimate=pl.CostEstimate(
            flops=int(micros * FLOPS_PER_MICRO), bytes_accessed=0, transcendentals=0
        ),
        compiler_params=pltpu.CompilerParams(
            vmem_limit_bytes=limit * MIB, dimension_semantics=("arbitrary",)
        ),
    )


def kept_shapes(count):
    return [pltpu.VMEM((count, WIN, WIDE), BF16)] + [
        pltpu.VMEM((count, WIN, BR), BF16) for _ in range(4)
    ] + [pltpu.VMEM((count, WIN, BR), F32)]


def resident(arrays):
    return [pltpu.with_memory_space_constraint(item, pltpu.VMEM) for item in arrays]


def in_hbm(arrays):
    return [pltpu.with_memory_space_constraint(item, pltpu.HBM) for item in arrays]


def forward_scratch():
    return [
        pltpu.VMEM((2, WIDE, BR), BF16),
        pltpu.VMEM((2, WIDE, 2 * BR), BF16),
        pltpu.VMEM((2, WIN, BR), F32),
        pltpu.VMEM((2, WIN, BR), F32),
        pltpu.VMEM((WIN, WIDE), F32),
    ]


def backward_scratch():
    return [
        pltpu.VMEM((2, WIDE, BR), BF16),
        pltpu.VMEM((2, WIDE, 2 * BR), BF16),
        pltpu.VMEM((2, WIN, WIDE), BF16),
    ]


FLOPS_PER_MICRO = 1.15e9
ATTENTION_LIMIT = 15
MLP_LIMIT = 18


def pack_first(info, qkv, lepe, shift):
    width = qkv.shape[-1]
    return call(
        pack_kernel, "pack", 1, [SCALARS, spec(qkv.shape), spec(lepe.shape), spec(shift.shape)],
        [spec((2 * FIRST_HALF, width)), spec((FIRST_HALF, width))],
        [shaped((2 * FIRST_HALF, width), BF16), shaped((FIRST_HALF, width), BF16)], [], 1, 8,
    )(info, *in_hbm([qkv, lepe, shift]))


def pack_late(info, w1, w2, proj, vectors):
    width = w2.shape[1]
    rows = 4 * LATE
    return call(
        late_pack_kernel, "pack_late", 1,
        [SCALARS, spec(w1.shape), spec(w2.shape), spec(proj.shape), spec(vectors.shape)],
        [spec((rows, width)), spec((LATE, width))],
        [shaped((rows, width), BF16), shaped((LATE, width), BF16)], [], 1, 8,
    )(info, w1, w2, proj, vectors)


def split_quadrants(info, x_pairs):
    count, _, width = x_pairs.shape
    images = count // 2
    block = (1, WIN, width)

    def clamp(image):
        return lambda i: (jnp.clip(i - 2 * image, 0, 1), 0, 0)

    return call(
        partial(quadrant_kernel, images), "quadrants", count,
        [SCALARS, spec((1, PAIR, width), lambda i: (i, 0, 0))],
        [spec(block, lambda i: (i, 0, 0))] + [spec(block, clamp(image)) for image in range(images)],
        [shaped((count, WIN, width), BF16)] + [shaped((2, WIN, width), BF16)] * images,
        [pltpu.VMEM((PAIR, width), F32), pltpu.VMEM((WIN, width), F32), pltpu.VMEM((WIN, width), F32)],
        2, 16,
    )(info, x_pairs)


def rows_forward(image, heights, info, x_pairs, gain, bias, packs, known):
    count, _, width = x_pairs.shape
    pair = spec((1, PAIR, width), lambda i: (2 * image + i, 0, 0))
    in_specs = [SCALARS, SCALARS, pair, spec((1, width)), spec((1, width))]
    operands = [heights, info, x_pairs, gain, bias]
    out_shapes = kept_shapes(4) + [pltpu.VMEM((4, WIN, BR), BF16)]
    scratch = forward_scratch()
    if known is None:
        in_specs += [spec(item.shape) for item in packs]
        operands += list(packs)
        scratch = [pltpu.VMEM((2 * FIRST_HALF, width), BF16)] + scratch
        out_shapes += [
            pltpu.VMEM((2, width, 3 * BR), BF16), pltpu.VMEM((2, 3 * BR, width), BF16),
            pltpu.VMEM((2, 16, BR), F32),
        ]
    else:
        in_specs += [RESIDENT] * 2
        operands += resident(known)
    return call(
        partial(rows_forward_kernel, image, known is None), "rows_forward", 2, in_specs,
        [RESIDENT] * len(out_shapes), out_shapes, scratch,
        6.5, ATTENTION_LIMIT,
    )(*operands)


def columns_forward(image, heights, info, own, other, gain, bias, weight, taps):
    width = own.shape[2]
    fixed = spec((2, WIN, BR), lambda i: (0, 0, 0))
    return call(
        partial(columns_forward_kernel, image), "columns_forward", 2,
        [
            SCALARS, SCALARS, spec((2, WIN, width), lambda i: (image, 0, 0)), spec((2, WIN, width)),
            spec((1, width)), spec((1, width)), RESIDENT, RESIDENT,
        ],
        [RESIDENT] * 7 + [fixed, fixed],
        kept_shapes(4) + [pltpu.VMEM((4, WIN, width), BF16)] + [shaped((2, WIN, BR), BF16)] * 2,
        [pltpu.VMEM((2, 2 * PAIR, BR), F32), pltpu.VMEM((2 * PAIR, BR), F32)] + forward_scratch(),
        6.5, ATTENTION_LIMIT,
    )(heights, info, own, other, gain, bias, *resident([weight, taps]))


def mlp(image, last, heights, info, x_pairs, cot_pairs, mixed_rows, mixed_own, mixed_other, params, previous):
    count, _, width = x_pairs.shape
    gain, bias, *late = params
    pair = spec((1, PAIR, width), lambda i: (2 * image + i, 0, 0))
    part = spec((1, WIN, BR), lambda i: (i, 0, 0))
    row = spec((1, width))
    sums = [RESIDENT, RESIDENT]
    sum_shapes = [pltpu.VMEM((2, GRAD_ROWS, width), F32), pltpu.VMEM((8, width), F32)]
    in_specs = [
        SCALARS, SCALARS, pair, pair, spec((2, WIN, BR), lambda i: (i, 0, 0)), part, part, row, row,
        *[RESIDENT] * 5,
    ]
    operands = [
        heights, info, x_pairs, cot_pairs, mixed_rows, mixed_own, mixed_other, gain, bias,
        *resident(late),
    ]
    aliases = {}
    first = previous is None
    if not first:
        in_specs += sums + [pl.BlockSpec(memory_space=pl.ANY)]
        operands += [*resident(previous[:2]), previous[2]]
        at = len(operands) - 3
        aliases = {at: 5, at + 1: 6, at + 2: 0}
    out_specs = [
        pair, spec((1, PAIR, width), lambda i: (i, 0, 0)), spec((2, WIN, BR), lambda i: (i, 0, 0)),
        part, part,
    ] + sums
    out_shapes = [
        shaped(x_pairs.shape, BF16), shaped((2, PAIR, width), F32), shaped((4, WIN, BR), BF16),
        shaped((2, WIN, BR), BF16), shaped((2, WIN, BR), BF16),
    ] + sum_shapes
    if last:
        quarter = (2, 2, GRAD_ROWS // 4, width)
        out_specs += [spec(quarter), spec(quarter)]
        out_shapes += [shaped(quarter, BF16), shaped(quarter, BF16)]
    return call(
        partial(mlp_kernel, image, first, last), "feed_forward", 2, in_specs, out_specs, out_shapes,
        [
            pltpu.VMEM((2 * BR, width), BF16), pltpu.VMEM((8 * LATE, width), BF16),
            pltpu.VMEM((PAIR, BR), F32), pltpu.VMEM((WIN, BR), F32), pltpu.VMEM((WIN, BR), F32),
            pltpu.VMEM((PAIR, width), F32), pltpu.VMEM((PAIR, width), F32),
            pltpu.VMEM((PAIR, width), BF16), pltpu.VMEM((PAIR, width), BF16),
            pltpu.VMEM((width, PAIR), BF16), pltpu.VMEM((width, PAIR), BF16),
        ],
        15, MLP_LIMIT, aliases,
    )(*operands)


def columns_backward(image, heights, info, grad_own, grad_other, kept, unit, weight_t, taps):
    width = weight_t.shape[2]
    fixed = spec((2, WIN, width))
    grads = spec((2, WIN, BR))
    return call(
        partial(columns_backward_kernel, image), "columns_backward", 2,
        [SCALARS, SCALARS, grads, grads] + [RESIDENT] * 9,
        [spec((width, 3 * BR)), spec((8, 3 * BR)), spec((16, BR)), fixed, fixed],
        [shaped((width, 3 * BR), F32), shaped((8, 3 * BR), F32), shaped((16, BR), F32)]
        + [shaped((2, WIN, width), BF16)] * 2,
        [pltpu.VMEM((2 * PAIR, BR), F32), pltpu.VMEM((2, 2 * PAIR, BR), F32)] + backward_scratch(),
        9.7, ATTENTION_LIMIT,
    )(heights, info, grad_own, grad_other, *resident([*kept, unit, weight_t, taps]))


def rows_backward(image, heights, info, x_pairs, grad_mixed, kept, weight_t, taps, final):
    width = weight_t.shape[2]
    pair = spec((1, PAIR, width), lambda i: (2 * image + i, 0, 0))
    in_specs = [SCALARS, SCALARS, pair, spec((2, WIN, BR), lambda i: (i, 0, 0))] + [RESIDENT] * 8
    operands = [heights, info, x_pairs, grad_mixed, *resident([*kept, weight_t, taps])]
    sum_shapes = [(width, 3 * BR), (8, 3 * BR), (16, BR)]
    out_specs = [spec((2, WIN, 3 * BR), lambda i: (i, 0, 0))]
    out_shapes = [shaped((4, WIN, 3 * BR), BF16)]
    scratch = backward_scratch()
    others = 0
    if final is None:
        out_specs += [spec(shape) for shape in sum_shapes]
        out_shapes += [shaped(shape, F32) for shape in sum_shapes]
    else:
        gain, bias, small2, items = final
        others = len(items)
        in_specs += [spec((1, width)), spec((1, width)), spec((8, width))]
        operands += [gain, bias, small2]
        for item in items:
            in_specs += [spec(shape) for shape in sum_shapes]
            operands += list(item)
        half = (2, LAST_ROWS // 2, width)
        out_specs += [spec(half), spec(half)]
        out_shapes += [shaped(half, BF16), shaped(half, BF16)]
        scratch = (
            [pltpu.VMEM(shape, F32) for shape in sum_shapes]
            + [pltpu.VMEM((2, LAST_ROWS, width), F32)]
            + scratch
        )
    return call(
        partial(rows_backward_kernel, image, final is not None, others), "rows_backward", 2,
        in_specs, out_specs, out_shapes, scratch, 9.7, ATTENTION_LIMIT,
    )(*operands)


def input_rows(image, heights, info, x_pairs, rows, grad_mid, back_own, back_other, weight_t, gain, previous):
    width = weight_t.shape[2]
    pair = spec((1, PAIR, width), lambda i: (2 * image + i, 0, 0))
    part = spec((1, WIN, width), lambda i: (i, 0, 0))
    in_specs = [
        SCALARS, SCALARS, pair, spec((2, WIN, 3 * BR), lambda i: (i, 0, 0)),
        spec((1, PAIR, width), lambda i: (i, 0, 0)), part, part, RESIDENT, spec((1, width)),
    ]
    operands = [
        heights, info, x_pairs, rows, grad_mid, back_own, back_other, *resident([weight_t]), gain,
    ]
    aliases = {}
    if previous is not None:
        in_specs.append(pl.BlockSpec(memory_space=pl.ANY))
        operands.append(previous)
        aliases = {len(operands) - 1: 0}
    return call(
        partial(input_kernel, image, previous is None), "input_rows", 2, in_specs,
        [pair, spec((8, 128))], [shaped(x_pairs.shape, BF16), shaped((8, 128), F32)],
        [pltpu.VMEM((PAIR, width), F32), pltpu.VMEM((WIN, width), F32), pltpu.VMEM((WIN, width), F32)],
        3.1, 20, aliases,
    )(*operands)


def unpack(info, a, ax, b, bx, c, cx, hidden, width):
    row = spec((1, width))
    rows = a.shape[0]
    last = c.shape[0]
    return call(
        unpack_kernel, "unpack", 1,
        [SCALARS] + [spec((rows, width))] * 4 + [spec((last, width))] * 2,
        [
            spec((width, hidden)), spec((hidden, width)), spec((BR, width)), spec((3, 2, BR // 2, width)),
            spec((9, 2, BR // 2)), spec((2, BR // 2)), spec((2, width)), row, row, row, row, row, row,
        ],
        [
            shaped((width, hidden), F32), shaped((hidden, width), F32), shaped((BR, width), F32),
            shaped((3, 2, BR // 2, width), F32), shaped((9, 2, BR // 2), F32), shaped((2, BR // 2), F32),
            shaped((2, width), F32),
        ] + [shaped((1, width), F32)] * 6,
        [], 1.3, 16,
    )(info, a, ax, b, bx, c, cx)


def after(value, *marks):
    return lax.optimization_barrier((value,) + marks)[0]


def swap_tensor(values):
    return lax.ppermute(values, "tensor", [(0, 1), (1, 0)])


def swap_dp(values, size, mask):
    return lax.ppermute(values, "dp", [(i, i ^ mask) for i in range(size)])


def swap_both(values, size, mask):
    pairs = [(2 * i + t, 2 * (i ^ mask) + 1 - t) for i in range(size) for t in range(2)]
    return lax.ppermute(values, ("dp", "tensor"), pairs)


def add_kernel(count, *refs):
    refs, outs = refs[:count], refs[count:]
    items = [ref[...].astype(F32) for ref in refs]
    while len(items) > 1:
        items = [items[i] + items[i + 1] for i in range(0, len(items), 2)]
    whole = items[0].astype(BF16)
    whole = whole.reshape((len(outs),) + outs[0].shape)
    for at, out in enumerate(outs):
        out[...] = whole[at]


def added(*items, parts=1):
    shape = items[0].shape
    last = shape[-2:]
    outs = call(
        partial(add_kernel, len(items)), "add", 1, [spec(shape)] * len(items), [spec(last)] * parts,
        [shaped(last, BF16)] * parts, [], 0.5, 8,
    )(*items)
    return outs[0] if parts == 1 else outs


def partner_groups(size):
    bits = list(range(1, size.bit_length() - 1))
    groups = []
    while bits:
        pair, bits = bits[:2], bits[2:]
        low = 1 << pair[0]
        groups.append([low] if len(pair) == 1 else [low, 1 << pair[1], low | (1 << pair[1])])
    return groups


def per_device(
    size, block_input, heights, widths, norm1_gain, norm1_bias, qkv_weight, lepe_weight, lepe_bias,
    proj_weight, proj_bias, norm2_gain, norm2_bias, fc1_weight, fc1_bias, fc2_weight, fc2_bias,
    cotangent,
):
    images, local_cells, width = block_input.shape
    hidden = fc1_weight.shape[1]
    x_pairs = block_input.reshape(2 * images, PAIR, width)
    cot_pairs = cotangent.reshape(2 * images, PAIR, width)
    gain1, bias1 = norm1_gain[None], norm1_bias[None]
    pairs = range(images)
    index = lax.axis_index("dp")
    places = jnp.stack([lax.axis_index("tensor"), index % 2, index // 2 % 2]).astype(jnp.int32)
    info = jnp.concatenate([widths, places])

    own, own_half = pack_first(
        info, qkv_weight.transpose(1, 2, 3, 0), lepe_weight.transpose(1, 0, 2), lepe_bias
    )
    near = swap_tensor(own_half)
    far = swap_dp(near, size, 1)
    quad_own, *quad_send = split_quadrants(info, after(x_pairs, own))
    vectors = jnp.concatenate([fc1_bias, proj_bias, fc2_bias]).reshape(-1, width)
    late_own, late_send = pack_late(info, *after((fc1_weight, fc2_weight, proj_weight, vectors), quad_own))
    quad_other = [swap_tensor(quad_send[0])]

    row_kept, mixed_rows = [], []
    known = None
    for image in pairs:
        *kept, mixed = rows_forward(
            image, after(heights, late_own), info, x_pairs, gain1, bias1, (own, near, far), known
        )
        if known is None:
            *kept, mixed, weight, weight_t, taps = [*kept, mixed]
            known = (weight, taps)
        row_kept.append(kept)
        mixed_rows.append(mixed)
        if image + 1 < images:
            quad_other.append(swap_tensor(after(quad_send[image + 1], taps)))
    late_near = swap_tensor(after(late_send, mixed_rows[-1]))
    columns = []
    for image in pairs:
        *kept, unit, keep, send = columns_forward(
            image, heights, info, quad_own, quad_other[image], gain1, bias1, weight, taps
        )
        columns.append((kept, unit, keep, swap_tensor(send)))
        if image == 0:
            ready = after(late_near, keep)
            late_parts = [ready] + [swap_dp(ready, size, mask) for mask in (2, 1, 3)]
    params = (norm2_gain[None], norm2_bias[None], late_own, *late_parts)
    previous = None
    middle = []
    for image in pairs:
        _, _, keep, arrived = columns[image]
        output, grad_mid, grad_rows, grad_keep, grad_send, *sums = mlp(
            image, image == images - 1, heights, info, x_pairs, cot_pairs, mixed_rows[image], keep,
            arrived, params, previous,
        )
        previous = (sums[0], sums[1], output)
        middle.append((grad_mid, grad_rows, grad_keep, swap_tensor(grad_send)))
    _, small2, kept1, sent1 = sums

    arrived = swap_dp(sent1, size, 1)
    row_rows = []
    rows, *row_sums = rows_backward(
        0, heights, info, x_pairs, middle[0][1], row_kept[0], weight_t, taps, None
    )
    row_rows.append((rows, row_sums))
    first, toward_x, toward_y, toward_xy = added(kept1, after(arrived, row_sums[2]), parts=4)
    crossed = [swap_dp(toward_x, size, 2), swap_tensor(toward_y), swap_both(toward_xy, size, 2)]
    column_back = []
    bits = size.bit_length() - 1
    now = after(heights, first)
    for image in pairs:
        kept, unit, _, _ = columns[image]
        _, _, grad_keep, grad_other = middle[image]
        *column_sums, back_keep, back_send = columns_backward(
            image, now, info, grad_keep, grad_other, kept, unit, weight_t, taps
        )
        column_back.append((column_sums, back_keep, swap_tensor(back_send)))
        if image == 0:
            first = added(first, *[after(item, column_sums[2]) for item in crossed])
        else:
            first = added(first, after(arrived, column_sums[2]))
        now = after(heights, first)
        bit = 2 + image
        arrived = swap_dp(first, size, 1 << bit) if bit < bits else jnp.zeros_like(first)
    for image in range(1, images):
        final = None
        if image == images - 1:
            order = []
            for at in range(images):
                order.append(column_back[at][0])
                if at < len(row_rows):
                    order.append(row_rows[at][1])
            final = (gain1, bias1, small2, order)
        now = after(heights, column_back[0][2], first)
        rows, *row_sums = rows_backward(
            image, now, info, x_pairs, middle[image][1], row_kept[image], weight_t, taps, final
        )
        row_rows.append((rows, row_sums))
    kept2, sent2 = row_sums

    input_grad = None

    def meanwhile(image, sent):
        nonlocal input_grad
        _, back_keep, back_other = column_back[image]
        input_grad, mark = input_rows(
            image, after(heights, sent), info, x_pairs, row_rows[image][0], middle[image][0],
            back_keep, back_other, weight_t, gain1, input_grad,
        )
        return mark

    later = swap_dp(sent2, size, 1)
    first = added(first, after(arrived, kept2))
    for bit in range(2 + images, bits):
        first = added(first, swap_dp(first, size, 1 << bit))
    first_x = swap_dp(first, size, 2)
    last, toward_y = added(kept2, after(later, first), parts=2)
    arrived = swap_tensor(toward_y)
    mark = meanwhile(images - 1, last)
    last = added(last, after(arrived, mark, first_x))
    first_core = [swap_dp(first, size, 1), swap_dp(first_x, size, 1)]
    waiting = list(range(images - 1))
    for group in partner_groups(size):
        arrived = [swap_dp(last, size, mask) for mask in group]
        if waiting:
            mark = meanwhile(waiting.pop(), last)
        last = added(last, *[after(item, mark, *first_core) for item in arrived])
    last_other = swap_dp(last, size, 1)
    (
        grad_fc1, grad_fc2, grad_proj, grad_qkv, grad_lepe, grad_shift, grad_b1,
        grad_gain1, grad_bias1, grad_gain2, grad_bias2, grad_projb, grad_b2,
    ) = unpack(info, first, first_x, first_core[0], first_core[1], last, last_other, hidden, width)
    return (
        output.reshape(block_input.shape), input_grad.reshape(block_input.shape),
        grad_gain1[0], grad_bias1[0], grad_qkv.transpose(3, 0, 1, 2), grad_lepe.transpose(1, 0, 2),
        grad_shift, grad_proj.reshape(2, BR // 2, width), grad_projb[0], grad_gain2[0], grad_bias2[0],
        grad_fc1, grad_b1.reshape(-1), grad_fc2, grad_b2[0],
    )


def solution(mesh):
    placed = (
        P("dp", "tensor", None),
        P("dp"),
        P("dp"),
        P(),
        P(),
        P(None, None, None, "tensor"),
        P(None, None, "tensor"),
        P(None, "tensor"),
        P(None, "tensor", None),
        P(),
        P(),
        P(),
        P(None, "tensor"),
        P("tensor"),
        P("tensor", None),
        P(),
        P("dp", "tensor", None),
    )
    return jax.shard_map(
        partial(per_device, mesh.shape["dp"]),
        mesh=mesh,
        in_specs=placed,
        out_specs=(
            P("dp", "tensor", None),
            P("dp", "tensor", None),
            P(),
            P(),
            P(None, None, None, "tensor"),
            P(None, None, "tensor"),
            P(None, "tensor"),
            P(None, "tensor", None),
            P(),
            P(),
            P(),
            P(None, "tensor"),
            P("tensor"),
            P("tensor", None),
            P(),
        ),
        check_vma=False,
    )
```

```python
from functools import partial

import jax
import jax.numpy as jnp
from jax import lax
from jax.experimental import pallas as pl
from jax.experimental.pallas import tpu as pltpu
from jax.sharding import PartitionSpec as P

HEAD_DIM = 32
STRIPE = 7
PH = 56
PW = 56
HEADS = 4
BR = HEADS * HEAD_DIM
WIN = STRIPE * PW
WIDE = HEADS * WIN
MAIN = WIN // 128 * 128
REST = WIN - MAIN
HALF = 28
PAIR = 2 * WIN
CHUNK = 256
CHUNKS = [(lo, min(lo + CHUNK, WIDE)) for lo in range(0, WIDE, CHUNK)]

MASKED = -30.0
EPSILON = 1e-05
LOG2E = 1.4426950408889634
LN2 = 0.6931471805599453
ROOT_HALF = 0.7071067811865476
DENSITY = 0.3989422804014327
DEN_LOW = 2.0**-60
DEN_HIGH = 2.0**100

F32 = jnp.float32
BF16 = jnp.bfloat16
MIB = 2**20
GRAD_ROWS = 1152
LAST_ROWS = 416
SMALL_AT = 3 * BR
FIRST_HALF = 208
LATE = 304


def dot(a, b):
    return jnp.dot(a, b, preferred_element_type=F32)


def dot_nt(a, b):
    return lax.dot_general(a, b, (((1,), (1,)), ((), ())), preferred_element_type=F32)


def dot_tn(a, b):
    return lax.dot_general(a, b, (((0,), (0,)), ((), ())), preferred_element_type=F32)


def split_index(count, width, lanes, axis=0):
    shape = (count, lanes) if axis == 0 else (lanes, count)
    index = lax.broadcasted_iota(jnp.int32, shape, axis)
    step = -(-65536 // width)
    major = lax.shift_right_logical(index * step, 16)
    return major, index - major * width


def inside(parts, base_major, base_minor, lim_major, lim_minor):
    major, minor = parts
    return (major < lim_major - base_major) & (minor < lim_minor - base_minor)


def as_float(flag):
    return jnp.where(flag, 1.0, 0.0).astype(F32)


def twice(values):
    return jnp.concatenate([values, values], axis=1)


def head_lane(head):
    lane = lax.broadcasted_iota(jnp.int32, (1, BR), 1)
    return as_float((lane >= head * HEAD_DIM) & (lane < (head + 1) * HEAD_DIM))


def head_blocks(values):
    lanes = [head_lane(head) for head in range(HEADS)]
    top = [values[:MAIN] * lane for lane in lanes]
    rest = [values[MAIN:] * lane for lane in lanes]
    return jnp.concatenate(top + rest, axis=0)


def from_wide(values):
    rows = []
    for head in range(HEADS):
        own = values[head * HEAD_DIM : (head + 1) * HEAD_DIM]
        rest = HEADS * MAIN + head * REST
        rows.append(
            jnp.concatenate(
                [own[:, head * MAIN : (head + 1) * MAIN], own[:, rest : rest + REST]], axis=1
            )
        )
    return jnp.concatenate(rows, axis=0)


def norm_parts(values):
    centred = values - jnp.mean(values, -1, keepdims=True)
    inverse = lax.rsqrt(jnp.mean(centred * centred, -1, keepdims=True) + EPSILON)
    return centred * inverse, inverse


def norm_back(grad_rows, unit_rows, inverse, gain):
    scaled = grad_rows * gain
    return inverse * (
        scaled
        - jnp.mean(scaled, -1, keepdims=True)
        - unit_rows * jnp.mean(scaled * unit_rows, -1, keepdims=True)
    )


def neighbours(values):
    _, minor = split_index(WIN, PW, BR)
    before = jnp.where(minor == 0, 0.0, pltpu.roll(values, 1, 0))
    after = jnp.where(minor == PW - 1, 0.0, pltpu.roll(values, WIN - 1, 0))
    return before, after


def add_rows(low, mid, high):
    gap = jnp.zeros((PW, mid.shape[1]), F32)
    return (
        mid
        + jnp.concatenate([gap, low[: WIN - PW]], axis=0)
        + jnp.concatenate([high[PW:], gap], axis=0)
    )


def lepe_apply(values, taps):
    before, after = neighbours(values)
    rows = [
        taps[3 * a : 3 * a + 1] * before
        + taps[3 * a + 1 : 3 * a + 2] * values
        + taps[3 * a + 2 : 3 * a + 3] * after
        for a in range(3)
    ]
    return add_rows(rows[0], rows[1], rows[2])


def lepe_back(grads, values, taps):
    before, after = neighbours(grads)
    rows = [
        taps[3 * a : 3 * a + 1] * after
        + taps[3 * a + 1 : 3 * a + 2] * grads
        + taps[3 * a + 2 : 3 * a + 3] * before
        for a in range(3)
    ]
    back = add_rows(rows[2], rows[1], rows[0])
    value_before, value_after = neighbours(values)
    tap_rows = []
    for a in range(3):
        for item in (value_before, values, value_after):
            if a == 0:
                product = grads[PW:] * item[: WIN - PW]
            elif a == 1:
                product = grads * item
            else:
                product = grads[: WIN - PW] * item[PW:]
            tap_rows.append(jnp.sum(product, 0, keepdims=True))
    tap_rows.append(jnp.sum(grads, 0, keepdims=True))
    return back, tap_rows


def window_valid(window_base, lim_major, lim_minor):
    return inside(split_index(WIN, PW, BR), window_base, 0, lim_major, lim_minor)


def window_forward(projected, valid, taps, shift, first, k, refs):
    p_ref, q_ref, k_ref, v_ref, o_ref, rl_ref, kb_ref, vb_ref, lepe_ref, mixed_ref = refs
    queries = (projected[:, :BR] * (HEAD_DIM**-0.5 * LOG2E)).astype(BF16)
    key_rows = projected[:, BR : 2 * BR]
    values = projected[:, 2 * BR :].astype(BF16).astype(F32)
    valid_float = as_float(valid)
    weight = jnp.where(valid, 1.0, jnp.exp(jnp.full((WIN, BR), MASKED, F32)))
    q_ref[first + k] = queries
    k_ref[first + k] = (key_rows * valid_float).astype(BF16)
    v_ref[first + k] = values.astype(BF16)
    kb_ref[k] = head_blocks(key_rows * valid_float).astype(BF16)
    vb_ref[k, :, :BR] = head_blocks(values * weight).astype(BF16)
    vb_ref[k, :, BR:] = head_blocks(weight).astype(BF16)
    for lo, hi in CHUNKS:
        p_ref[first + k, :, lo:hi] = jnp.exp2(dot_nt(queries, kb_ref[k, lo:hi])).astype(BF16)
    sums = dot(p_ref[first + k], vb_ref[k])
    totals = sums[:, BR:]
    inverse = 1.0 / totals
    attended = sums[:, :BR] * inverse
    o_ref[first + k] = attended.astype(BF16)
    rl_ref[first + k] = inverse
    lepe = lepe_apply(values, taps) + shift
    lepe_ref[k] = lepe
    mixed_ref[k] = attended + lepe
    safe = (totals > DEN_LOW) & (totals < DEN_HIGH)
    return jnp.max(jnp.where(safe, 0.0, 1.0))


def window_forward_safe(first, k, refs, s_ref):
    p_ref, q_ref, k_ref, v_ref, o_ref, rl_ref, kb_ref, vb_ref, lepe_ref, mixed_ref = refs
    s_ref[...] = dot_nt(q_ref[first + k], kb_ref[k])
    for head in range(HEADS):
        cut = slice(head * MAIN, (head + 1) * MAIN)
        rest = HEADS * MAIN + head * REST
        left = s_ref[:, cut]
        right = s_ref[:, rest : rest + REST]
        peak = jnp.maximum(jnp.max(left, -1, keepdims=True), jnp.max(right, -1, keepdims=True))
        s_ref[:, cut] = left - peak
        s_ref[:, rest : rest + REST] = right - peak
    for lo, hi in CHUNKS:
        p_ref[first + k, :, lo:hi] = jnp.exp2(s_ref[:, lo:hi]).astype(BF16)
    sums = dot(p_ref[first + k], vb_ref[k])
    inverse = 1.0 / sums[:, BR:]
    attended = sums[:, :BR] * inverse
    o_ref[first + k] = attended.astype(BF16)
    rl_ref[first + k] = inverse
    mixed_ref[k] = attended + lepe_ref[k]


def window_backward(grads, base, lim_major, lim_minor, taps, first, k, refs):
    p_ref, q_ref, k_ref, v_ref, o_ref, rl_ref, kb_ref, vb_ref, ds_ref = refs
    lane = lax.broadcasted_iota(jnp.int32, (WIN, BR), 1)
    scaled = (grads * rl_ref[first + k]).astype(BF16)
    product = scaled.astype(F32) * o_ref[first + k].astype(F32)
    high = product.astype(BF16)
    low = (product - high.astype(F32)).astype(BF16)
    row = lax.broadcasted_iota(jnp.int32, (2 * BR, BR), 0)
    col = lax.broadcasted_iota(jnp.int32, (2 * BR, BR), 1)
    head_of = lax.shift_right_logical(row & (BR - 1), 5)
    picks = as_float((col < 2 * HEADS) & (head_of == (col & (HEADS - 1)))).astype(BF16)
    inner = dot(jnp.concatenate([high, low], axis=1), picks)
    inner_high = inner.astype(BF16).astype(F32)
    extra = jnp.where(lane < HEADS, inner_high, inner - inner_high).astype(BF16)
    left = jnp.concatenate([scaled, extra], axis=1)
    values = v_ref[first + k].astype(F32)
    vb_ref[k, :, :BR] = head_blocks(values).astype(BF16)
    kb_ref[k] = head_blocks(k_ref[first + k].astype(F32)).astype(BF16)
    for lo, hi in CHUNKS:
        grad_probs = dot_nt(left, vb_ref[k, lo:hi])
        ds_ref[k, :, lo:hi] = grad_probs.astype(BF16) * p_ref[first + k, :, lo:hi]
    grad_query = dot(ds_ref[k], kb_ref[k]) * (HEAD_DIM**-0.5)
    query_t = q_ref[first + k].astype(F32).T.astype(BF16)
    scaled_t = scaled.astype(F32).T.astype(BF16)
    valid_t = inside(split_index(WIN, PW, BR, 1), base, 0, lim_major, lim_minor)
    weight_t = jnp.where(valid_t, 1.0, jnp.exp(jnp.full((BR, WIN), MASKED, F32)))
    grad_key = (from_wide(dot(query_t, ds_ref[k])) * jnp.where(valid_t, LN2, 0.0)).T
    grad_value = (from_wide(dot(scaled_t, p_ref[first + k])) * weight_t).T
    back, tap_rows = lepe_back(grads, values, taps)
    out = jnp.concatenate([grad_query, grad_key, grad_value + back], axis=1)
    return out.astype(BF16), tap_rows


def set_indicator(vb_ref):
    row = lax.broadcasted_iota(jnp.int32, (WIDE, BR), 0)
    col = lax.broadcasted_iota(jnp.int32, (WIDE, BR), 1)
    head = jnp.zeros((WIDE, BR), jnp.int32)
    for cut in range(1, HEADS):
        head = head + jnp.where(row >= cut * MAIN, 1, 0)
    tail = lax.shift_right_logical(row - HEADS * MAIN, 3)
    head = jnp.where(row >= HEADS * MAIN, tail, head)
    hit = (col < 2 * HEADS) & ((col & (HEADS - 1)) == head)
    for k in range(2):
        vb_ref[k, :, BR:] = jnp.where(hit, -1.0, 0.0).astype(BF16)


def split_columns(source, left, right):
    for row in range(STRIPE * 2):
        left[row * HALF : (row + 1) * HALF] = source[row * PW : row * PW + HALF]
        right[row * HALF : (row + 1) * HALF] = source[row * PW + HALF : (row + 1) * PW]


def merge_columns(left, right, target):
    for row in range(STRIPE * 2):
        target[row * PW : row * PW + HALF] = left[row * HALF : (row + 1) * HALF]
        target[row * PW + HALF : (row + 1) * PW] = right[row * HALF : (row + 1) * HALF]


def sides(image, heights, info):
    return heights[image], info[image]


def tensor_place(info):
    return info[info.shape[0] - 3]


def core_place(info):
    return info[info.shape[0] - 2]


def along_place(info):
    return info[info.shape[0] - 1]


def pack_kernel(qkv_ref, lepe_ref, shift_ref, out_ref, send_ref):
    for item in range(3):
        for direction in range(2):
            row = (2 * item + direction) * BR // 2
            out_ref[row : row + BR // 2] = qkv_ref[item, direction]
    rows = [
        jnp.concatenate([lepe_ref[tap, 0:1], lepe_ref[tap, 1:2]], axis=1).astype(F32)
        for tap in range(9)
    ]
    rows.append(jnp.concatenate([shift_ref[0:1], shift_ref[1:2]], axis=1).astype(F32))
    rows.append(jnp.zeros((2 * FIRST_HALF - SMALL_AT - 10, BR), F32))
    small = jnp.concatenate(rows, axis=0)
    out_ref[SMALL_AT:] = jnp.concatenate([small, jnp.zeros_like(small)], axis=1).astype(BF16)
    core = lax.axis_index("dp") % 2
    send_ref[...] = out_ref[pl.ds(pl.multiple_of(core * FIRST_HALF, 16), FIRST_HALF)]


def late_pack_kernel(info, w1_ref, w2_ref, proj_ref, vectors_ref, out_ref, send_ref):
    for j in range(2):
        out_ref[j * CHUNK : (j + 1) * CHUNK] = w1_ref[:, j * CHUNK : (j + 1) * CHUNK]
    out_ref[2 * CHUNK : 4 * CHUNK] = w2_ref[...]
    for b in range(2):
        at = 4 * CHUNK + b * BR // 2
        out_ref[at : at + BR // 2] = proj_ref[b]
    vectors = vectors_ref[...].astype(F32)
    tail = jnp.concatenate([vectors, jnp.zeros((4 * LATE - GRAD_ROWS - 4, 2 * BR), F32)], axis=0)
    out_ref[GRAD_ROWS:] = tail.astype(BF16)
    part = 2 * core_place(info) + along_place(info)
    send_ref[...] = out_ref[pl.ds(pl.multiple_of(part * LATE, 16), LATE)]


def quadrant_kernel(images, info, x_ref, own_ref, *rest):
    sends, (whole, left, right) = rest[:images], rest[images:]
    step = pl.program_id(0)
    whole[...] = x_ref[0].astype(F32)
    split_columns(whole, left, right)
    first = tensor_place(info) == 0
    own_ref[0] = jnp.where(first, left[...], right[...]).astype(BF16)
    other = jnp.where(first, right[...], left[...]).astype(BF16)
    for image in range(images):

        @pl.when(step // 2 == image)
        def _():
            sends[image][0] = other


def rows_forward_kernel(image, first, *refs):
    heights, info, x_ref, gain_ref, bias_ref = refs[:5]
    if first:
        own_ref, near_ref, far_ref, p_ref, q_ref, k_ref, v_ref, o_ref, rl_ref, m_ref, w_ref, wt_ref, taps_ref = refs[5:18]
        other_ref = refs[-6]
    else:
        w_ref, taps_ref, p_ref, q_ref, k_ref, v_ref, o_ref, rl_ref, m_ref = refs[5:14]
    kb_ref, vb_ref, lepe_ref, mixed_ref, s_ref = refs[-5:]
    step = pl.program_id(0)
    height, width = sides(image, heights, info)
    row_base = tensor_place(info) * HALF + step * 2 * STRIPE

    def unpack_weights():
        core = core_place(info)
        for part, piece in ((core, near_ref), (1 - core, far_ref)):
            other_ref[pl.ds(pl.multiple_of(part * FIRST_HALF, 16), FIRST_HALF)] = piece[...]
        for direction in range(2):
            for item in range(3):
                row = (2 * item + direction) * BR // 2
                at = item * BR
                wt_ref[direction, at : at + BR // 2] = own_ref[row : row + BR // 2]
                wt_ref[direction, at + BR // 2 : at + BR] = other_ref[row : row + BR // 2]
            w_ref[direction] = wt_ref[direction].astype(F32).T.astype(BF16)
        own = own_ref[SMALL_AT : SMALL_AT + 16].astype(F32)
        other = other_ref[SMALL_AT : SMALL_AT + 16].astype(F32)
        half = BR // 2
        for direction in range(2):
            cut = slice(direction * half, (direction + 1) * half)
            both = jnp.concatenate([own[:, cut], other[:, cut]], axis=1)
            if direction == 1:
                order = [3 * (tap % 3) + tap // 3 for tap in range(9)] + list(range(9, 16))
                both = jnp.concatenate([both[tap : tap + 1] for tap in order], axis=0)
            taps_ref[direction] = both

    if first:
        pl.when(step == 0)(unpack_weights)

    mask = as_float(inside(split_index(PAIR, PW, BR), row_base, 0, height, width))
    unit, _ = norm_parts(x_ref[0].astype(F32) * twice(mask))
    normed = (unit * gain_ref[...] + bias_ref[...]).astype(BF16)
    projected = dot(normed, w_ref[0])
    refs = (p_ref, q_ref, k_ref, v_ref, o_ref, rl_ref, kb_ref, vb_ref, lepe_ref, mixed_ref)
    bad = jnp.float32(0)
    for k in range(2):
        valid = window_valid(row_base + k * STRIPE, height, width)
        rows = projected[k * WIN : (k + 1) * WIN]
        bad = jnp.maximum(
            bad,
            window_forward(rows, valid, taps_ref[0, :9], taps_ref[0, 9:10], 2 * step, k, refs),
        )

    @pl.when(bad > 0.0)
    def _():
        def one(k, carry):
            window_forward_safe(2 * step, k, refs, s_ref)
            return carry

        lax.fori_loop(0, 2, one, 0)

    for k in range(2):
        m_ref[2 * step + k] = mixed_ref[k].astype(BF16)


def columns_forward_kernel(
    image, heights, info, own_ref, other_ref, gain_ref, bias_ref, w_ref, taps_ref,
    p_ref, q_ref, k_ref, v_ref, o_ref, rl_ref, n_ref, keep_ref, send_ref,
    unit_ref, out_ref, kb_ref, vb_ref, lepe_ref, mixed_ref, s_ref,
):
    step = pl.program_id(0)
    place = tensor_place(info)
    height, width = sides(image, heights, info)
    column_base = place * HALF

    @pl.when(step == 0)
    def _():
        for source, side in ((own_ref, place), (other_ref, 1 - place)):
            for s in range(2):
                flag = inside(
                    split_index(WIN, HALF, BR), side * HALF + s * 2 * STRIPE, column_base,
                    height, width,
                )
                unit, _ = norm_parts(source[s].astype(F32) * twice(as_float(flag)))
                start = pl.multiple_of(side * PAIR + s * WIN, 8)
                unit_ref[0, pl.ds(start, WIN)] = unit[:, :BR]
                unit_ref[1, pl.ds(start, WIN)] = unit[:, BR:]

    refs = (p_ref, q_ref, k_ref, v_ref, o_ref, rl_ref, kb_ref, vb_ref, lepe_ref, mixed_ref)
    bad = jnp.float32(0)
    for k in range(2):
        column = (2 * step + k) * STRIPE
        halves = [
            jnp.concatenate(
                [unit_ref[j, pl.ds(column + q, PH, stride=HALF)] for q in range(STRIPE)], axis=0
            )
            for j in range(2)
        ]
        unit = jnp.concatenate(halves, axis=1)
        n_ref[2 * step + k] = unit.astype(BF16)
        normed = (unit * gain_ref[...] + bias_ref[...]).astype(BF16)
        valid = window_valid(column_base + column, width, height)
        rows = dot(normed, w_ref[1])
        bad = jnp.maximum(
            bad,
            window_forward(rows, valid, taps_ref[1, :9], taps_ref[1, 9:10], 2 * step, k, refs),
        )

    @pl.when(bad > 0.0)
    def _():
        def one(k, carry):
            window_forward_safe(2 * step, k, refs, s_ref)
            return carry

        lax.fori_loop(0, 2, one, 0)

    for k in range(2):
        column = (2 * step + k) * STRIPE
        mixed = mixed_ref[k]
        for q in range(STRIPE):
            out_ref[pl.ds(column + q, PH, stride=HALF)] = mixed[q * PH : (q + 1) * PH]

    @pl.when(step == 1)
    def _():
        for s in range(2):
            keep = pl.multiple_of(place * PAIR + s * WIN, 8)
            send = pl.multiple_of((1 - place) * PAIR + s * WIN, 8)
            keep_ref[s] = out_ref[pl.ds(keep, WIN)].astype(BF16)
            send_ref[s] = pltpu.roll(out_ref[pl.ds(send, WIN)], BR // 2, 1).astype(BF16)


def mlp_kernel(images, *refs):
    heights, info, x_ref, cot_ref = refs[:4]
    mh_refs, mo_refs, mr_refs = (refs[4 + i * images : 4 + (i + 1) * images] for i in range(3))
    refs = refs[4 + 3 * images :]
    gain_ref, bias_ref, late_own, *late_parts = refs[:7]
    out_ref, gmid_ref, gh_ref, gk_ref, gs_ref, small_ref, kept_ref, sent_ref = refs[7:15]
    acc_ref, pw_ref, late_ref, whole, left, right, normed_ref, grad_ref, normed_t_ref, grad_t_ref = refs[15:]
    step = pl.program_id(0)
    image, pair = step // 2, step % 2
    place = tensor_place(info)
    height, width = sides(image, heights, info)
    row_base = place * HALF + pair * 2 * STRIPE
    half = BR // 2

    def of_image(items, at):
        value = items[0][at].astype(F32)
        for index in range(1, images):
            value = jnp.where(image == index, items[index][at].astype(F32), value)
        return value

    @pl.when(step == 0)
    def _():
        far = 4 * LATE
        late_ref[:far] = late_own[...]
        core, along = core_place(info), along_place(info)
        for at, piece in enumerate(late_parts):
            part = 2 * (core if at < 2 else 1 - core) + (along if at % 2 == 0 else 1 - along)
            late_ref[pl.ds(pl.multiple_of(far + part * LATE, 16), LATE)] = piece[...]
        for b in range(2):
            at = 4 * CHUNK + b * half
            pw_ref[b * BR : b * BR + half] = late_ref[at : at + half]
            pw_ref[b * BR + half : (b + 1) * BR] = late_ref[far + at : far + at + half]
        acc_ref[...] = jnp.zeros_like(acc_ref)
        small_ref[...] = jnp.zeros_like(small_ref)

    vectors = late_own[GRAD_ROWS : GRAD_ROWS + 16].astype(F32)
    mask = twice(as_float(inside(split_index(PAIR, PW, BR), row_base, 0, height, width)))
    first_half = place == 0
    own = of_image(mo_refs, pair)
    other = of_image(mr_refs, pair)
    left[...] = jnp.where(first_half, own, other)
    right[...] = jnp.where(first_half, other, own)
    merge_columns(left, right, whole)
    rows_part = jnp.concatenate([of_image(mh_refs, 2 * pair + k) for k in range(2)], axis=0)
    mixed = jnp.concatenate([rows_part, whole[...]], axis=1).astype(BF16)
    x_in = x_ref[0].astype(F32) * mask
    x_mid = x_in + dot(mixed, pw_ref[...]) + vectors[2:3]
    unit, inverse = norm_parts(x_mid)
    normed = (unit * gain_ref[...] + bias_ref[...]).astype(BF16)
    grad_result = cot_ref[0].astype(F32) * mask
    grad_low = grad_result.astype(BF16)
    normed_t = normed.astype(F32).T.astype(BF16)
    grad_t = grad_result.T.astype(BF16)
    normed_ref[...] = normed
    grad_ref[...] = grad_low
    normed_t_ref[...] = normed_t
    grad_t_ref[...] = grad_t

    def holder_chunks(holder, carry):
        base = holder * 4 * LATE
        rows = late_ref[base + GRAD_ROWS : base + GRAD_ROWS + 16].astype(F32)
        total, grad_normed = carry
        for part in range(2):
            cut = part * CHUNK
            at = base + cut
            w1, w2 = late_ref[at : at + CHUNK], late_ref[at + 2 * CHUNK : at + 3 * CHUNK]
            pre = dot(normed_ref[...], w1) + rows[part : part + 1]
            bell = jnp.exp2(pre * pre * (-0.5 * LOG2E))
            below = 0.5 + 0.5 * lax.erf(pre * ROOT_HALF)
            hidden = (pre * below).astype(BF16)
            slope = below + pre * bell * DENSITY
            grad_pre = (dot_nt(grad_ref[...], w2) * slope).astype(BF16)
            total = total + dot(hidden, w2)
            grad_normed = grad_normed + dot_nt(grad_pre, w1)
            acc_ref[holder, cut : cut + CHUNK] += dot(normed_t_ref[...], grad_pre)
            acc_ref[holder, cut + 2 * CHUNK : cut + 3 * CHUNK] += dot(grad_t_ref[...], hidden)
            row = 4 + 2 * holder + part
            small_ref[row : row + 1] += jnp.sum(grad_pre.astype(F32), 0, keepdims=True)
        return total, grad_normed

    carry = holder_chunks(0, (x_mid + vectors[3:4], jnp.zeros_like(x_mid)))
    total, grad_normed = holder_chunks(1, carry)
    out_ref[0] = (mask * total).astype(BF16)
    grad_mid = grad_result + norm_back(grad_normed, unit, inverse, gain_ref[...])
    gmid_ref[0] = grad_mid
    small_ref[0:1] += jnp.sum(grad_normed * unit, 0, keepdims=True)
    small_ref[1:2] += jnp.sum(grad_normed, 0, keepdims=True)
    small_ref[2:3] += jnp.sum(grad_mid, 0, keepdims=True)
    small_ref[3:4] += jnp.sum(grad_result, 0, keepdims=True)
    mid_low = grad_mid.astype(BF16)
    grad_proj = dot_tn(mixed, mid_low)
    for b in range(2):
        at = 4 * CHUNK + b * half
        acc_ref[0, at : at + half] += grad_proj[b * BR : b * BR + half]
        acc_ref[1, at : at + half] += grad_proj[b * BR + half : (b + 1) * BR]
    grad_mixed = dot_nt(mid_low, pw_ref[...])
    gh_ref[0] = grad_mixed[:WIN, :BR].astype(BF16)
    gh_ref[1] = grad_mixed[WIN:, :BR].astype(BF16)
    whole[...] = grad_mixed[:, BR:]
    split_columns(whole, left, right)
    gk_ref[0] = jnp.where(first_half, left[...], right[...]).astype(BF16)
    gs_ref[0] = pltpu.roll(jnp.where(first_half, right[...], left[...]), half, 1).astype(BF16)

    @pl.when(step == 2 * images - 1)
    def _():
        for s in range(2):
            for j in range(2, 4):
                cut = slice(j * CHUNK, (j + 1) * CHUNK)
                acc_ref[s, cut] = acc_ref[s, cut].T
        core, along = core_place(info), along_place(info)
        rows = GRAD_ROWS // 4
        for s in range(2):
            for near in range(2):
                side = along if near == 0 else 1 - along
                mine = pl.multiple_of((2 * core + side) * rows, 8)
                theirs = pl.multiple_of((2 * (1 - core) + side) * rows, 8)
                kept_ref[s, near] = acc_ref[s, pl.ds(mine, rows)].astype(BF16)
                sent_ref[s, near] = acc_ref[s, pl.ds(theirs, rows)].astype(BF16)


def backward_sums(rows, unit, acc_ref, sum_ref):
    acc_ref[...] += dot_tn(unit, rows)
    sum_ref[0:1] += jnp.sum(rows.astype(F32), 0, keepdims=True)


def columns_backward_kernel(
    image, heights, info, gk_ref, gr_ref, p_ref, q_ref, k_ref, v_ref, o_ref, rl_ref, n_ref, wt_ref,
    taps_ref, acc_ref, sum_ref, lepe_ref, keep_ref, send_ref,
    grad_ref, out_ref, kb_ref, vb_ref, ds_ref,
):
    step = pl.program_id(0)
    place = tensor_place(info)
    height, width = sides(image, heights, info)

    @pl.when(step == 0)
    def _():
        set_indicator(vb_ref)
        acc_ref[...] = jnp.zeros_like(acc_ref)
        sum_ref[...] = jnp.zeros_like(sum_ref)
        lepe_ref[...] = jnp.zeros_like(lepe_ref)
        for source, side in ((gk_ref, place), (gr_ref, 1 - place)):
            for s in range(2):
                start = pl.multiple_of(side * PAIR + s * WIN, 8)
                grad_ref[pl.ds(start, WIN)] = source[s].astype(F32)

    refs = (p_ref, q_ref, k_ref, v_ref, o_ref, rl_ref, kb_ref, vb_ref, ds_ref)
    for k in range(2):
        column = (2 * step + k) * STRIPE
        grads = jnp.concatenate(
            [grad_ref[pl.ds(column + q, PH, stride=HALF)] for q in range(STRIPE)], axis=0
        )
        base = place * HALF + column
        rows, tap_rows = window_backward(
            grads, base, width, height, taps_ref[1, :9], 2 * step, k, refs
        )
        for index, item in enumerate(tap_rows):
            lepe_ref[index : index + 1] += item
        backward_sums(rows, n_ref[2 * step + k], acc_ref, sum_ref)
        back = dot(rows, wt_ref[1])
        for q in range(STRIPE):
            cut = slice(q * PH, (q + 1) * PH)
            out_ref[0, pl.ds(column + q, PH, stride=HALF)] = back[cut, :BR]
            out_ref[1, pl.ds(column + q, PH, stride=HALF)] = back[cut, BR:]

    @pl.when(step == 1)
    def _():
        for s in range(2):
            keep = pl.multiple_of(place * PAIR + s * WIN, 8)
            send = pl.multiple_of((1 - place) * PAIR + s * WIN, 8)
            for j in range(2):
                lanes = slice(j * BR, (j + 1) * BR)
                keep_ref[s, :, lanes] = out_ref[j, pl.ds(keep, WIN)].astype(BF16)
                send_ref[s, :, lanes] = out_ref[j, pl.ds(send, WIN)].astype(BF16)


def direction_grads(acc, sums, gain, bias, weight_t):
    moved = acc.T
    shift = sums[0:1]
    high = shift.astype(BF16)
    low = (shift - high.astype(F32)).astype(BF16)
    wide = dot(high, weight_t) + dot(low, weight_t)
    column = sums.T[:, 0:1]
    grad_qkv = moved * gain + column * bias
    grad_gain = jnp.sum(weight_t.astype(F32) * moved, 0, keepdims=True)
    return grad_qkv, grad_gain, wide


def rows_backward_kernel(image, start, count, last, others, *refs):
    (
        heights, info, x_ref, gm_ref, p_ref, q_ref, k_ref, v_ref, o_ref, rl_ref, wt_ref, taps_ref,
    ) = refs[:12]
    refs = refs[12:]
    if last:
        gain_ref, bias_ref, small2_ref = refs[:3]
        other_refs = refs[3 : 3 + 3 * sum(others)]
        refs = refs[3 + 3 * sum(others) :]
        gp_ref, kept_ref, sent_ref = refs[:3]
        acc_ref, sum_ref, lepe_ref, pack_ref, kb_ref, vb_ref, ds_ref = refs[3:]
    else:
        gp_ref, acc_ref, sum_ref, lepe_ref, kb_ref, vb_ref, ds_ref = refs
    step = pl.program_id(0)
    pair = start + step
    height, width = sides(image, heights, info)
    row_base = tensor_place(info) * HALF + pair * 2 * STRIPE

    @pl.when(step == 0)
    def _():
        set_indicator(vb_ref)
        acc_ref[...] = jnp.zeros_like(acc_ref)
        sum_ref[...] = jnp.zeros_like(sum_ref)
        lepe_ref[...] = jnp.zeros_like(lepe_ref)

    mask = twice(as_float(inside(split_index(PAIR, PW, BR), row_base, 0, height, width)))
    unit, _ = norm_parts(x_ref[0].astype(F32) * mask)
    refs = (p_ref, q_ref, k_ref, v_ref, o_ref, rl_ref, kb_ref, vb_ref, ds_ref)
    first_window = 2 * pair
    for k in range(2):
        base = row_base + k * STRIPE
        rows, tap_rows = window_backward(
            gm_ref[k].astype(F32), base, height, width, taps_ref[0, :9], first_window, k, refs
        )
        for index, item in enumerate(tap_rows):
            lepe_ref[index : index + 1] += item
        gp_ref[k] = rows
        backward_sums(rows, unit[k * WIN : (k + 1) * WIN].astype(BF16), acc_ref, sum_ref)
    if last:

        @pl.when(step == count - 1)
        def _():
            row_items = [acc_ref[...], sum_ref[...], lepe_ref[...]]
            column_items = [0.0, 0.0, 0.0]
            for at in range(sum(others)):
                kind = other_refs[3 * at : 3 * at + 3]
                if at < others[0]:
                    row_items = [old + ref[...] for old, ref in zip(row_items, kind)]
                else:
                    column_items = [old + ref[...] for old, ref in zip(column_items, kind)]
            gain, bias = gain_ref[...], bias_ref[...]
            grad_gain = grad_bias = 0.0
            half = BR // 2
            for direction, items in enumerate((row_items, column_items)):
                grad_qkv, gain_row, bias_row = direction_grads(
                    items[0], items[1], gain, bias, wt_ref[direction]
                )
                grad_gain = grad_gain + gain_row
                grad_bias = grad_bias + bias_row
                for s in range(2):
                    for item in range(3):
                        at = direction * 3 * half + item * half
                        take = item * BR + s * half
                        pack_ref[s, at : at + half] = grad_qkv[take : take + half]
            small2 = small2_ref[...]
            for s in range(2):
                cut = slice(s * half, (s + 1) * half)
                lepe = jnp.concatenate(
                    [row_items[2][:, cut], column_items[2][:, cut], jnp.zeros((16, BR), F32)], axis=1
                )
                head = jnp.concatenate(
                    [grad_gain, grad_bias, small2[:4], small2[4 + 2 * s : 6 + 2 * s]], axis=0
                )
                pack_ref[s, SMALL_AT : SMALL_AT + 8] = head
                pack_ref[s, SMALL_AT + 8 : SMALL_AT + 24] = lepe
                pack_ref[s, SMALL_AT + 24 :] = jnp.zeros((LAST_ROWS - SMALL_AT - 24, 2 * BR), F32)
            core = core_place(info)
            rows = LAST_ROWS // 2
            for s in range(2):
                mine = pl.multiple_of(core * rows, 8)
                theirs = pl.multiple_of((1 - core) * rows, 8)
                kept_ref[s] = pack_ref[s, pl.ds(mine, rows)].astype(BF16)
                sent_ref[s] = pack_ref[s, pl.ds(theirs, rows)].astype(BF16)


def input_kernel(image, start, first, *refs):
    heights, info, x_ref, gp_ref, gmid_ref, vk_ref, vr_ref, wt_ref, gain_ref = refs[:9]
    refs = refs[9:] if first else refs[10:]
    out_ref, mark_ref, whole, left, right = refs
    mark_ref[...] = jnp.zeros_like(mark_ref)
    pair = start + pl.program_id(0)
    place = tensor_place(info)
    height, width = sides(image, heights, info)
    row_base = place * HALF + pair * 2 * STRIPE
    mask = twice(as_float(inside(split_index(PAIR, PW, BR), row_base, 0, height, width)))
    unit, inverse = norm_parts(x_ref[0].astype(F32) * mask)
    first_half = place == 0
    own = vk_ref[0].astype(F32)
    other = vr_ref[0].astype(F32)
    left[...] = jnp.where(first_half, own, other)
    right[...] = jnp.where(first_half, other, own)
    merge_columns(left, right, whole)
    parts = [dot(gp_ref[k], wt_ref[0]) for k in range(2)]
    grad_normed = jnp.concatenate(parts, axis=0) + whole[...]
    back = norm_back(grad_normed, unit, inverse, gain_ref[...])
    out_ref[0] = (mask * (gmid_ref[0] + back)).astype(BF16)


def unpack_first_kernel(info, a_ref, ax_ref, b_ref, bx_ref, fc1_ref, fc2_ref, proj_ref):
    core, along = core_place(info) == 0, along_place(info) == 0
    quarters = []
    for c in range(2):
        for side in range(2):
            here = core if c == 0 else jnp.logical_not(core)
            near = along if side == 0 else jnp.logical_not(along)
            mine = jnp.where(near, a_ref[...].astype(F32), ax_ref[...].astype(F32))
            theirs = jnp.where(near, b_ref[...].astype(F32), bx_ref[...].astype(F32))
            quarters.append(jnp.where(here, mine, theirs))
    total = jnp.concatenate(quarters, axis=0)
    fc1_ref[:, :CHUNK] = total[:CHUNK]
    fc1_ref[:, CHUNK:] = total[CHUNK : 2 * CHUNK]
    fc2_ref[...] = total[2 * CHUNK : 4 * CHUNK]
    proj_ref[...] = total[4 * CHUNK :]


def unpack_last_kernel(
    info, c_ref, cx_ref, qkv_ref, lepe_ref, shift_ref, b1_ref,
    gain1_ref, bias1_ref, gain2_ref, bias2_ref, projb_ref, b2_ref,
):
    core = core_place(info) == 0
    mine, theirs = c_ref[...].astype(F32), cx_ref[...].astype(F32)
    last = jnp.concatenate([jnp.where(core, mine, theirs), jnp.where(core, theirs, mine)], axis=0)
    half = BR // 2
    for direction in range(2):
        for item in range(3):
            at = direction * 3 * half + item * half
            qkv_ref[item, direction] = last[at : at + half]
    small = last[SMALL_AT : SMALL_AT + 24]
    for row, ref in enumerate((gain1_ref, bias1_ref, gain2_ref, bias2_ref, projb_ref, b2_ref)):
        ref[...] = small[row : row + 1]
    b1_ref[...] = small[6:8]
    for tap in range(9):
        turned = 8 + 3 * (tap % 3) + tap // 3
        lepe_ref[tap, 0:1] = small[8 + tap : 9 + tap, :half]
        lepe_ref[tap, 1:2] = small[turned : turned + 1, half : 2 * half]
    shift_ref[0:1] = small[17:18, :half]
    shift_ref[1:2] = small[17:18, half : 2 * half]


def spec(shape, index=None):
    if index is None:
        return pl.BlockSpec(shape, lambda i: (0,) * len(shape))
    return pl.BlockSpec(shape, index)


def shaped(shape, dtype):
    return jax.ShapeDtypeStruct(shape, dtype)


SCALARS = pl.BlockSpec(memory_space=pltpu.SMEM)
RESIDENT = pl.BlockSpec(memory_space=pltpu.VMEM)


def call(
    kernel, name, grid, in_specs, out_specs, out_shape, scratch, micros, limit, aliases=None, marks=0
):
    known = len(in_specs)

    def body(*refs):
        kernel(*refs[:known], *refs[known + marks :])

    in_specs = list(in_specs) + [pl.BlockSpec(memory_space=pl.ANY)] * marks
    return pl.pallas_call(
        body,
        name=name,
        grid=(grid,),
        in_specs=in_specs,
        out_specs=out_specs,
        out_shape=out_shape,
        scratch_shapes=scratch,
        input_output_aliases=aliases or {},
        cost_estimate=pl.CostEstimate(
            flops=int(micros * FLOPS_PER_MICRO), bytes_accessed=0, transcendentals=0
        ),
        compiler_params=pltpu.CompilerParams(
            vmem_limit_bytes=limit * MIB, dimension_semantics=("arbitrary",)
        ),
    )


def kept_shapes(count):
    return [pltpu.VMEM((count, WIN, WIDE), BF16)] + [
        pltpu.VMEM((count, WIN, BR), BF16) for _ in range(4)
    ] + [pltpu.VMEM((count, WIN, BR), F32)]


def resident(arrays):
    return [pltpu.with_memory_space_constraint(item, pltpu.VMEM) for item in arrays]


def in_hbm(arrays):
    return [pltpu.with_memory_space_constraint(item, pltpu.HBM) for item in arrays]


def forward_scratch():
    return [
        pltpu.VMEM((2, WIDE, BR), BF16),
        pltpu.VMEM((2, WIDE, 2 * BR), BF16),
        pltpu.VMEM((2, WIN, BR), F32),
        pltpu.VMEM((2, WIN, BR), F32),
        pltpu.VMEM((WIN, WIDE), F32),
    ]


def backward_scratch():
    return [
        pltpu.VMEM((2, WIDE, BR), BF16),
        pltpu.VMEM((2, WIDE, 2 * BR), BF16),
        pltpu.VMEM((2, WIN, WIDE), BF16),
    ]


FLOPS_PER_MICRO = 1.15e9
ATTENTION_LIMIT = 15
MLP_LIMIT = 18


def pack_first(qkv, lepe, shift):
    width = qkv.shape[-1]
    return call(
        pack_kernel, "pack", 1, [spec(qkv.shape), spec(lepe.shape), spec(shift.shape)],
        [spec((2 * FIRST_HALF, width)), spec((FIRST_HALF, width))],
        [shaped((2 * FIRST_HALF, width), BF16), shaped((FIRST_HALF, width), BF16)], [], 1, 8,
    )(*in_hbm([qkv, lepe, shift]))


def pack_late(info, w1, w2, proj, vectors):
    width = w2.shape[1]
    rows = 4 * LATE
    return call(
        late_pack_kernel, "pack_late", 1,
        [SCALARS, spec(w1.shape), spec(w2.shape), spec(proj.shape), spec(vectors.shape)],
        [spec((rows, width)), spec((LATE, width))],
        [shaped((rows, width), BF16), shaped((LATE, width), BF16)], [], 1, 8,
    )(info, w1, w2, proj, vectors)


def split_quadrants(info, x_pairs):
    count, _, width = x_pairs.shape
    images = count // 2
    block = (1, WIN, width)

    def clamp(image):
        return lambda i: (jnp.clip(i - 2 * image, 0, 1), 0, 0)

    return call(
        partial(quadrant_kernel, images), "quadrants", count,
        [SCALARS, spec((1, PAIR, width), lambda i: (i, 0, 0))],
        [spec(block, lambda i: (i, 0, 0))] + [spec(block, clamp(image)) for image in range(images)],
        [shaped((count, WIN, width), BF16)] + [shaped((2, WIN, width), BF16)] * images,
        [pltpu.VMEM((PAIR, width), F32), pltpu.VMEM((WIN, width), F32), pltpu.VMEM((WIN, width), F32)],
        2, 16,
    )(info, x_pairs)


def rows_forward(image, heights, info, x_pairs, gain, bias, packs, known):
    count, _, width = x_pairs.shape
    pair = spec((1, PAIR, width), lambda i: (2 * image + i, 0, 0))
    in_specs = [SCALARS, SCALARS, pair, spec((1, width)), spec((1, width))]
    operands = [heights, info, x_pairs, gain, bias]
    out_shapes = kept_shapes(4) + [pltpu.VMEM((4, WIN, BR), BF16)]
    scratch = forward_scratch()
    if known is None:
        in_specs += [spec(item.shape) for item in packs]
        operands += list(packs)
        scratch = [pltpu.VMEM((2 * FIRST_HALF, width), BF16)] + scratch
        out_shapes += [
            pltpu.VMEM((2, width, 3 * BR), BF16), pltpu.VMEM((2, 3 * BR, width), BF16),
            pltpu.VMEM((2, 16, BR), F32),
        ]
    else:
        in_specs += [RESIDENT] * 2
        operands += resident(known)
    return call(
        partial(rows_forward_kernel, image, known is None), "rows_forward", 2, in_specs,
        [RESIDENT] * len(out_shapes), out_shapes, scratch,
        6.5, ATTENTION_LIMIT,
    )(*operands)


def columns_forward(image, heights, info, own, other, gain, bias, weight, taps):
    width = own.shape[2]
    fixed = spec((2, WIN, BR), lambda i: (0, 0, 0))
    return call(
        partial(columns_forward_kernel, image), "columns_forward", 2,
        [
            SCALARS, SCALARS, spec((2, WIN, width), lambda i: (image, 0, 0)), spec((2, WIN, width)),
            spec((1, width)), spec((1, width)), RESIDENT, RESIDENT,
        ],
        [RESIDENT] * 7 + [fixed, fixed],
        kept_shapes(4) + [pltpu.VMEM((4, WIN, width), BF16)] + [shaped((2, WIN, BR), BF16)] * 2,
        [pltpu.VMEM((2, 2 * PAIR, BR), F32), pltpu.VMEM((2 * PAIR, BR), F32)] + forward_scratch(),
        6.5, ATTENTION_LIMIT,
    )(heights, info, own, other, gain, bias, *resident([weight, taps]))


def mlp(heights, info, x_pairs, cot_pairs, mixed_rows, mixed_own, mixed_other, gain, bias, late):
    count, _, width = x_pairs.shape
    images = count // 2
    pair = spec((1, PAIR, width), lambda i: (i, 0, 0))
    part = spec((1, WIN, BR), lambda i: (i, 0, 0))
    row = spec((1, width))
    quarter = (2, 2, GRAD_ROWS // 4, width)
    return call(
        partial(mlp_kernel, images), "feed_forward", count,
        [SCALARS, SCALARS, pair, pair] + [RESIDENT] * (3 * images) + [row, row] + [RESIDENT] * 5,
        [
            pair, pair, spec((2, WIN, BR), lambda i: (i, 0, 0)), part, part, spec((8, width)),
            spec(quarter), spec(quarter),
        ],
        [
            shaped(x_pairs.shape, BF16), shaped(x_pairs.shape, F32), shaped((2 * count, WIN, BR), BF16),
            shaped((count, WIN, BR), BF16), shaped((count, WIN, BR), BF16), shaped((8, width), F32),
            shaped(quarter, BF16), shaped(quarter, BF16),
        ],
        [
            pltpu.VMEM((2, GRAD_ROWS, width), F32),
            pltpu.VMEM((2 * BR, width), BF16), pltpu.VMEM((8 * LATE, width), BF16),
            pltpu.VMEM((PAIR, BR), F32), pltpu.VMEM((WIN, BR), F32), pltpu.VMEM((WIN, BR), F32),
            pltpu.VMEM((PAIR, width), BF16), pltpu.VMEM((PAIR, width), BF16),
            pltpu.VMEM((width, PAIR), BF16), pltpu.VMEM((width, PAIR), BF16),
        ],
        24, MLP_LIMIT,
    )(
        heights, info, x_pairs, cot_pairs, *resident([*mixed_rows, *mixed_own, *mixed_other]), gain, bias,
        *resident(late),
    )


def columns_backward(image, heights, info, grad_own, grad_other, kept, unit, weight_t, taps):
    width = weight_t.shape[2]
    fixed = spec((2, WIN, width))
    grads = spec((2, WIN, BR), lambda i: (image, 0, 0))
    return call(
        partial(columns_backward_kernel, image), "columns_backward", 2,
        [SCALARS, SCALARS, grads, grads] + [RESIDENT] * 9,
        [spec((width, 3 * BR)), spec((8, 3 * BR)), spec((16, BR)), fixed, fixed],
        [shaped((width, 3 * BR), F32), shaped((8, 3 * BR), F32), shaped((16, BR), F32)]
        + [shaped((2, WIN, width), BF16)] * 2,
        [pltpu.VMEM((2 * PAIR, BR), F32), pltpu.VMEM((2, 2 * PAIR, BR), F32)] + backward_scratch(),
        9.7, ATTENTION_LIMIT,
    )(heights, info, grad_own, grad_other, *resident([*kept, unit, weight_t, taps]))


def rows_backward(image, start, count, heights, info, x_pairs, grad_mixed, kept, weight_t, taps, final):
    width = weight_t.shape[2]
    at = 2 * image + start
    pair = spec((1, PAIR, width), lambda i: (at + i, 0, 0))
    in_specs = [SCALARS, SCALARS, pair, spec((2, WIN, BR), lambda i: (at + i, 0, 0))] + [RESIDENT] * 8
    operands = [heights, info, x_pairs, grad_mixed, *resident([*kept, weight_t, taps])]
    sum_shapes = [(width, 3 * BR), (8, 3 * BR), (16, BR)]
    out_specs = [spec((2, WIN, 3 * BR), lambda i: (i, 0, 0))]
    out_shapes = [shaped((2 * count, WIN, 3 * BR), BF16)]
    scratch = backward_scratch()
    others = (0, 0)
    if final is None:
        out_specs += [spec(shape) for shape in sum_shapes]
        out_shapes += [shaped(shape, F32) for shape in sum_shapes]
    else:
        gain, bias, small2, row_items, column_items = final
        others = (len(row_items), len(column_items))
        in_specs += [spec((1, width)), spec((1, width)), spec((8, width))]
        operands += [gain, bias, small2]
        for item in [*row_items, *column_items]:
            in_specs += [spec(shape) for shape in sum_shapes]
            operands += list(item)
        half = (2, LAST_ROWS // 2, width)
        out_specs += [spec(half), spec(half)]
        out_shapes += [shaped(half, BF16), shaped(half, BF16)]
        scratch = (
            [pltpu.VMEM(shape, F32) for shape in sum_shapes]
            + [pltpu.VMEM((2, LAST_ROWS, width), F32)]
            + scratch
        )
    return call(
        partial(rows_backward_kernel, image, start, count, final is not None, others), "rows_backward",
        count, in_specs, out_specs, out_shapes, scratch, 4.8 * count, ATTENTION_LIMIT,
    )(*operands)


def input_rows(
    image, start, count, heights, info, x_pairs, rows, grad_mid, back_own, back_other, weight_t, gain,
    previous,
):
    width = weight_t.shape[2]
    pair = spec((1, PAIR, width), lambda i: (2 * image + start + i, 0, 0))
    part = spec((1, WIN, width), lambda i: (start + i, 0, 0))
    in_specs = [
        SCALARS, SCALARS, pair, spec((2, WIN, 3 * BR), lambda i: (start + i, 0, 0)), pair, part, part,
        RESIDENT, spec((1, width)),
    ]
    operands = [
        heights, info, x_pairs, rows, grad_mid, back_own, back_other, *resident([weight_t]), gain,
    ]
    aliases = {}
    if previous is not None:
        in_specs.append(pl.BlockSpec(memory_space=pl.ANY))
        operands.append(previous)
        aliases = {len(operands) - 1: 0}
    return call(
        partial(input_kernel, image, start, previous is None), "input_rows", count, in_specs,
        [pair, spec((8, 128))], [shaped(x_pairs.shape, BF16), shaped((8, 128), F32)],
        [pltpu.VMEM((PAIR, width), F32), pltpu.VMEM((WIN, width), F32), pltpu.VMEM((WIN, width), F32)],
        1.6 * count, 20, aliases,
    )(*operands)


def unpack_first(info, a, ax, b, bx, hidden, width):
    return call(
        unpack_first_kernel, "unpack_first", 1, [SCALARS] + [spec(a.shape)] * 4,
        [spec((width, hidden)), spec((hidden, width)), spec((BR, width))],
        [shaped((width, hidden), F32), shaped((hidden, width), F32), shaped((BR, width), F32)],
        [], 1, 16,
    )(info, a, ax, b, bx)


def unpack_last(info, c, cx, width):
    row = spec((1, width))
    return call(
        unpack_last_kernel, "unpack_last", 1, [SCALARS] + [spec(c.shape)] * 2,
        [
            spec((3, 2, BR // 2, width)), spec((9, 2, BR // 2)), spec((2, BR // 2)), spec((2, width)),
            row, row, row, row, row, row,
        ],
        [
            shaped((3, 2, BR // 2, width), F32), shaped((9, 2, BR // 2), F32), shaped((2, BR // 2), F32),
            shaped((2, width), F32),
        ] + [shaped((1, width), F32)] * 6,
        [], 1, 16,
    )(info, c, cx)


def after(value, *marks):
    return lax.optimization_barrier((value,) + marks)[0]


def swap_tensor(values):
    return lax.ppermute(values, "tensor", [(0, 1), (1, 0)])


def swap_dp(values, size, mask):
    return lax.ppermute(values, "dp", [(i, i ^ mask) for i in range(size)])


def swap_both(values, size, mask):
    pairs = [(2 * i + t, 2 * (i ^ mask) + 1 - t) for i in range(size) for t in range(2)]
    return lax.ppermute(values, ("dp", "tensor"), pairs)


def add_kernel(count, *refs):
    refs, outs = refs[:count], refs[count:]
    items = [ref[...].astype(F32) for ref in refs]
    while len(items) > 1:
        items = [items[i] + items[i + 1] for i in range(0, len(items), 2)]
    whole = items[0].astype(BF16)
    whole = whole.reshape((len(outs),) + outs[0].shape)
    for at, out in enumerate(outs):
        out[...] = whole[at]


def added(*items, parts=1, marks=()):
    shape = items[0].shape
    last = shape[-2:]
    outs = call(
        partial(add_kernel, len(items)), "add", 1, [spec(shape)] * len(items), [spec(last)] * parts,
        [shaped(last, BF16)] * parts, [], 0.5, 8, marks=len(marks),
    )(*items, *marks)
    return outs[0] if parts == 1 else outs


def partner_groups(size):
    bits = list(range(1, size.bit_length() - 1))
    groups = []
    while bits:
        pair, bits = bits[:2], bits[2:]
        low = 1 << pair[0]
        groups.append([low] if len(pair) == 1 else [low, 1 << pair[1], low | (1 << pair[1])])
    return groups


def per_device(
    size, block_input, heights, widths, norm1_gain, norm1_bias, qkv_weight, lepe_weight, lepe_bias,
    proj_weight, proj_bias, norm2_gain, norm2_bias, fc1_weight, fc1_bias, fc2_weight, fc2_bias,
    cotangent,
):
    images, local_cells, width = block_input.shape
    hidden = fc1_weight.shape[1]
    x_pairs = block_input.reshape(2 * images, PAIR, width)
    cot_pairs = cotangent.reshape(2 * images, PAIR, width)
    gain1, bias1 = norm1_gain[None], norm1_bias[None]
    pairs = range(images)
    index = lax.axis_index("dp")
    places = jnp.stack([lax.axis_index("tensor"), index % 2, index // 2 % 2]).astype(jnp.int32)
    info = jnp.concatenate([widths, places])

    own, own_half = pack_first(
        qkv_weight.transpose(1, 2, 3, 0), lepe_weight.transpose(1, 0, 2), lepe_bias
    )
    near = swap_tensor(own_half)
    far = swap_dp(near, size, 1)
    quad_own, *quad_send = split_quadrants(info, after(x_pairs, own))
    vectors = jnp.concatenate([fc1_bias, proj_bias, fc2_bias]).reshape(-1, width)
    late_own, late_send = pack_late(info, *after((fc1_weight, fc2_weight, proj_weight, vectors), quad_own))
    quad_other = [swap_tensor(quad_send[0])]

    late_near = swap_tensor(late_send)

    def forward_rows(image, mark, known):
        return rows_forward(
            image, after(heights, mark), info, x_pairs, gain1, bias1, (own, near, far), known
        )

    *kept, mixed, weight, weight_t, taps = forward_rows(0, late_own, None)
    row_kept, mixed_rows = [kept], [mixed]
    quad_other += [swap_tensor(after(item, taps)) for item in quad_send[1:]]
    columns = []
    for image in pairs:
        *kept, unit, keep, send = columns_forward(
            image, heights, info, quad_own, quad_other[image], gain1, bias1, weight, taps
        )
        columns.append((kept, unit, keep, swap_tensor(send)))
        if image == 0:
            ready = after(late_near, keep)
            late_parts = [ready] + [swap_dp(ready, size, mask) for mask in (2, 1, 3)]
    for image in range(1, images):
        *kept, mixed = forward_rows(image, columns[-1][2], (weight, taps))
        row_kept.append(kept)
        mixed_rows.append(mixed)
    output, grad_mid, grad_rows, grad_keep, grad_send, small2, kept1, sent1 = mlp(
        heights, info, x_pairs, cot_pairs, mixed_rows, [item[2] for item in columns],
        [item[3] for item in columns], norm2_gain[None], norm2_bias[None], (late_own, *late_parts),
    )
    grad_other = swap_tensor(grad_send)

    arrived = swap_dp(sent1, size, 1)
    bits = size.bit_length() - 1
    row_pairs, row_sums = [], []

    def backward_rows(image, start, count, mark, final=None):
        rows, *rest = rows_backward(
            image, start, count, after(heights, mark), info, x_pairs, grad_rows, row_kept[image],
            weight_t, taps, final,
        )
        row_pairs.append(rows)
        return rest

    for image in range(images - 1):
        row_sums.append(backward_rows(image, 0, 2, small2))
    mark = row_sums[-1][2] if row_sums else small2
    first, toward_x, toward_y, toward_xy = added(kept1, after(arrived, mark), parts=4)
    crossed = [swap_dp(toward_x, size, 2), swap_tensor(toward_y), swap_both(toward_xy, size, 2)]
    mark = first
    column_back = []
    for image in pairs:
        kept, unit, _, _ = columns[image]
        *column_sums, back_keep, back_send = columns_backward(
            image, after(heights, mark), info, grad_keep, grad_other, kept, unit, weight_t, taps
        )
        column_back.append((column_sums, back_keep, swap_tensor(back_send)))
        mark = column_sums[2]
        if image == 0:
            first = added(first, *[after(item, mark) for item in crossed])
        else:
            first = added(first, after(arrived, mark))
        bit = 2 + image
        arrived = swap_dp(first, size, 1 << bit) if bit < bits else jnp.zeros_like(first)
        mark = first
    final = (gain1, bias1, small2, row_sums, [item[0] for item in column_back])
    kept2, sent2 = backward_rows(images - 1, 0, 2, mark, final)

    input_grad = None

    def meanwhile(image, start, count, mark):
        nonlocal input_grad
        _, back_keep, back_other = column_back[image]
        input_grad, mark = input_rows(
            image, start, count, after(heights, mark), info, x_pairs, row_pairs[image], grad_mid,
            back_keep, back_other, weight_t, gain1, input_grad,
        )
        return mark

    first = added(first, arrived, marks=[kept2])
    core_part = swap_dp(after(sent2, first), size, 1)
    last, toward_y = added(kept2, core_part, parts=2, marks=[item[2] for item in column_back])
    for bit in range(2 + images, bits):
        first = added(first, swap_dp(first, size, 1 << bit))
    first_x = swap_dp(first, size, 2)
    across = swap_tensor(toward_y)
    for image in range(images - 1):
        mark = meanwhile(image, 0, 2, last)
    last = added(last, across, marks=[mark])
    for at, group in enumerate(partner_groups(size)):
        arrived = [swap_dp(last, size, mask) for mask in group]
        marks = []
        if at == 0:
            marks = [meanwhile(images - 1, 0, 1, last), first_x]
        if at == 1:
            first_core = [swap_dp(after(item, last), size, 1) for item in (first, first_x)]
            grad_fc1, grad_fc2, grad_proj = unpack_first(
                after(info, last), first, first_x, first_core[0], first_core[1], hidden, width
            )
            marks = [meanwhile(images - 1, 1, 1, last), grad_proj]
        last = added(last, *arrived, marks=marks)
    last_other = swap_dp(last, size, 1)
    (
        grad_qkv, grad_lepe, grad_shift, grad_b1,
        grad_gain1, grad_bias1, grad_gain2, grad_bias2, grad_projb, grad_b2,
    ) = unpack_last(info, last, last_other, width)
    return (
        output.reshape(block_input.shape), input_grad.reshape(block_input.shape),
        grad_gain1[0], grad_bias1[0], grad_qkv.transpose(3, 0, 1, 2), grad_lepe.transpose(1, 0, 2),
        grad_shift, grad_proj.reshape(2, BR // 2, width), grad_projb[0], grad_gain2[0], grad_bias2[0],
        grad_fc1, grad_b1.reshape(-1), grad_fc2, grad_b2[0],
    )


def solution(mesh):
    placed = (
        P("dp", "tensor", None),
        P("dp"),
        P("dp"),
        P(),
        P(),
        P(None, None, None, "tensor"),
        P(None, None, "tensor"),
        P(None, "tensor"),
        P(None, "tensor", None),
        P(),
        P(),
        P(),
        P(None, "tensor"),
        P("tensor"),
        P("tensor", None),
        P(),
        P("dp", "tensor", None),
    )
    return jax.shard_map(
        partial(per_device, mesh.shape["dp"]),
        mesh=mesh,
        in_specs=placed,
        out_specs=(
            P("dp", "tensor", None),
            P("dp", "tensor", None),
            P(),
            P(),
            P(None, None, None, "tensor"),
            P(None, None, "tensor"),
            P(None, "tensor"),
            P(None, "tensor", None),
            P(),
            P(),
            P(),
            P(None, "tensor"),
            P("tensor"),
            P("tensor", None),
            P(),
        ),
        check_vma=False,
    )
```

```python
from functools import partial

import jax
import jax.numpy as jnp
from jax import lax
from jax.experimental import pallas as pl
from jax.experimental.pallas import tpu as pltpu
from jax.sharding import PartitionSpec as P

HEAD_DIM = 32
STRIPE = 7
PH = 56
PW = 56
HEADS = 4
BR = HEADS * HEAD_DIM
WIN = STRIPE * PW
WIDE = HEADS * WIN
MAIN = WIN // 128 * 128
REST = WIN - MAIN
GAP = 64
PAD_ROWS = STRIPE * GAP + 16
HALF = 28
PAIR = 2 * WIN
CHUNK = 256
CHUNKS = [(lo, min(lo + CHUNK, WIDE)) for lo in range(0, WIDE, CHUNK)]

MASKED_WEIGHT = 9.357622968840175e-14
EPSILON = 1e-05
LOG2E = 1.4426950408889634
LN2 = 0.6931471805599453
ROOT_HALF = 0.7071067811865476
DENSITY = 0.3989422804014327
DEN_LOW = 2.0**-60
DEN_HIGH = 2.0**100

F32 = jnp.float32
BF16 = jnp.bfloat16
MIB = 2**20
GRAD_ROWS = 1152
LAST_ROWS = 416
SMALL_AT = 3 * BR
FIRST_HALF = 208
LATE = 304


def dot(a, b):
    return jnp.dot(a, b, preferred_element_type=F32)


def dot_nt(a, b):
    return lax.dot_general(a, b, (((1,), (1,)), ((), ())), preferred_element_type=F32)


def dot_tn(a, b):
    return lax.dot_general(a, b, (((0,), (0,)), ((), ())), preferred_element_type=F32)


def split_index(count, width, lanes, axis=0):
    shape = (count, lanes) if axis == 0 else (lanes, count)
    index = lax.broadcasted_iota(jnp.int32, shape, axis)
    step = -(-65536 // width)
    major = lax.shift_right_logical(index * step, 16)
    return major, index - major * width


def inside(parts, base_major, base_minor, lim_major, lim_minor):
    major, minor = parts
    return (major < lim_major - base_major) & (minor < lim_minor - base_minor)


def as_float(flag):
    return jnp.where(flag, 1.0, 0.0).astype(F32)


def twice(values):
    return jnp.concatenate([values, values], axis=1)


def head_lane(head):
    lane = lax.broadcasted_iota(jnp.int32, (1, BR), 1)
    return as_float((lane >= head * HEAD_DIM) & (lane < (head + 1) * HEAD_DIM))


def head_blocks(values):
    lanes = [head_lane(head) for head in range(HEADS)]
    top = [values[:MAIN] * lane for lane in lanes]
    rest = [values[MAIN:] * lane for lane in lanes]
    return jnp.concatenate(top + rest, axis=0)


def from_wide(values):
    rows = []
    for head in range(HEADS):
        own = values[head * HEAD_DIM : (head + 1) * HEAD_DIM]
        rest = HEADS * MAIN + head * REST
        rows.append(
            jnp.concatenate(
                [own[:, head * MAIN : (head + 1) * MAIN], own[:, rest : rest + REST]], axis=1
            )
        )
    return jnp.concatenate(rows, axis=0)


def norm_parts(values):
    centred = values - jnp.mean(values, -1, keepdims=True)
    inverse = lax.rsqrt(jnp.mean(centred * centred, -1, keepdims=True) + EPSILON)
    return centred * inverse, inverse


def norm_back(grad_rows, unit_rows, inverse, gain):
    scaled = grad_rows * gain
    return inverse * (
        scaled
        - jnp.mean(scaled, -1, keepdims=True)
        - unit_rows * jnp.mean(scaled * unit_rows, -1, keepdims=True)
    )


def spread(pad_ref, values):
    for row in range(STRIPE):
        pad_ref[8 + GAP * row : 8 + GAP * row + PW] = values[row * PW : (row + 1) * PW]


def neighbours(pad_ref):
    return [
        [pad_ref[8 + GAP * row + shift : 8 + GAP * row + shift + PW] for shift in (-1, 0, 1)]
        for row in range(STRIPE)
    ]


def filtered(rows, taps, flip):
    order = [8 - tap if flip else tap for tap in range(9)]
    taps = [taps[tap : tap + 1] for tap in order]
    out = []
    for row in range(STRIPE):
        total = None
        for a in range(3):
            if 0 <= row + a - 1 < STRIPE:
                for e in range(3):
                    term = taps[3 * a + e] * rows[row + a - 1][e]
                    total = term if total is None else total + term
        out.append(total)
    return jnp.concatenate(out, axis=0)


def tap_sums(grad_rows, value_rows):
    sums = []
    for a in range(3):
        for e in range(3):
            total = None
            for row in range(STRIPE):
                if 0 <= row + a - 1 < STRIPE:
                    term = grad_rows[row][1] * value_rows[row + a - 1][e]
                    total = term if total is None else total + term
            sums.append(jnp.sum(total, 0, keepdims=True))
    total = grad_rows[0][1]
    for row in range(1, STRIPE):
        total = total + grad_rows[row][1]
    sums.append(jnp.sum(total, 0, keepdims=True))
    return sums


def window_valid(window_base, lim_major, lim_minor):
    return inside(split_index(WIN, PW, BR), window_base, 0, lim_major, lim_minor)


def window_scores(projected, valid, first, k, refs):
    p_ref, q_ref, k_ref, v_ref, o_ref, rl_ref, kb_ref, vb_ref, lepe_ref, mixed_ref, pad_ref = refs
    queries = (projected[:, :BR] * (HEAD_DIM**-0.5 * LOG2E)).astype(BF16)
    key_rows = projected[:, BR : 2 * BR]
    values = projected[:, 2 * BR :].astype(BF16).astype(F32)
    valid_float = as_float(valid)
    weight = jnp.where(valid, 1.0, MASKED_WEIGHT)
    q_ref[first + k] = queries
    k_ref[first + k] = (key_rows * valid_float).astype(BF16)
    v_ref[first + k] = values.astype(BF16)
    kb_ref[k] = head_blocks(key_rows * valid_float).astype(BF16)
    vb_ref[k, :, :BR] = head_blocks(values * weight).astype(BF16)
    vb_ref[k, :, BR:] = head_blocks(weight).astype(BF16)
    for lo, hi in CHUNKS:
        p_ref[first + k, :, lo:hi] = jnp.exp2(dot_nt(queries, kb_ref[k, lo:hi])).astype(BF16)
    return values


def window_mixed(values, taps, shift, first, k, refs):
    p_ref, q_ref, k_ref, v_ref, o_ref, rl_ref, kb_ref, vb_ref, lepe_ref, mixed_ref, pad_ref = refs
    sums = dot(p_ref[first + k], vb_ref[k])
    totals = sums[:, BR:]
    inverse = 1.0 / totals
    attended = sums[:, :BR] * inverse
    o_ref[first + k] = attended.astype(BF16)
    rl_ref[first + k] = inverse
    spread(pad_ref.at[k], values)
    lepe = filtered(neighbours(pad_ref.at[k]), taps, False) + shift
    lepe_ref[k] = lepe
    mixed_ref[k] = attended + lepe
    safe = (totals > DEN_LOW) & (totals < DEN_HIGH)
    return jnp.max(jnp.where(safe, 0.0, 1.0))


def window_forward_safe(first, k, refs, s_ref):
    p_ref, q_ref, k_ref, v_ref, o_ref, rl_ref, kb_ref, vb_ref, lepe_ref, mixed_ref, _ = refs
    s_ref[...] = dot_nt(q_ref[first + k], kb_ref[k])
    for head in range(HEADS):
        cut = slice(head * MAIN, (head + 1) * MAIN)
        rest = HEADS * MAIN + head * REST
        left = s_ref[:, cut]
        right = s_ref[:, rest : rest + REST]
        peak = jnp.maximum(jnp.max(left, -1, keepdims=True), jnp.max(right, -1, keepdims=True))
        s_ref[:, cut] = left - peak
        s_ref[:, rest : rest + REST] = right - peak
    for lo, hi in CHUNKS:
        p_ref[first + k, :, lo:hi] = jnp.exp2(s_ref[:, lo:hi]).astype(BF16)
    sums = dot(p_ref[first + k], vb_ref[k])
    inverse = 1.0 / sums[:, BR:]
    attended = sums[:, :BR] * inverse
    o_ref[first + k] = attended.astype(BF16)
    rl_ref[first + k] = inverse
    mixed_ref[k] = attended + lepe_ref[k]


def window_scores_back(grads, first, k, refs):
    p_ref, q_ref, k_ref, v_ref, o_ref, rl_ref, kb_ref, vb_ref, ds_ref, pad_ref = refs
    lane = lax.broadcasted_iota(jnp.int32, (WIN, BR), 1)
    scaled = (grads * rl_ref[first + k]).astype(BF16)
    product = scaled.astype(F32) * o_ref[first + k].astype(F32)
    high = product.astype(BF16)
    low = (product - high.astype(F32)).astype(BF16)
    row = lax.broadcasted_iota(jnp.int32, (2 * BR, BR), 0)
    col = lax.broadcasted_iota(jnp.int32, (2 * BR, BR), 1)
    head_of = lax.shift_right_logical(row & (BR - 1), 5)
    picks = as_float((col < 2 * HEADS) & (head_of == (col & (HEADS - 1)))).astype(BF16)
    inner = dot(jnp.concatenate([high, low], axis=1), picks)
    inner_high = inner.astype(BF16).astype(F32)
    extra = jnp.where(lane < HEADS, inner_high, inner - inner_high).astype(BF16)
    left = jnp.concatenate([scaled, extra], axis=1)
    values = v_ref[first + k].astype(F32)
    vb_ref[k, :, :BR] = head_blocks(values).astype(BF16)
    kb_ref[k] = head_blocks(k_ref[first + k].astype(F32)).astype(BF16)
    for lo, hi in CHUNKS:
        grad_probs = dot_nt(left, vb_ref[k, lo:hi])
        ds_ref[k, :, lo:hi] = grad_probs.astype(BF16) * p_ref[first + k, :, lo:hi]
    scaled_t = scaled.astype(F32).T.astype(BF16)
    return dot(scaled_t, p_ref[first + k])


def window_products_back(scaled, first, k, refs):
    p_ref, q_ref, k_ref, v_ref, o_ref, rl_ref, kb_ref, vb_ref, ds_ref, pad_ref = refs
    grad_query = dot(ds_ref[k], kb_ref[k]) * (HEAD_DIM**-0.5)
    query_t = q_ref[first + k].astype(F32).T.astype(BF16)
    return grad_query, dot(query_t, ds_ref[k]), scaled


def window_rows_back(grads, products, base, lim_major, lim_minor, taps, first, k, refs):
    v_ref, pad_ref = refs[3], refs[9]
    grad_query, wide_key, wide_value = products
    values = v_ref[first + k].astype(F32)
    valid_t = inside(split_index(WIN, PW, BR, 1), base, 0, lim_major, lim_minor)
    weight_t = jnp.where(valid_t, 1.0, MASKED_WEIGHT)
    grad_key = (from_wide(wide_key) * jnp.where(valid_t, LN2, 0.0)).T
    grad_value = (from_wide(wide_value) * weight_t).T
    spread(pad_ref.at[2 * k], grads)
    spread(pad_ref.at[2 * k + 1], values)
    grad_rows, value_rows = neighbours(pad_ref.at[2 * k]), neighbours(pad_ref.at[2 * k + 1])
    back, tap_rows = filtered(grad_rows, taps, True), tap_sums(grad_rows, value_rows)
    out = jnp.concatenate([grad_query, grad_key, grad_value + back], axis=1)
    return out.astype(BF16), tap_rows


def window_pair_back(grads, first, refs):
    scaled = [window_scores_back(grads[k], first, k, refs) for k in range(2)]
    return [window_products_back(scaled[k], first, k, refs) for k in range(2)]


def set_indicator(vb_ref):
    row = lax.broadcasted_iota(jnp.int32, (WIDE, BR), 0)
    col = lax.broadcasted_iota(jnp.int32, (WIDE, BR), 1)
    head = jnp.zeros((WIDE, BR), jnp.int32)
    for cut in range(1, HEADS):
        head = head + jnp.where(row >= cut * MAIN, 1, 0)
    tail = lax.shift_right_logical(row - HEADS * MAIN, 3)
    head = jnp.where(row >= HEADS * MAIN, tail, head)
    hit = (col < 2 * HEADS) & ((col & (HEADS - 1)) == head)
    for k in range(2):
        vb_ref[k, :, BR:] = jnp.where(hit, -1.0, 0.0).astype(BF16)


def split_columns(source, left, right):
    for row in range(STRIPE * 2):
        left[row * HALF : (row + 1) * HALF] = source[row * PW : row * PW + HALF]
        right[row * HALF : (row + 1) * HALF] = source[row * PW + HALF : (row + 1) * PW]


def merge_columns(left, right, target):
    for row in range(STRIPE * 2):
        target[row * PW : row * PW + HALF] = left[row * HALF : (row + 1) * HALF]
        target[row * PW + HALF : (row + 1) * PW] = right[row * HALF : (row + 1) * HALF]


def sides(image, heights, info):
    return heights[image], info[image]


def tensor_place(info):
    return info[info.shape[0] - 3]


def core_place(info):
    return info[info.shape[0] - 2]


def along_place(info):
    return info[info.shape[0] - 1]


def pack_kernel(qkv_ref, lepe_ref, shift_ref, out_ref, send_ref):
    for item in range(3):
        for direction in range(2):
            row = (2 * item + direction) * BR // 2
            out_ref[row : row + BR // 2] = qkv_ref[item, direction]
    rows = [
        jnp.concatenate([lepe_ref[tap, 0:1], lepe_ref[tap, 1:2]], axis=1).astype(F32)
        for tap in range(9)
    ]
    rows.append(jnp.concatenate([shift_ref[0:1], shift_ref[1:2]], axis=1).astype(F32))
    rows.append(jnp.zeros((2 * FIRST_HALF - SMALL_AT - 10, BR), F32))
    small = jnp.concatenate(rows, axis=0)
    out_ref[SMALL_AT:] = jnp.concatenate([small, jnp.zeros_like(small)], axis=1).astype(BF16)
    core = lax.axis_index("dp") % 2
    send_ref[...] = out_ref[pl.ds(pl.multiple_of(core * FIRST_HALF, 16), FIRST_HALF)]


def late_pack_kernel(info, w1_ref, w2_ref, proj_ref, b1_ref, pb_ref, b2_ref, out_ref, send_ref):
    for j in range(2):
        out_ref[j * CHUNK : (j + 1) * CHUNK] = w1_ref[:, j * CHUNK : (j + 1) * CHUNK]
    out_ref[2 * CHUNK : 4 * CHUNK] = w2_ref[...]
    for b in range(2):
        at = 4 * CHUNK + b * BR // 2
        out_ref[at : at + BR // 2] = proj_ref[b]
    first = b1_ref[...].astype(F32).reshape(1, 2 * CHUNK)
    vectors = [first[:, :CHUNK], first[:, CHUNK:]]
    vectors += [ref[...].astype(F32).reshape(1, 2 * BR) for ref in (pb_ref, b2_ref)]
    tail = jnp.concatenate(vectors + [jnp.zeros((4 * LATE - GRAD_ROWS - 4, 2 * BR), F32)], axis=0)
    out_ref[GRAD_ROWS:] = tail.astype(BF16)
    part = 2 * core_place(info) + along_place(info)
    send_ref[...] = out_ref[pl.ds(pl.multiple_of(part * LATE, 16), LATE)]


def quadrant_kernel(images, info, x_ref, own_ref, *rest):
    sends, (whole, left, right) = rest[:images], rest[images:]
    step = pl.program_id(0)
    whole[...] = x_ref[0].astype(F32)
    split_columns(whole, left, right)
    first = tensor_place(info) == 0
    own_ref[0] = jnp.where(first, left[...], right[...]).astype(BF16)
    other = jnp.where(first, right[...], left[...]).astype(BF16)
    for image in range(images):

        @pl.when(step // 2 == image)
        def _():
            sends[image][0] = other


def rows_forward_kernel(image, first, *refs):
    heights, info, x_ref, gain_ref, bias_ref = refs[:5]
    if first:
        own_ref, near_ref, far_ref, p_ref, q_ref, k_ref, v_ref, o_ref, rl_ref, m_ref, w_ref, wt_ref, taps_ref = refs[5:18]
        other_ref = refs[-7]
    else:
        w_ref, taps_ref, p_ref, q_ref, k_ref, v_ref, o_ref, rl_ref, m_ref = refs[5:14]
    kb_ref, vb_ref, lepe_ref, mixed_ref, s_ref, pad_ref = refs[-6:]
    step = pl.program_id(0)
    height, width = sides(image, heights, info)
    row_base = tensor_place(info) * HALF + step * 2 * STRIPE

    def unpack_weights():
        core = core_place(info)
        for part, piece in ((core, near_ref), (1 - core, far_ref)):
            other_ref[pl.ds(pl.multiple_of(part * FIRST_HALF, 16), FIRST_HALF)] = piece[...]
        for direction in range(2):
            for item in range(3):
                row = (2 * item + direction) * BR // 2
                at = item * BR
                wt_ref[direction, at : at + BR // 2] = own_ref[row : row + BR // 2]
                wt_ref[direction, at + BR // 2 : at + BR] = other_ref[row : row + BR // 2]
            w_ref[direction] = wt_ref[direction].astype(F32).T.astype(BF16)
        own = own_ref[SMALL_AT : SMALL_AT + 16].astype(F32)
        other = other_ref[SMALL_AT : SMALL_AT + 16].astype(F32)
        half = BR // 2
        for direction in range(2):
            cut = slice(direction * half, (direction + 1) * half)
            both = jnp.concatenate([own[:, cut], other[:, cut]], axis=1)
            if direction == 1:
                order = [3 * (tap % 3) + tap // 3 for tap in range(9)] + list(range(9, 16))
                both = jnp.concatenate([both[tap : tap + 1] for tap in order], axis=0)
            taps_ref[direction] = both

    if first:
        pl.when(step == 0)(unpack_weights)

    @pl.when(step == 0)
    def _():
        pad_ref[...] = jnp.zeros_like(pad_ref)

    mask = as_float(inside(split_index(PAIR, PW, BR), row_base, 0, height, width))
    unit, _ = norm_parts(x_ref[0].astype(F32) * twice(mask))
    normed = (unit * gain_ref[...] + bias_ref[...]).astype(BF16)
    projected = dot(normed, w_ref[0])
    refs = (
        p_ref, q_ref, k_ref, v_ref, o_ref, rl_ref, kb_ref, vb_ref, lepe_ref, mixed_ref, pad_ref
    )
    bad = jnp.float32(0)
    values = []
    for k in range(2):
        valid = window_valid(row_base + k * STRIPE, height, width)
        rows = projected[k * WIN : (k + 1) * WIN]
        values.append(window_scores(rows, valid, 2 * step, k, refs))
    for k in range(2):
        bad = jnp.maximum(
            bad, window_mixed(values[k], taps_ref[0, :9], taps_ref[0, 9:10], 2 * step, k, refs)
        )

    @pl.when(bad > 0.0)
    def _():
        def one(k, carry):
            window_forward_safe(2 * step, k, refs, s_ref)
            return carry

        lax.fori_loop(0, 2, one, 0)

    for k in range(2):
        m_ref[2 * step + k] = mixed_ref[k].astype(BF16)


def columns_forward_kernel(
    image, heights, info, own_ref, other_ref, gain_ref, bias_ref, w_ref, taps_ref,
    p_ref, q_ref, k_ref, v_ref, o_ref, rl_ref, n_ref, keep_ref, send_ref,
    unit_ref, out_ref, kb_ref, vb_ref, lepe_ref, mixed_ref, s_ref, pad_ref,
):
    step = pl.program_id(0)
    place = tensor_place(info)
    height, width = sides(image, heights, info)
    column_base = place * HALF

    @pl.when(step == 0)
    def _():
        pad_ref[...] = jnp.zeros_like(pad_ref)
        for source, side in ((own_ref, place), (other_ref, 1 - place)):
            for s in range(2):
                flag = inside(
                    split_index(WIN, HALF, BR), side * HALF + s * 2 * STRIPE, column_base,
                    height, width,
                )
                unit, _ = norm_parts(source[s].astype(F32) * twice(as_float(flag)))
                start = pl.multiple_of(side * PAIR + s * WIN, 8)
                unit_ref[0, pl.ds(start, WIN)] = unit[:, :BR]
                unit_ref[1, pl.ds(start, WIN)] = unit[:, BR:]

    refs = (
        p_ref, q_ref, k_ref, v_ref, o_ref, rl_ref, kb_ref, vb_ref, lepe_ref, mixed_ref, pad_ref
    )
    bad = jnp.float32(0)
    values = []
    for k in range(2):
        column = (2 * step + k) * STRIPE
        halves = [
            jnp.concatenate(
                [unit_ref[j, pl.ds(column + q, PH, stride=HALF)] for q in range(STRIPE)], axis=0
            )
            for j in range(2)
        ]
        unit = jnp.concatenate(halves, axis=1)
        n_ref[2 * step + k] = unit.astype(BF16)
        normed = (unit * gain_ref[...] + bias_ref[...]).astype(BF16)
        valid = window_valid(column_base + column, width, height)
        values.append(window_scores(dot(normed, w_ref[1]), valid, 2 * step, k, refs))
    for k in range(2):
        bad = jnp.maximum(
            bad, window_mixed(values[k], taps_ref[1, :9], taps_ref[1, 9:10], 2 * step, k, refs)
        )

    @pl.when(bad > 0.0)
    def _():
        def one(k, carry):
            window_forward_safe(2 * step, k, refs, s_ref)
            return carry

        lax.fori_loop(0, 2, one, 0)

    for k in range(2):
        column = (2 * step + k) * STRIPE
        mixed = mixed_ref[k]
        for q in range(STRIPE):
            out_ref[pl.ds(column + q, PH, stride=HALF)] = mixed[q * PH : (q + 1) * PH]

    @pl.when(step == 1)
    def _():
        for s in range(2):
            keep = pl.multiple_of(place * PAIR + s * WIN, 8)
            send = pl.multiple_of((1 - place) * PAIR + s * WIN, 8)
            keep_ref[s] = out_ref[pl.ds(keep, WIN)].astype(BF16)
            send_ref[s] = pltpu.roll(out_ref[pl.ds(send, WIN)], BR // 2, 1).astype(BF16)


def mlp_kernel(images, *refs):
    heights, info, x_ref, cot_ref = refs[:4]
    mh_refs, mo_refs, mr_refs = (refs[4 + i * images : 4 + (i + 1) * images] for i in range(3))
    refs = refs[4 + 3 * images :]
    gain_ref, bias_ref, late_own, *late_parts = refs[:7]
    out_ref, gmid_ref, gh_ref, gk_ref, gs_ref, small_ref, kept_ref, sent_ref = refs[7:15]
    acc_ref, pw_ref, late_ref, whole, left, right, normed_ref, grad_ref, normed_t_ref, grad_t_ref = refs[15:]
    step = pl.program_id(0)
    image, pair = step // 2, step % 2
    place = tensor_place(info)
    height, width = sides(image, heights, info)
    row_base = place * HALF + pair * 2 * STRIPE
    half = BR // 2

    def of_image(items, at):
        value = items[0][at].astype(F32)
        for index in range(1, images):
            value = jnp.where(image == index, items[index][at].astype(F32), value)
        return value

    @pl.when(step == 0)
    def _():
        far = 4 * LATE
        late_ref[:far] = late_own[...]
        core, along = core_place(info), along_place(info)
        for at, piece in enumerate(late_parts):
            part = 2 * (core if at < 2 else 1 - core) + (along if at % 2 == 0 else 1 - along)
            late_ref[pl.ds(pl.multiple_of(far + part * LATE, 16), LATE)] = piece[...]
        for b in range(2):
            at = 4 * CHUNK + b * half
            pw_ref[b * BR : b * BR + half] = late_ref[at : at + half]
            pw_ref[b * BR + half : (b + 1) * BR] = late_ref[far + at : far + at + half]
        acc_ref[...] = jnp.zeros_like(acc_ref)
        small_ref[...] = jnp.zeros_like(small_ref)

    vectors = late_own[GRAD_ROWS : GRAD_ROWS + 16].astype(F32)
    mask = twice(as_float(inside(split_index(PAIR, PW, BR), row_base, 0, height, width)))
    first_half = place == 0
    own = of_image(mo_refs, pair)
    other = of_image(mr_refs, pair)
    left[...] = jnp.where(first_half, own, other)
    right[...] = jnp.where(first_half, other, own)
    merge_columns(left, right, whole)
    rows_part = jnp.concatenate([of_image(mh_refs, 2 * pair + k) for k in range(2)], axis=0)
    mixed = jnp.concatenate([rows_part, whole[...]], axis=1).astype(BF16)
    x_in = x_ref[0].astype(F32) * mask
    x_mid = x_in + dot(mixed, pw_ref[...]) + vectors[2:3]
    unit, inverse = norm_parts(x_mid)
    normed = (unit * gain_ref[...] + bias_ref[...]).astype(BF16)
    grad_result = cot_ref[0].astype(F32) * mask
    grad_low = grad_result.astype(BF16)
    normed_t = normed.astype(F32).T.astype(BF16)
    grad_t = grad_result.T.astype(BF16)
    normed_ref[...] = normed
    grad_ref[...] = grad_low
    normed_t_ref[...] = normed_t
    grad_t_ref[...] = grad_t

    total = x_mid + vectors[3:4]
    grad_normed = jnp.zeros_like(x_mid)

    def chunk_start(j):
        base = (j // 2) * 4 * LATE
        at = base + (j % 2) * CHUNK
        w1, w2 = late_ref[at : at + CHUNK], late_ref[at + 2 * CHUNK : at + 3 * CHUNK]
        rows = late_ref[base + GRAD_ROWS : base + GRAD_ROWS + 16].astype(F32)
        pre = dot(normed_ref[...], w1) + rows[j % 2 : j % 2 + 1]
        return w1, w2, pre, dot_nt(grad_ref[...], w2)

    ahead = chunk_start(0)
    for j in range(4):
        w1, w2, pre, grad_hidden = ahead
        if j < 3:
            ahead = chunk_start(j + 1)
        holder, cut = j // 2, (j % 2) * CHUNK
        bell = jnp.exp2(pre * pre * (-0.5 * LOG2E))
        below = 0.5 + 0.5 * lax.erf(pre * ROOT_HALF)
        hidden = (pre * below).astype(BF16)
        slope = below + pre * bell * DENSITY
        grad_pre = (grad_hidden * slope).astype(BF16)
        total = total + dot(hidden, w2)
        grad_normed = grad_normed + dot_nt(grad_pre, w1)
        acc_ref[holder, cut : cut + CHUNK] += dot(normed_t_ref[...], grad_pre)
        acc_ref[holder, cut + 2 * CHUNK : cut + 3 * CHUNK] += dot(grad_t_ref[...], hidden)
        small_ref[4 + j : 5 + j] += jnp.sum(grad_pre.astype(F32), 0, keepdims=True)
    out_ref[0] = (mask * total).astype(BF16)
    grad_mid = grad_result + norm_back(grad_normed, unit, inverse, gain_ref[...])
    gmid_ref[0] = grad_mid
    small_ref[0:1] += jnp.sum(grad_normed * unit, 0, keepdims=True)
    small_ref[1:2] += jnp.sum(grad_normed, 0, keepdims=True)
    small_ref[2:3] += jnp.sum(grad_mid, 0, keepdims=True)
    small_ref[3:4] += jnp.sum(grad_result, 0, keepdims=True)
    mid_low = grad_mid.astype(BF16)
    grad_proj = dot_tn(mixed, mid_low)
    for b in range(2):
        at = 4 * CHUNK + b * half
        acc_ref[0, at : at + half] += grad_proj[b * BR : b * BR + half]
        acc_ref[1, at : at + half] += grad_proj[b * BR + half : (b + 1) * BR]
    grad_mixed = dot_nt(mid_low, pw_ref[...])
    gh_ref[0] = grad_mixed[:WIN, :BR].astype(BF16)
    gh_ref[1] = grad_mixed[WIN:, :BR].astype(BF16)
    whole[...] = grad_mixed[:, BR:]
    split_columns(whole, left, right)
    gk_ref[0] = jnp.where(first_half, left[...], right[...]).astype(BF16)
    gs_ref[0] = pltpu.roll(jnp.where(first_half, right[...], left[...]), half, 1).astype(BF16)

    @pl.when(step == 2 * images - 1)
    def _():
        for s in range(2):
            for j in range(2, 4):
                cut = slice(j * CHUNK, (j + 1) * CHUNK)
                acc_ref[s, cut] = acc_ref[s, cut].T
        core, along = core_place(info), along_place(info)
        rows = GRAD_ROWS // 4
        for s in range(2):
            for near in range(2):
                side = along if near == 0 else 1 - along
                mine = pl.multiple_of((2 * core + side) * rows, 8)
                theirs = pl.multiple_of((2 * (1 - core) + side) * rows, 8)
                kept_ref[s, near] = acc_ref[s, pl.ds(mine, rows)].astype(BF16)
                sent_ref[s, near] = acc_ref[s, pl.ds(theirs, rows)].astype(BF16)


def backward_sums(rows, unit, acc_ref, sum_ref):
    acc_ref[...] += dot_tn(unit, rows)
    sum_ref[0:1] += jnp.sum(rows.astype(F32), 0, keepdims=True)


def columns_backward_kernel(
    image, heights, info, gk_ref, gr_ref, p_ref, q_ref, k_ref, v_ref, o_ref, rl_ref, n_ref, wt_ref,
    taps_ref, acc_ref, sum_ref, lepe_ref, keep_ref, send_ref,
    grad_ref, out_ref, kb_ref, vb_ref, ds_ref, pad_ref,
):
    step = pl.program_id(0)
    place = tensor_place(info)
    height, width = sides(image, heights, info)

    @pl.when(step == 0)
    def _():
        set_indicator(vb_ref)
        pad_ref[...] = jnp.zeros_like(pad_ref)
        acc_ref[...] = jnp.zeros_like(acc_ref)
        sum_ref[...] = jnp.zeros_like(sum_ref)
        lepe_ref[...] = jnp.zeros_like(lepe_ref)
        for source, side in ((gk_ref, place), (gr_ref, 1 - place)):
            for s in range(2):
                start = pl.multiple_of(side * PAIR + s * WIN, 8)
                grad_ref[pl.ds(start, WIN)] = source[s].astype(F32)

    refs = (p_ref, q_ref, k_ref, v_ref, o_ref, rl_ref, kb_ref, vb_ref, ds_ref, pad_ref)
    first = 2 * step
    columns = [(first + k) * STRIPE for k in range(2)]
    grads = [
        jnp.concatenate([grad_ref[pl.ds(column + q, PH, stride=HALF)] for q in range(STRIPE)], axis=0)
        for column in columns
    ]
    products = window_pair_back(grads, first, refs)
    for k in range(2):
        column = columns[k]
        rows, tap_rows = window_rows_back(
            grads[k], products[k], place * HALF + column, width, height, taps_ref[1, :9], first, k, refs
        )
        for index, item in enumerate(tap_rows):
            lepe_ref[index : index + 1] += item
        backward_sums(rows, n_ref[2 * step + k], acc_ref, sum_ref)
        back = dot(rows, wt_ref[1])
        for q in range(STRIPE):
            cut = slice(q * PH, (q + 1) * PH)
            out_ref[0, pl.ds(column + q, PH, stride=HALF)] = back[cut, :BR]
            out_ref[1, pl.ds(column + q, PH, stride=HALF)] = back[cut, BR:]

    @pl.when(step == 1)
    def _():
        for s in range(2):
            keep = pl.multiple_of(place * PAIR + s * WIN, 8)
            send = pl.multiple_of((1 - place) * PAIR + s * WIN, 8)
            for j in range(2):
                lanes = slice(j * BR, (j + 1) * BR)
                keep_ref[s, :, lanes] = out_ref[j, pl.ds(keep, WIN)].astype(BF16)
                send_ref[s, :, lanes] = out_ref[j, pl.ds(send, WIN)].astype(BF16)


def direction_grads(acc, sums, gain, bias, weight_t):
    moved = acc.T
    shift = sums[0:1]
    high = shift.astype(BF16)
    low = (shift - high.astype(F32)).astype(BF16)
    wide = dot(high, weight_t) + dot(low, weight_t)
    column = sums.T[:, 0:1]
    grad_qkv = moved * gain + column * bias
    grad_gain = jnp.sum(weight_t.astype(F32) * moved, 0, keepdims=True)
    return grad_qkv, grad_gain, wide


def rows_backward_kernel(image, start, count, last, others, *refs):
    (
        heights, info, x_ref, gm_ref, p_ref, q_ref, k_ref, v_ref, o_ref, rl_ref, wt_ref, taps_ref,
    ) = refs[:12]
    refs = refs[12:]
    if last:
        gain_ref, bias_ref, small2_ref = refs[:3]
        other_refs = refs[3 : 3 + 3 * sum(others)]
        refs = refs[3 + 3 * sum(others) :]
        gp_ref, kept_ref, sent_ref = refs[:3]
        acc_ref, sum_ref, lepe_ref, pack_ref, kb_ref, vb_ref, ds_ref, pad_ref = refs[3:]
    else:
        gp_ref, acc_ref, sum_ref, lepe_ref, kb_ref, vb_ref, ds_ref, pad_ref = refs
    step = pl.program_id(0)
    pair = start + step
    height, width = sides(image, heights, info)
    row_base = tensor_place(info) * HALF + pair * 2 * STRIPE

    @pl.when(step == 0)
    def _():
        set_indicator(vb_ref)
        pad_ref[...] = jnp.zeros_like(pad_ref)
        acc_ref[...] = jnp.zeros_like(acc_ref)
        sum_ref[...] = jnp.zeros_like(sum_ref)
        lepe_ref[...] = jnp.zeros_like(lepe_ref)

    mask = twice(as_float(inside(split_index(PAIR, PW, BR), row_base, 0, height, width)))
    unit, _ = norm_parts(x_ref[0].astype(F32) * mask)
    refs = (p_ref, q_ref, k_ref, v_ref, o_ref, rl_ref, kb_ref, vb_ref, ds_ref, pad_ref)
    first_window = 2 * pair
    grads = [gm_ref[k].astype(F32) for k in range(2)]
    products = window_pair_back(grads, first_window, refs)
    for k in range(2):
        base = row_base + k * STRIPE
        rows, tap_rows = window_rows_back(
            grads[k], products[k], base, height, width, taps_ref[0, :9], first_window, k, refs
        )
        for index, item in enumerate(tap_rows):
            lepe_ref[index : index + 1] += item
        gp_ref[k] = rows
        backward_sums(rows, unit[k * WIN : (k + 1) * WIN].astype(BF16), acc_ref, sum_ref)
    if last:

        @pl.when(step == count - 1)
        def _():
            row_items = [acc_ref[...], sum_ref[...], lepe_ref[...]]
            column_items = [0.0, 0.0, 0.0]
            for at in range(sum(others)):
                kind = other_refs[3 * at : 3 * at + 3]
                if at < others[0]:
                    row_items = [old + ref[...] for old, ref in zip(row_items, kind)]
                else:
                    column_items = [old + ref[...] for old, ref in zip(column_items, kind)]
            gain, bias = gain_ref[...], bias_ref[...]
            grad_gain = grad_bias = 0.0
            half = BR // 2
            for direction, items in enumerate((row_items, column_items)):
                grad_qkv, gain_row, bias_row = direction_grads(
                    items[0], items[1], gain, bias, wt_ref[direction]
                )
                grad_gain = grad_gain + gain_row
                grad_bias = grad_bias + bias_row
                for s in range(2):
                    for item in range(3):
                        at = direction * 3 * half + item * half
                        take = item * BR + s * half
                        pack_ref[s, at : at + half] = grad_qkv[take : take + half]
            small2 = small2_ref[...]
            for s in range(2):
                cut = slice(s * half, (s + 1) * half)
                lepe = jnp.concatenate(
                    [row_items[2][:, cut], column_items[2][:, cut], jnp.zeros((16, BR), F32)], axis=1
                )
                head = jnp.concatenate(
                    [grad_gain, grad_bias, small2[:4], small2[4 + 2 * s : 6 + 2 * s]], axis=0
                )
                pack_ref[s, SMALL_AT : SMALL_AT + 8] = head
                pack_ref[s, SMALL_AT + 8 : SMALL_AT + 24] = lepe
                pack_ref[s, SMALL_AT + 24 :] = jnp.zeros((LAST_ROWS - SMALL_AT - 24, 2 * BR), F32)
            core = core_place(info)
            rows = LAST_ROWS // 2
            for s in range(2):
                mine = pl.multiple_of(core * rows, 8)
                theirs = pl.multiple_of((1 - core) * rows, 8)
                kept_ref[s] = pack_ref[s, pl.ds(mine, rows)].astype(BF16)
                sent_ref[s] = pack_ref[s, pl.ds(theirs, rows)].astype(BF16)


def input_kernel(image, start, first, *refs):
    heights, info, x_ref, gp_ref, gmid_ref, vk_ref, vr_ref, wt_ref, gain_ref = refs[:9]
    refs = refs[9:] if first else refs[10:]
    out_ref, mark_ref, whole, left, right = refs
    mark_ref[...] = jnp.zeros_like(mark_ref)
    pair = start + pl.program_id(0)
    place = tensor_place(info)
    height, width = sides(image, heights, info)
    row_base = place * HALF + pair * 2 * STRIPE
    mask = twice(as_float(inside(split_index(PAIR, PW, BR), row_base, 0, height, width)))
    unit, inverse = norm_parts(x_ref[0].astype(F32) * mask)
    first_half = place == 0
    own = vk_ref[0].astype(F32)
    other = vr_ref[0].astype(F32)
    left[...] = jnp.where(first_half, own, other)
    right[...] = jnp.where(first_half, other, own)
    merge_columns(left, right, whole)
    parts = [dot(gp_ref[k], wt_ref[0]) for k in range(2)]
    grad_normed = jnp.concatenate(parts, axis=0) + whole[...]
    back = norm_back(grad_normed, unit, inverse, gain_ref[...])
    out_ref[0] = (mask * (gmid_ref[0] + back)).astype(BF16)


def unpack_first_kernel(info, a_ref, ax_ref, b_ref, bx_ref, fc1_ref, fc2_ref, proj_ref, mark_ref):
    mark_ref[...] = jnp.zeros_like(mark_ref)
    core, along = core_place(info) == 0, along_place(info) == 0
    quarters = []
    for c in range(2):
        for side in range(2):
            here = core if c == 0 else jnp.logical_not(core)
            near = along if side == 0 else jnp.logical_not(along)
            mine = jnp.where(near, a_ref[...].astype(F32), ax_ref[...].astype(F32))
            theirs = jnp.where(near, b_ref[...].astype(F32), bx_ref[...].astype(F32))
            quarters.append(jnp.where(here, mine, theirs))
    total = jnp.concatenate(quarters, axis=0)
    fc1_ref[:, :CHUNK] = total[:CHUNK]
    fc1_ref[:, CHUNK:] = total[CHUNK : 2 * CHUNK]
    fc2_ref[...] = total[2 * CHUNK : 4 * CHUNK]
    proj_ref[...] = total[4 * CHUNK :]


def unpack_last_kernel(
    info, c_ref, cx_ref, qkv_ref, lepe_ref, shift_ref, b1_ref,
    gain1_ref, bias1_ref, gain2_ref, bias2_ref, projb_ref, b2_ref,
):
    core = core_place(info) == 0
    mine, theirs = c_ref[...].astype(F32), cx_ref[...].astype(F32)
    last = jnp.concatenate([jnp.where(core, mine, theirs), jnp.where(core, theirs, mine)], axis=0)
    half = BR // 2
    for direction in range(2):
        for item in range(3):
            at = direction * 3 * half + item * half
            qkv_ref[item, direction] = last[at : at + half]
    small = last[SMALL_AT : SMALL_AT + 24]
    for row, ref in enumerate((gain1_ref, bias1_ref, gain2_ref, bias2_ref, projb_ref, b2_ref)):
        ref[...] = small[row : row + 1]
    for part in range(4):
        b1_ref[part : part + 1] = small[6 + part // 2 : 7 + part // 2, part % 2 * BR : (part % 2 + 1) * BR]
    for tap in range(9):
        turned = 8 + 3 * (tap % 3) + tap // 3
        lepe_ref[tap, 0:1] = small[8 + tap : 9 + tap, :half]
        lepe_ref[tap, 1:2] = small[turned : turned + 1, half : 2 * half]
    shift_ref[0:1] = small[17:18, :half]
    shift_ref[1:2] = small[17:18, half : 2 * half]


def spec(shape, index=None):
    if index is None:
        return pl.BlockSpec(shape, lambda i: (0,) * len(shape))
    return pl.BlockSpec(shape, index)


def shaped(shape, dtype):
    return jax.ShapeDtypeStruct(shape, dtype)


SCALARS = pl.BlockSpec(memory_space=pltpu.SMEM)
RESIDENT = pl.BlockSpec(memory_space=pltpu.VMEM)


def call(
    kernel, name, grid, in_specs, out_specs, out_shape, scratch, micros, limit, aliases=None, marks=0
):
    known = len(in_specs)

    def body(*refs):
        kernel(*refs[:known], *refs[known + marks :])

    in_specs = list(in_specs) + [pl.BlockSpec(memory_space=pl.ANY)] * marks
    return pl.pallas_call(
        body,
        name=name,
        grid=(grid,),
        in_specs=in_specs,
        out_specs=out_specs,
        out_shape=out_shape,
        scratch_shapes=scratch,
        input_output_aliases=aliases or {},
        cost_estimate=pl.CostEstimate(
            flops=int(micros * FLOPS_PER_MICRO), bytes_accessed=0, transcendentals=0
        ),
        compiler_params=pltpu.CompilerParams(
            vmem_limit_bytes=limit * MIB, dimension_semantics=("arbitrary",)
        ),
    )


def kept_shapes(count):
    return [pltpu.VMEM((count, WIN, WIDE), BF16)] + [
        pltpu.VMEM((count, WIN, BR), BF16) for _ in range(4)
    ] + [pltpu.VMEM((count, WIN, BR), F32)]


def resident(arrays):
    return [pltpu.with_memory_space_constraint(item, pltpu.VMEM) for item in arrays]


def in_hbm(arrays):
    return [pltpu.with_memory_space_constraint(item, pltpu.HBM) for item in arrays]


def forward_scratch():
    return [
        pltpu.VMEM((2, WIDE, BR), BF16),
        pltpu.VMEM((2, WIDE, 2 * BR), BF16),
        pltpu.VMEM((2, WIN, BR), F32),
        pltpu.VMEM((2, WIN, BR), F32),
        pltpu.VMEM((WIN, WIDE), F32),
        pltpu.VMEM((2, PAD_ROWS, BR), F32),
    ]


def backward_scratch():
    return [
        pltpu.VMEM((2, WIDE, BR), BF16),
        pltpu.VMEM((2, WIDE, 2 * BR), BF16),
        pltpu.VMEM((2, WIN, WIDE), BF16),
        pltpu.VMEM((4, PAD_ROWS, BR), F32),
    ]


FLOPS_PER_MICRO = 1.15e9
ATTENTION_LIMIT = 15
MLP_LIMIT = 18


def pack_first(qkv, lepe, shift):
    width = qkv.shape[-1]
    return call(
        pack_kernel, "pack", 1, [spec(qkv.shape), spec(lepe.shape), spec(shift.shape)],
        [spec((2 * FIRST_HALF, width)), spec((FIRST_HALF, width))],
        [shaped((2 * FIRST_HALF, width), BF16), shaped((FIRST_HALF, width), BF16)], [], 1, 8,
    )(*in_hbm([qkv, lepe, shift]))


def pack_late(info, w1, w2, proj, vectors):
    width = w2.shape[1]
    rows = 4 * LATE
    return call(
        late_pack_kernel, "pack_late", 1,
        [SCALARS, spec(w1.shape), spec(w2.shape), spec(proj.shape)] + [spec(v.shape) for v in vectors],
        [spec((rows, width)), spec((LATE, width))],
        [shaped((rows, width), BF16), shaped((LATE, width), BF16)], [], 1, 8,
    )(info, w1, w2, proj, *vectors)


def split_quadrants(info, x_pairs):
    count, _, width = x_pairs.shape
    images = count // 2
    block = (1, WIN, width)

    def clamp(image):
        return lambda i: (jnp.clip(i - 2 * image, 0, 1), 0, 0)

    return call(
        partial(quadrant_kernel, images), "quadrants", count,
        [SCALARS, spec((1, PAIR, width), lambda i: (i, 0, 0))],
        [spec(block, lambda i: (i, 0, 0))] + [spec(block, clamp(image)) for image in range(images)],
        [shaped((count, WIN, width), BF16)] + [shaped((2, WIN, width), BF16)] * images,
        [pltpu.VMEM((PAIR, width), F32), pltpu.VMEM((WIN, width), F32), pltpu.VMEM((WIN, width), F32)],
        2, 16,
    )(info, x_pairs)


def rows_forward(image, heights, info, x_pairs, gain, bias, packs, known):
    count, _, width = x_pairs.shape
    pair = spec((1, PAIR, width), lambda i: (2 * image + i, 0, 0))
    in_specs = [SCALARS, SCALARS, pair, spec((1, width)), spec((1, width))]
    operands = [heights, info, x_pairs, gain, bias]
    out_shapes = kept_shapes(4) + [pltpu.VMEM((4, WIN, BR), BF16)]
    scratch = forward_scratch()
    if known is None:
        in_specs += [spec(item.shape) for item in packs]
        operands += list(packs)
        scratch = [pltpu.VMEM((2 * FIRST_HALF, width), BF16)] + scratch
        out_shapes += [
            pltpu.VMEM((2, width, 3 * BR), BF16), pltpu.VMEM((2, 3 * BR, width), BF16),
            pltpu.VMEM((2, 16, BR), F32),
        ]
    else:
        in_specs += [RESIDENT] * 2
        operands += resident(known)
    return call(
        partial(rows_forward_kernel, image, known is None), "rows_forward", 2, in_specs,
        [RESIDENT] * len(out_shapes), out_shapes, scratch,
        6.5, ATTENTION_LIMIT,
    )(*operands)


def columns_forward(image, heights, info, own, other, gain, bias, weight, taps):
    width = own.shape[2]
    fixed = spec((2, WIN, BR), lambda i: (0, 0, 0))
    return call(
        partial(columns_forward_kernel, image), "columns_forward", 2,
        [
            SCALARS, SCALARS, spec((2, WIN, width), lambda i: (image, 0, 0)), spec((2, WIN, width)),
            spec((1, width)), spec((1, width)), RESIDENT, RESIDENT,
        ],
        [RESIDENT] * 7 + [fixed, fixed],
        kept_shapes(4) + [pltpu.VMEM((4, WIN, width), BF16)] + [shaped((2, WIN, BR), BF16)] * 2,
        [pltpu.VMEM((2, 2 * PAIR, BR), F32), pltpu.VMEM((2 * PAIR, BR), F32)] + forward_scratch(),
        6.5, ATTENTION_LIMIT,
    )(heights, info, own, other, gain, bias, *resident([weight, taps]))


def mlp(heights, info, x_pairs, cot_pairs, mixed_rows, mixed_own, mixed_other, gain, bias, late):
    count, _, width = x_pairs.shape
    images = count // 2
    pair = spec((1, PAIR, width), lambda i: (i, 0, 0))
    part = spec((1, WIN, BR), lambda i: (i, 0, 0))
    row = spec((1, width))
    quarter = (2, 2, GRAD_ROWS // 4, width)
    return call(
        partial(mlp_kernel, images), "feed_forward", count,
        [SCALARS, SCALARS, pair, pair] + [RESIDENT] * (3 * images) + [row, row] + [RESIDENT] * 5,
        [
            pair, pair, spec((2, WIN, BR), lambda i: (i, 0, 0)), part, part, spec((8, width)),
            spec(quarter), spec(quarter),
        ],
        [
            shaped(x_pairs.shape, BF16), shaped(x_pairs.shape, F32), shaped((2 * count, WIN, BR), BF16),
            shaped((count, WIN, BR), BF16), shaped((count, WIN, BR), BF16), shaped((8, width), F32),
            shaped(quarter, BF16), shaped(quarter, BF16),
        ],
        [
            pltpu.VMEM((2, GRAD_ROWS, width), F32),
            pltpu.VMEM((2 * BR, width), BF16), pltpu.VMEM((8 * LATE, width), BF16),
            pltpu.VMEM((PAIR, BR), F32), pltpu.VMEM((WIN, BR), F32), pltpu.VMEM((WIN, BR), F32),
            pltpu.VMEM((PAIR, width), BF16), pltpu.VMEM((PAIR, width), BF16),
            pltpu.VMEM((width, PAIR), BF16), pltpu.VMEM((width, PAIR), BF16),
        ],
        24, MLP_LIMIT,
    )(
        heights, info, x_pairs, cot_pairs, *resident([*mixed_rows, *mixed_own, *mixed_other]), gain, bias,
        *resident(late),
    )


def columns_backward(image, heights, info, grad_own, grad_other, kept, unit, weight_t, taps):
    width = weight_t.shape[2]
    fixed = spec((2, WIN, width))
    grads = spec((2, WIN, BR), lambda i: (image, 0, 0))
    return call(
        partial(columns_backward_kernel, image), "columns_backward", 2,
        [SCALARS, SCALARS, grads, grads] + [RESIDENT] * 9,
        [spec((width, 3 * BR)), spec((8, 3 * BR)), spec((16, BR)), fixed, fixed],
        [shaped((width, 3 * BR), F32), shaped((8, 3 * BR), F32), shaped((16, BR), F32)]
        + [shaped((2, WIN, width), BF16)] * 2,
        [pltpu.VMEM((2 * PAIR, BR), F32), pltpu.VMEM((2, 2 * PAIR, BR), F32)] + backward_scratch(),
        9.7, ATTENTION_LIMIT,
    )(heights, info, grad_own, grad_other, *resident([*kept, unit, weight_t, taps]))


def rows_backward(image, start, count, heights, info, x_pairs, grad_mixed, kept, weight_t, taps, final):
    width = weight_t.shape[2]
    at = 2 * image + start
    pair = spec((1, PAIR, width), lambda i: (at + i, 0, 0))
    in_specs = [SCALARS, SCALARS, pair, spec((2, WIN, BR), lambda i: (at + i, 0, 0))] + [RESIDENT] * 8
    operands = [heights, info, x_pairs, grad_mixed, *resident([*kept, weight_t, taps])]
    sum_shapes = [(width, 3 * BR), (8, 3 * BR), (16, BR)]
    out_specs = [spec((2, WIN, 3 * BR), lambda i: (i, 0, 0))]
    out_shapes = [shaped((2 * count, WIN, 3 * BR), BF16)]
    scratch = backward_scratch()
    others = (0, 0)
    if final is None:
        out_specs += [spec(shape) for shape in sum_shapes]
        out_shapes += [shaped(shape, F32) for shape in sum_shapes]
    else:
        gain, bias, small2, row_items, column_items = final
        others = (len(row_items), len(column_items))
        in_specs += [spec((1, width)), spec((1, width)), spec((8, width))]
        operands += [gain, bias, small2]
        for item in [*row_items, *column_items]:
            in_specs += [spec(shape) for shape in sum_shapes]
            operands += list(item)
        half = (2, LAST_ROWS // 2, width)
        out_specs += [spec(half), spec(half)]
        out_shapes += [shaped(half, BF16), shaped(half, BF16)]
        scratch = (
            [pltpu.VMEM(shape, F32) for shape in sum_shapes]
            + [pltpu.VMEM((2, LAST_ROWS, width), F32)]
            + scratch
        )
    return call(
        partial(rows_backward_kernel, image, start, count, final is not None, others), "rows_backward",
        count, in_specs, out_specs, out_shapes, scratch, 4.8 * count, ATTENTION_LIMIT,
    )(*operands)


def input_rows(
    image, start, count, heights, info, x_pairs, rows, grad_mid, back_own, back_other, weight_t, gain,
    previous,
):
    width = weight_t.shape[2]
    pair = spec((1, PAIR, width), lambda i: (2 * image + start + i, 0, 0))
    part = spec((1, WIN, width), lambda i: (start + i, 0, 0))
    in_specs = [
        SCALARS, SCALARS, pair, spec((2, WIN, 3 * BR), lambda i: (start + i, 0, 0)), pair, part, part,
        RESIDENT, spec((1, width)),
    ]
    operands = [
        heights, info, x_pairs, rows, grad_mid, back_own, back_other, *resident([weight_t]), gain,
    ]
    aliases = {}
    if previous is not None:
        in_specs.append(pl.BlockSpec(memory_space=pl.ANY))
        operands.append(previous)
        aliases = {len(operands) - 1: 0}
    return call(
        partial(input_kernel, image, start, previous is None), "input_rows", count, in_specs,
        [pair, spec((8, 128))], [shaped(x_pairs.shape, BF16), shaped((8, 128), F32)],
        [pltpu.VMEM((PAIR, width), F32), pltpu.VMEM((WIN, width), F32), pltpu.VMEM((WIN, width), F32)],
        1.6 * count, 20, aliases,
    )(*operands)


def unpack_first(info, a, ax, b, bx, hidden, width):
    return call(
        unpack_first_kernel, "unpack_first", 1, [SCALARS] + [spec(a.shape)] * 4,
        [spec((width, hidden)), spec((hidden, width)), spec((BR, width)), spec((8, 128))],
        [
            shaped((width, hidden), F32), shaped((hidden, width), F32), shaped((BR, width), F32),
            shaped((8, 128), F32),
        ],
        [], 1, 16,
    )(info, a, ax, b, bx)


def unpack_last(info, c, cx, width):
    row = spec((1, width))
    return call(
        unpack_last_kernel, "unpack_last", 1, [SCALARS] + [spec(c.shape)] * 2,
        [
            spec((3, 2, BR // 2, width)), spec((9, 2, BR // 2)), spec((2, BR // 2)), spec((4, BR)),
            row, row, row, row, row, row,
        ],
        [
            shaped((3, 2, BR // 2, width), F32), shaped((9, 2, BR // 2), F32), shaped((2, BR // 2), F32),
            shaped((4, BR), F32),
        ] + [shaped((1, width), F32)] * 6,
        [], 1, 16,
    )(info, c, cx)


def after(value, *marks):
    return lax.optimization_barrier((value,) + marks)[0]


def swap_tensor(values):
    return lax.ppermute(values, "tensor", [(0, 1), (1, 0)])


def swap_dp(values, size, mask):
    return lax.ppermute(values, "dp", [(i, i ^ mask) for i in range(size)])


def swap_both(values, size, mask):
    pairs = [(2 * i + t, 2 * (i ^ mask) + 1 - t) for i in range(size) for t in range(2)]
    return lax.ppermute(values, ("dp", "tensor"), pairs)


def add_kernel(count, *refs):
    refs, outs = refs[:count], refs[count:]
    items = [ref[...].astype(F32) for ref in refs]
    while len(items) > 1:
        items = [items[i] + items[i + 1] for i in range(0, len(items), 2)]
    whole = items[0].astype(BF16)
    whole = whole.reshape((len(outs),) + outs[0].shape)
    for at, out in enumerate(outs):
        out[...] = whole[at]


def added(*items, parts=1, marks=()):
    shape = items[0].shape
    last = shape[-2:]
    outs = call(
        partial(add_kernel, len(items)), "add", 1, [spec(shape)] * len(items), [spec(last)] * parts,
        [shaped(last, BF16)] * parts, [], 0.5, 8, marks=len(marks),
    )(*items, *marks)
    return outs[0] if parts == 1 else outs


def partner_groups(size):
    bits = list(range(1, size.bit_length() - 1))
    groups = []
    while bits:
        pair, bits = bits[:2], bits[2:]
        low = 1 << pair[0]
        groups.append([low] if len(pair) == 1 else [low, 1 << pair[1], low | (1 << pair[1])])
    return groups


def per_device(
    size, block_input, heights, widths, norm1_gain, norm1_bias, qkv_weight, lepe_weight, lepe_bias,
    proj_weight, proj_bias, norm2_gain, norm2_bias, fc1_weight, fc1_bias, fc2_weight, fc2_bias,
    cotangent,
):
    images, local_cells, width = block_input.shape
    hidden = fc1_weight.shape[1]
    x_pairs = block_input.reshape(2 * images, PAIR, width)
    cot_pairs = cotangent.reshape(2 * images, PAIR, width)
    gain1, bias1 = norm1_gain[None], norm1_bias[None]
    pairs = range(images)
    index = lax.axis_index("dp")
    places = jnp.stack([lax.axis_index("tensor"), index % 2, index // 2 % 2]).astype(jnp.int32)
    info = jnp.concatenate([widths, places])

    own, own_half = pack_first(
        qkv_weight.transpose(1, 2, 3, 0), lepe_weight.transpose(1, 0, 2), lepe_bias
    )
    near = swap_tensor(own_half)
    far = swap_dp(near, size, 1)
    quad_own, *quad_send = split_quadrants(info, after(x_pairs, own))
    vectors = (fc1_bias, proj_bias, fc2_bias)
    late_own, late_send = pack_late(info, *after((fc1_weight, fc2_weight, proj_weight, vectors), quad_own))
    quad_other = [swap_tensor(quad_send[0])]

    late_near = swap_tensor(late_send)

    def forward_rows(image, mark, known):
        return rows_forward(
            image, after(heights, mark), info, x_pairs, gain1, bias1, (own, near, far), known
        )

    *kept, mixed, weight, weight_t, taps = forward_rows(0, late_own, None)
    row_kept, mixed_rows = [kept], [mixed]
    quad_other += [swap_tensor(after(item, taps)) for item in quad_send[1:]]
    columns = []
    for image in pairs:
        *kept, unit, keep, send = columns_forward(
            image, heights, info, quad_own, quad_other[image], gain1, bias1, weight, taps
        )
        columns.append((kept, unit, keep, swap_tensor(send)))
        if image == 0:
            ready = after(late_near, keep)
            late_parts = [ready] + [swap_dp(ready, size, mask) for mask in (2, 1, 3)]
    for image in range(1, images):
        *kept, mixed = forward_rows(image, columns[-1][2], (weight, taps))
        row_kept.append(kept)
        mixed_rows.append(mixed)
    output, grad_mid, grad_rows, grad_keep, grad_send, small2, kept1, sent1 = mlp(
        heights, info, x_pairs, cot_pairs, mixed_rows, [item[2] for item in columns],
        [item[3] for item in columns], norm2_gain[None], norm2_bias[None], (late_own, *late_parts),
    )
    grad_other = swap_tensor(grad_send)

    arrived = swap_dp(sent1, size, 1)
    bits = size.bit_length() - 1
    row_pairs, row_sums = [], []

    def backward_rows(image, start, count, mark, final=None):
        rows, *rest = rows_backward(
            image, start, count, after(heights, mark), info, x_pairs, grad_rows, row_kept[image],
            weight_t, taps, final,
        )
        row_pairs.append(rows)
        return rest

    for image in range(images - 1):
        row_sums.append(backward_rows(image, 0, 2, small2))
    mark = row_sums[-1][2] if row_sums else small2
    first, toward_x, toward_y, toward_xy = added(kept1, after(arrived, mark), parts=4)
    crossed = [swap_dp(toward_x, size, 2), swap_tensor(toward_y), swap_both(toward_xy, size, 2)]
    mark = first
    column_back = []
    for image in pairs:
        kept, unit, _, _ = columns[image]
        *column_sums, back_keep, back_send = columns_backward(
            image, after(heights, mark), info, grad_keep, grad_other, kept, unit, weight_t, taps
        )
        column_back.append((column_sums, back_keep, swap_tensor(back_send)))
        mark = column_sums[2]
        if image == 0:
            first = added(first, *[after(item, mark) for item in crossed])
        else:
            first = added(first, after(arrived, mark))
        bit = 2 + image
        arrived = swap_dp(first, size, 1 << bit) if bit < bits else jnp.zeros_like(first)
        mark = first
    final = (gain1, bias1, small2, row_sums, [item[0] for item in column_back])
    kept2, sent2 = backward_rows(images - 1, 0, 2, mark, final)

    input_grad = None

    def meanwhile(image, start, count, mark):
        nonlocal input_grad
        _, back_keep, back_other = column_back[image]
        input_grad, mark = input_rows(
            image, start, count, after(heights, mark), info, x_pairs, row_pairs[image], grad_mid,
            back_keep, back_other, weight_t, gain1, input_grad,
        )
        return mark

    first = added(first, arrived, marks=[kept2])
    core_part = swap_dp(after(sent2, first), size, 1)
    last, toward_y = added(kept2, core_part, parts=2, marks=[item[2] for item in column_back])
    for bit in range(2 + images, bits):
        first = added(first, swap_dp(first, size, 1 << bit))
    first_x = swap_dp(first, size, 2)
    across = swap_tensor(toward_y)
    for image in range(images - 1):
        mark = meanwhile(image, 0, 2, last)
    last = added(last, across, marks=[mark])
    for at, group in enumerate(partner_groups(size)):
        arrived = [swap_dp(last, size, mask) for mask in group]
        marks = []
        if at == 0:
            marks = [meanwhile(images - 1, 0, 1, last), first_x]
        if at == 1:
            first_core = [swap_dp(after(item, last), size, 1) for item in (first, first_x)]
            grad_fc1, grad_fc2, grad_proj, mark = unpack_first(
                after(info, last), first, first_x, first_core[0], first_core[1], hidden, width
            )
            marks = [meanwhile(images - 1, 1, 1, last), mark]
        last = added(last, *arrived, marks=marks)
    last_other = swap_dp(last, size, 1)
    (
        grad_qkv, grad_lepe, grad_shift, grad_b1,
        grad_gain1, grad_bias1, grad_gain2, grad_bias2, grad_projb, grad_b2,
    ) = unpack_last(info, last, last_other, width)
    return (
        output.reshape(block_input.shape), input_grad.reshape(block_input.shape),
        grad_gain1[0], grad_bias1[0], grad_qkv.transpose(3, 0, 1, 2), grad_lepe.transpose(1, 0, 2),
        grad_shift, grad_proj.reshape(2, BR // 2, width), grad_projb[0], grad_gain2[0], grad_bias2[0],
        grad_fc1, grad_b1.reshape(-1), grad_fc2, grad_b2[0],
    )


def solution(mesh):
    placed = (
        P("dp", "tensor", None),
        P("dp"),
        P("dp"),
        P(),
        P(),
        P(None, None, None, "tensor"),
        P(None, None, "tensor"),
        P(None, "tensor"),
        P(None, "tensor", None),
        P(),
        P(),
        P(),
        P(None, "tensor"),
        P("tensor"),
        P("tensor", None),
        P(),
        P("dp", "tensor", None),
    )
    return jax.shard_map(
        partial(per_device, mesh.shape["dp"]),
        mesh=mesh,
        in_specs=placed,
        out_specs=(
            P("dp", "tensor", None),
            P("dp", "tensor", None),
            P(),
            P(),
            P(None, None, None, "tensor"),
            P(None, None, "tensor"),
            P(None, "tensor"),
            P(None, "tensor", None),
            P(),
            P(),
            P(),
            P(None, "tensor"),
            P("tensor"),
            P("tensor", None),
            P(),
        ),
        check_vma=False,
    )
```

```python
from functools import partial

import jax
import jax.numpy as jnp
from jax import lax
from jax.experimental import pallas as pl
from jax.experimental.pallas import tpu as pltpu
from jax.sharding import PartitionSpec as P

HEAD_DIM = 32
STRIPE = 7
PH = 56
PW = 56
HEADS = 4
BR = HEADS * HEAD_DIM
WIN = STRIPE * PW
WIDE = HEADS * WIN
MAIN = WIN // 128 * 128
REST = WIN - MAIN
GAP = 64
PAD_ROWS = STRIPE * GAP + 16
HALF = 28
PAIR = 2 * WIN
CHUNK = 256
CHUNKS = [(lo, min(lo + CHUNK, WIDE)) for lo in range(0, WIDE, CHUNK)]

MASKED_WEIGHT = 9.357622968840175e-14
EPSILON = 1e-05
LOG2E = 1.4426950408889634
ROOT_HALF = 0.7071067811865476
DENSITY = 0.3989422804014327
DEN_LOW = 2.0**-60
DEN_HIGH = 2.0**100

F32 = jnp.float32
BF16 = jnp.bfloat16
MIB = 2**20
GRAD_ROWS = 1152
LAST_ROWS = 416
SMALL_AT = 3 * BR
FIRST_HALF = 208
LATE = 304


def dot(a, b):
    return jnp.dot(a, b, preferred_element_type=F32)


def dot_nt(a, b):
    return lax.dot_general(a, b, (((1,), (1,)), ((), ())), preferred_element_type=F32)


def dot_tn(a, b):
    return lax.dot_general(a, b, (((0,), (0,)), ((), ())), preferred_element_type=F32)


def split_index(count, width, lanes, axis=0):
    shape = (count, lanes) if axis == 0 else (lanes, count)
    index = lax.broadcasted_iota(jnp.int32, shape, axis)
    step = -(-65536 // width)
    major = lax.shift_right_logical(index * step, 16)
    return major, index - major * width


def inside(parts, base_major, base_minor, lim_major, lim_minor):
    major, minor = parts
    return (major < lim_major - base_major) & (minor < lim_minor - base_minor)


def as_float(flag):
    return jnp.where(flag, 1.0, 0.0).astype(F32)


def twice(values):
    return jnp.concatenate([values, values], axis=1)


def head_lane(head):
    lane = lax.broadcasted_iota(jnp.int32, (1, BR), 1)
    return as_float((lane >= head * HEAD_DIM) & (lane < (head + 1) * HEAD_DIM))


def head_blocks(values):
    lanes = [head_lane(head) for head in range(HEADS)]
    top = [values[:MAIN] * lane for lane in lanes]
    rest = [values[MAIN:] * lane for lane in lanes]
    return jnp.concatenate(top + rest, axis=0)


def from_wide(values):
    rows = []
    for head in range(HEADS):
        own = values[head * HEAD_DIM : (head + 1) * HEAD_DIM]
        rest = HEADS * MAIN + head * REST
        rows.append(
            jnp.concatenate(
                [own[:, head * MAIN : (head + 1) * MAIN], own[:, rest : rest + REST]], axis=1
            )
        )
    return jnp.concatenate(rows, axis=0)


def norm_parts(values):
    centred = values - jnp.mean(values, -1, keepdims=True)
    inverse = lax.rsqrt(jnp.mean(centred * centred, -1, keepdims=True) + EPSILON)
    return centred * inverse, inverse


def norm_back(grad_rows, unit_rows, inverse, gain):
    scaled = grad_rows * gain
    return inverse * (
        scaled
        - jnp.mean(scaled, -1, keepdims=True)
        - unit_rows * jnp.mean(scaled * unit_rows, -1, keepdims=True)
    )


def spread(pad_ref, values):
    for row in range(STRIPE):
        pad_ref[8 + GAP * row : 8 + GAP * row + PW] = values[row * PW : (row + 1) * PW]


def neighbours(pad_ref):
    return [
        [pad_ref[8 + GAP * row + shift : 8 + GAP * row + shift + PW] for shift in (-1, 0, 1)]
        for row in range(STRIPE)
    ]


def filtered(rows, taps, flip):
    order = [8 - tap if flip else tap for tap in range(9)]
    taps = [taps[tap : tap + 1] for tap in order]
    out = []
    for row in range(STRIPE):
        total = None
        for a in range(3):
            if 0 <= row + a - 1 < STRIPE:
                for e in range(3):
                    term = taps[3 * a + e] * rows[row + a - 1][e]
                    total = term if total is None else total + term
        out.append(total)
    return jnp.concatenate(out, axis=0)


def tap_sums(grad_rows, value_rows):
    sums = []
    for a in range(3):
        for e in range(3):
            total = None
            for row in range(STRIPE):
                if 0 <= row + a - 1 < STRIPE:
                    term = grad_rows[row][1] * value_rows[row + a - 1][e]
                    total = term if total is None else total + term
            sums.append(jnp.sum(total, 0, keepdims=True))
    total = grad_rows[0][1]
    for row in range(1, STRIPE):
        total = total + grad_rows[row][1]
    sums.append(jnp.sum(total, 0, keepdims=True))
    return sums


def window_valid(window_base, lim_major, lim_minor):
    return inside(split_index(WIN, PW, BR), window_base, 0, lim_major, lim_minor)


def window_scores(projected, valid, first, k, refs):
    p_ref, q_ref, k_ref, v_ref, o_ref, rl_ref, kb_ref, vb_ref, lepe_ref, mixed_ref, pad_ref = refs
    queries = (projected[:, :BR] * HEAD_DIM**-0.5).astype(BF16)
    key_rows = projected[:, BR : 2 * BR]
    values = projected[:, 2 * BR :].astype(BF16).astype(F32)
    valid_float = as_float(valid)
    weight = jnp.where(valid, 1.0, MASKED_WEIGHT)
    q_ref[first + k] = queries
    k_ref[first + k] = (key_rows * valid_float).astype(BF16)
    v_ref[first + k] = values.astype(BF16)
    kb_ref[k] = head_blocks(key_rows * valid_float).astype(BF16)
    vb_ref[k, :, :BR] = head_blocks(values * weight).astype(BF16)
    vb_ref[k, :, BR:] = head_blocks(weight).astype(BF16)
    for lo, hi in CHUNKS:
        p_ref[first + k, :, lo:hi] = jnp.exp2(dot_nt(queries, kb_ref[k, lo:hi]) * LOG2E).astype(BF16)
    return values


def window_mixed(values, taps, shift, first, k, refs):
    p_ref, q_ref, k_ref, v_ref, o_ref, rl_ref, kb_ref, vb_ref, lepe_ref, mixed_ref, pad_ref = refs
    sums = dot(p_ref[first + k], vb_ref[k])
    totals = sums[:, BR:]
    inverse = 1.0 / totals
    attended = sums[:, :BR] * inverse
    o_ref[first + k] = attended
    rl_ref[first + k] = inverse
    spread(pad_ref.at[k], values)
    lepe = filtered(neighbours(pad_ref.at[k]), taps, False) + shift
    lepe_ref[k] = lepe
    mixed_ref[k] = attended + lepe
    safe = (totals > DEN_LOW) & (totals < DEN_HIGH)
    return jnp.max(jnp.where(safe, 0.0, 1.0))


def window_forward_safe(first, k, refs, s_ref):
    p_ref, q_ref, k_ref, v_ref, o_ref, rl_ref, kb_ref, vb_ref, lepe_ref, mixed_ref, _ = refs
    s_ref[...] = dot_nt(q_ref[first + k], kb_ref[k]) * LOG2E
    for head in range(HEADS):
        cut = slice(head * MAIN, (head + 1) * MAIN)
        rest = HEADS * MAIN + head * REST
        left = s_ref[:, cut]
        right = s_ref[:, rest : rest + REST]
        peak = jnp.maximum(jnp.max(left, -1, keepdims=True), jnp.max(right, -1, keepdims=True))
        s_ref[:, cut] = left - peak
        s_ref[:, rest : rest + REST] = right - peak
    for lo, hi in CHUNKS:
        p_ref[first + k, :, lo:hi] = jnp.exp2(s_ref[:, lo:hi]).astype(BF16)
    sums = dot(p_ref[first + k], vb_ref[k])
    inverse = 1.0 / sums[:, BR:]
    attended = sums[:, :BR] * inverse
    o_ref[first + k] = attended
    rl_ref[first + k] = inverse
    mixed_ref[k] = attended + lepe_ref[k]


def window_scores_back(grads, first, k, refs):
    p_ref, q_ref, k_ref, v_ref, o_ref, rl_ref, kb_ref, vb_ref, ds_ref, pad_ref = refs
    lane = lax.broadcasted_iota(jnp.int32, (WIN, BR), 1)
    scaled = (grads * rl_ref[first + k]).astype(BF16)
    product = scaled.astype(F32) * o_ref[first + k]
    high = product.astype(BF16)
    low = (product - high.astype(F32)).astype(BF16)
    row = lax.broadcasted_iota(jnp.int32, (2 * BR, BR), 0)
    col = lax.broadcasted_iota(jnp.int32, (2 * BR, BR), 1)
    head_of = lax.shift_right_logical(row & (BR - 1), 5)
    picks = as_float((col < 2 * HEADS) & (head_of == (col & (HEADS - 1)))).astype(BF16)
    inner = dot(jnp.concatenate([high, low], axis=1), picks)
    inner_high = inner.astype(BF16).astype(F32)
    extra = jnp.where(lane < HEADS, inner_high, inner - inner_high).astype(BF16)
    left = jnp.concatenate([scaled, extra], axis=1)
    values = v_ref[first + k].astype(F32)
    vb_ref[k, :, :BR] = head_blocks(values).astype(BF16)
    kb_ref[k] = head_blocks(k_ref[first + k].astype(F32)).astype(BF16)
    for lo, hi in CHUNKS:
        grad_probs = dot_nt(left, vb_ref[k, lo:hi])
        ds_ref[k, :, lo:hi] = grad_probs.astype(BF16) * p_ref[first + k, :, lo:hi]
    scaled_t = scaled.astype(F32).T.astype(BF16)
    return dot(scaled_t, p_ref[first + k])


def window_products_back(scaled, first, k, refs):
    p_ref, q_ref, k_ref, v_ref, o_ref, rl_ref, kb_ref, vb_ref, ds_ref, pad_ref = refs
    grad_query = dot(ds_ref[k], kb_ref[k]) * (HEAD_DIM**-0.5)
    query_t = q_ref[first + k].astype(F32).T.astype(BF16)
    return grad_query, dot(query_t, ds_ref[k]), scaled


def window_rows_back(grads, products, base, lim_major, lim_minor, taps, first, k, refs):
    v_ref, pad_ref = refs[3], refs[9]
    grad_query, wide_key, wide_value = products
    values = v_ref[first + k].astype(F32)
    valid_t = inside(split_index(WIN, PW, BR, 1), base, 0, lim_major, lim_minor)
    weight_t = jnp.where(valid_t, 1.0, MASKED_WEIGHT)
    grad_key = (from_wide(wide_key) * jnp.where(valid_t, 1.0, 0.0)).T
    grad_value = (from_wide(wide_value) * weight_t).T
    spread(pad_ref.at[2 * k], grads)
    spread(pad_ref.at[2 * k + 1], values)
    grad_rows, value_rows = neighbours(pad_ref.at[2 * k]), neighbours(pad_ref.at[2 * k + 1])
    back, tap_rows = filtered(grad_rows, taps, True), tap_sums(grad_rows, value_rows)
    out = jnp.concatenate([grad_query, grad_key, grad_value + back], axis=1)
    return out.astype(BF16), tap_rows


def window_pair_back(grads, first, refs):
    scaled = [window_scores_back(grads[k], first, k, refs) for k in range(2)]
    return [window_products_back(scaled[k], first, k, refs) for k in range(2)]


def set_indicator(vb_ref):
    row = lax.broadcasted_iota(jnp.int32, (WIDE, BR), 0)
    col = lax.broadcasted_iota(jnp.int32, (WIDE, BR), 1)
    head = jnp.zeros((WIDE, BR), jnp.int32)
    for cut in range(1, HEADS):
        head = head + jnp.where(row >= cut * MAIN, 1, 0)
    tail = lax.shift_right_logical(row - HEADS * MAIN, 3)
    head = jnp.where(row >= HEADS * MAIN, tail, head)
    hit = (col < 2 * HEADS) & ((col & (HEADS - 1)) == head)
    for k in range(2):
        vb_ref[k, :, BR:] = jnp.where(hit, -1.0, 0.0).astype(BF16)


def split_columns(source, left, right):
    for row in range(STRIPE * 2):
        left[row * HALF : (row + 1) * HALF] = source[row * PW : row * PW + HALF]
        right[row * HALF : (row + 1) * HALF] = source[row * PW + HALF : (row + 1) * PW]


def merge_columns(left, right, target):
    for row in range(STRIPE * 2):
        target[row * PW : row * PW + HALF] = left[row * HALF : (row + 1) * HALF]
        target[row * PW + HALF : (row + 1) * PW] = right[row * HALF : (row + 1) * HALF]


def sides(image, heights, info):
    return heights[image], info[image]


def tensor_place(info):
    return info[info.shape[0] - 3]


def core_place(info):
    return info[info.shape[0] - 2]


def along_place(info):
    return info[info.shape[0] - 1]


def pack_kernel(qkv_ref, lepe_ref, shift_ref, out_ref, send_ref):
    for item in range(3):
        for direction in range(2):
            row = (2 * item + direction) * BR // 2
            out_ref[row : row + BR // 2] = qkv_ref[item, direction]
    rows = [
        jnp.concatenate([lepe_ref[tap, 0:1], lepe_ref[tap, 1:2]], axis=1).astype(F32)
        for tap in range(9)
    ]
    rows.append(jnp.concatenate([shift_ref[0:1], shift_ref[1:2]], axis=1).astype(F32))
    rows.append(jnp.zeros((2 * FIRST_HALF - SMALL_AT - 10, BR), F32))
    small = jnp.concatenate(rows, axis=0)
    out_ref[SMALL_AT:] = jnp.concatenate([small, jnp.zeros_like(small)], axis=1).astype(BF16)
    core = lax.axis_index("dp") % 2
    send_ref[...] = out_ref[pl.ds(pl.multiple_of(core * FIRST_HALF, 16), FIRST_HALF)]


def late_pack_kernel(info, w1_ref, w2_ref, proj_ref, b1_ref, pb_ref, b2_ref, out_ref, send_ref):
    for j in range(2):
        out_ref[j * CHUNK : (j + 1) * CHUNK] = w1_ref[:, j * CHUNK : (j + 1) * CHUNK]
    out_ref[2 * CHUNK : 4 * CHUNK] = w2_ref[...]
    for b in range(2):
        at = 4 * CHUNK + b * BR // 2
        out_ref[at : at + BR // 2] = proj_ref[b]
    first = b1_ref[...].astype(F32).reshape(1, 2 * CHUNK)
    vectors = [first[:, :CHUNK], first[:, CHUNK:]]
    vectors += [ref[...].astype(F32).reshape(1, 2 * BR) for ref in (pb_ref, b2_ref)]
    tail = jnp.concatenate(vectors + [jnp.zeros((4 * LATE - GRAD_ROWS - 4, 2 * BR), F32)], axis=0)
    out_ref[GRAD_ROWS:] = tail.astype(BF16)
    part = 2 * core_place(info) + along_place(info)
    send_ref[...] = out_ref[pl.ds(pl.multiple_of(part * LATE, 16), LATE)]


def quadrant_kernel(images, info, x_ref, own_ref, *rest):
    sends, (whole, left, right) = rest[:images], rest[images:]
    step = pl.program_id(0)
    whole[...] = x_ref[0].astype(F32)
    split_columns(whole, left, right)
    first = tensor_place(info) == 0
    own_ref[0] = jnp.where(first, left[...], right[...]).astype(BF16)
    other = jnp.where(first, right[...], left[...]).astype(BF16)
    for image in range(images):

        @pl.when(step // 2 == image)
        def _():
            sends[image][0] = other


def rows_forward_kernel(image, first, *refs):
    heights, info, x_ref, gain_ref, bias_ref = refs[:5]
    if first:
        own_ref, near_ref, far_ref, p_ref, q_ref, k_ref, v_ref, o_ref, rl_ref, m_ref, w_ref, wt_ref, taps_ref = refs[5:18]
        other_ref = refs[-7]
    else:
        w_ref, taps_ref, p_ref, q_ref, k_ref, v_ref, o_ref, rl_ref, m_ref = refs[5:14]
    kb_ref, vb_ref, lepe_ref, mixed_ref, s_ref, pad_ref = refs[-6:]
    step = pl.program_id(0)
    height, width = sides(image, heights, info)
    row_base = tensor_place(info) * HALF + step * 2 * STRIPE

    def unpack_weights():
        core = core_place(info)
        for part, piece in ((core, near_ref), (1 - core, far_ref)):
            other_ref[pl.ds(pl.multiple_of(part * FIRST_HALF, 16), FIRST_HALF)] = piece[...]
        for direction in range(2):
            for item in range(3):
                row = (2 * item + direction) * BR // 2
                at = item * BR
                wt_ref[direction, at : at + BR // 2] = own_ref[row : row + BR // 2]
                wt_ref[direction, at + BR // 2 : at + BR] = other_ref[row : row + BR // 2]
            w_ref[direction] = wt_ref[direction].astype(F32).T.astype(BF16)
        own = own_ref[SMALL_AT : SMALL_AT + 16].astype(F32)
        other = other_ref[SMALL_AT : SMALL_AT + 16].astype(F32)
        half = BR // 2
        for direction in range(2):
            cut = slice(direction * half, (direction + 1) * half)
            both = jnp.concatenate([own[:, cut], other[:, cut]], axis=1)
            if direction == 1:
                order = [3 * (tap % 3) + tap // 3 for tap in range(9)] + list(range(9, 16))
                both = jnp.concatenate([both[tap : tap + 1] for tap in order], axis=0)
            taps_ref[direction] = both

    if first:
        pl.when(step == 0)(unpack_weights)

    @pl.when(step == 0)
    def _():
        pad_ref[...] = jnp.zeros_like(pad_ref)

    mask = as_float(inside(split_index(PAIR, PW, BR), row_base, 0, height, width))
    unit, _ = norm_parts(x_ref[0].astype(F32) * twice(mask))
    normed = (unit * gain_ref[...] + bias_ref[...]).astype(BF16)
    projected = dot(normed, w_ref[0])
    refs = (
        p_ref, q_ref, k_ref, v_ref, o_ref, rl_ref, kb_ref, vb_ref, lepe_ref, mixed_ref, pad_ref
    )
    bad = jnp.float32(0)
    values = []
    for k in range(2):
        valid = window_valid(row_base + k * STRIPE, height, width)
        rows = projected[k * WIN : (k + 1) * WIN]
        values.append(window_scores(rows, valid, 2 * step, k, refs))
    for k in range(2):
        bad = jnp.maximum(
            bad, window_mixed(values[k], taps_ref[0, :9], taps_ref[0, 9:10], 2 * step, k, refs)
        )

    @pl.when(bad > 0.0)
    def _():
        def one(k, carry):
            window_forward_safe(2 * step, k, refs, s_ref)
            return carry

        lax.fori_loop(0, 2, one, 0)

    for k in range(2):
        m_ref[2 * step + k] = mixed_ref[k].astype(BF16)


def columns_forward_kernel(
    image, heights, info, own_ref, other_ref, gain_ref, bias_ref, w_ref, taps_ref,
    p_ref, q_ref, k_ref, v_ref, o_ref, rl_ref, n_ref, keep_ref, send_ref,
    unit_ref, out_ref, kb_ref, vb_ref, lepe_ref, mixed_ref, s_ref, pad_ref,
):
    step = pl.program_id(0)
    place = tensor_place(info)
    height, width = sides(image, heights, info)
    column_base = place * HALF

    @pl.when(step == 0)
    def _():
        pad_ref[...] = jnp.zeros_like(pad_ref)
        for source, side in ((own_ref, place), (other_ref, 1 - place)):
            for s in range(2):
                flag = inside(
                    split_index(WIN, HALF, BR), side * HALF + s * 2 * STRIPE, column_base,
                    height, width,
                )
                unit, _ = norm_parts(source[s].astype(F32) * twice(as_float(flag)))
                start = pl.multiple_of(side * PAIR + s * WIN, 8)
                unit_ref[0, pl.ds(start, WIN)] = unit[:, :BR]
                unit_ref[1, pl.ds(start, WIN)] = unit[:, BR:]

    refs = (
        p_ref, q_ref, k_ref, v_ref, o_ref, rl_ref, kb_ref, vb_ref, lepe_ref, mixed_ref, pad_ref
    )
    bad = jnp.float32(0)
    values = []
    for k in range(2):
        column = (2 * step + k) * STRIPE
        halves = [
            jnp.concatenate(
                [unit_ref[j, pl.ds(column + q, PH, stride=HALF)] for q in range(STRIPE)], axis=0
            )
            for j in range(2)
        ]
        unit = jnp.concatenate(halves, axis=1)
        n_ref[2 * step + k] = unit.astype(BF16)
        normed = (unit * gain_ref[...] + bias_ref[...]).astype(BF16)
        valid = window_valid(column_base + column, width, height)
        values.append(window_scores(dot(normed, w_ref[1]), valid, 2 * step, k, refs))
    for k in range(2):
        bad = jnp.maximum(
            bad, window_mixed(values[k], taps_ref[1, :9], taps_ref[1, 9:10], 2 * step, k, refs)
        )

    @pl.when(bad > 0.0)
    def _():
        def one(k, carry):
            window_forward_safe(2 * step, k, refs, s_ref)
            return carry

        lax.fori_loop(0, 2, one, 0)

    for k in range(2):
        column = (2 * step + k) * STRIPE
        mixed = mixed_ref[k]
        for q in range(STRIPE):
            out_ref[pl.ds(column + q, PH, stride=HALF)] = mixed[q * PH : (q + 1) * PH]

    @pl.when(step == 1)
    def _():
        for s in range(2):
            keep = pl.multiple_of(place * PAIR + s * WIN, 8)
            send = pl.multiple_of((1 - place) * PAIR + s * WIN, 8)
            keep_ref[s] = out_ref[pl.ds(keep, WIN)].astype(BF16)
            send_ref[s] = pltpu.roll(out_ref[pl.ds(send, WIN)], BR // 2, 1).astype(BF16)


def mlp_kernel(images, *refs):
    heights, info, x_ref, cot_ref = refs[:4]
    mh_refs, mo_refs, mr_refs = (refs[4 + i * images : 4 + (i + 1) * images] for i in range(3))
    refs = refs[4 + 3 * images :]
    gain_ref, bias_ref, late_own, *late_parts = refs[:7]
    out_ref, gmid_ref, gh_ref, gk_ref, gs_ref, small_ref, kept_ref, sent_ref = refs[7:15]
    acc_ref, pw_ref, late_ref, whole, left, right = refs[15:]
    step = pl.program_id(0)
    image, pair = step // 2, step % 2
    place = tensor_place(info)
    height, width = sides(image, heights, info)
    row_base = place * HALF + pair * 2 * STRIPE
    half = BR // 2

    def of_image(items, at):
        value = items[0][at].astype(F32)
        for index in range(1, images):
            value = jnp.where(image == index, items[index][at].astype(F32), value)
        return value

    @pl.when(step == 0)
    def _():
        far = 4 * LATE
        late_ref[:far] = late_own[...]
        core, along = core_place(info), along_place(info)
        for at, piece in enumerate(late_parts):
            part = 2 * (core if at < 2 else 1 - core) + (along if at % 2 == 0 else 1 - along)
            late_ref[pl.ds(pl.multiple_of(far + part * LATE, 16), LATE)] = piece[...]
        for b in range(2):
            at = 4 * CHUNK + b * half
            pw_ref[b * BR : b * BR + half] = late_ref[at : at + half]
            pw_ref[b * BR + half : (b + 1) * BR] = late_ref[far + at : far + at + half]
        acc_ref[...] = jnp.zeros_like(acc_ref)
        small_ref[...] = jnp.zeros_like(small_ref)

    vectors = late_own[GRAD_ROWS : GRAD_ROWS + 16].astype(F32)
    mask = twice(as_float(inside(split_index(PAIR, PW, BR), row_base, 0, height, width)))
    first_half = place == 0
    own = of_image(mo_refs, pair)
    other = of_image(mr_refs, pair)
    left[...] = jnp.where(first_half, own, other)
    right[...] = jnp.where(first_half, other, own)
    merge_columns(left, right, whole)
    rows_part = jnp.concatenate([of_image(mh_refs, 2 * pair + k) for k in range(2)], axis=0)
    mixed = jnp.concatenate([rows_part, whole[...]], axis=1).astype(BF16)
    x_in = x_ref[0].astype(F32) * mask
    x_mid = x_in + dot(mixed, pw_ref[...]) + vectors[2:3]
    unit, inverse = norm_parts(x_mid)
    normed = (unit * gain_ref[...] + bias_ref[...]).astype(BF16)
    grad_result = cot_ref[0].astype(F32) * mask
    grad_low = grad_result.astype(BF16)
    normed_t = normed.T
    grad_t = grad_low.T

    total = x_mid + vectors[3:4]
    grad_normed = jnp.zeros_like(x_mid)

    def chunk_start(j):
        base = (j // 2) * 4 * LATE
        at = base + (j % 2) * CHUNK
        w1, w2 = late_ref[at : at + CHUNK], late_ref[at + 2 * CHUNK : at + 3 * CHUNK]
        rows = late_ref[base + GRAD_ROWS : base + GRAD_ROWS + 16].astype(F32)
        pre = dot(normed, w1) + rows[j % 2 : j % 2 + 1]
        return w1, w2, pre, dot_nt(grad_low, w2)

    ahead = chunk_start(0)
    for j in range(4):
        w1, w2, pre, grad_hidden = ahead
        if j < 3:
            ahead = chunk_start(j + 1)
        holder, cut = j // 2, (j % 2) * CHUNK
        bell = jnp.exp2(pre * pre * (-0.5 * LOG2E))
        below = 0.5 + 0.5 * lax.erf(pre * ROOT_HALF)
        hidden = (pre * below).astype(BF16)
        slope = below + pre * bell * DENSITY
        grad_pre = (grad_hidden * slope).astype(BF16)
        total = total + dot(hidden, w2)
        grad_normed = grad_normed + dot_nt(grad_pre, w1)
        acc_ref[holder, cut : cut + CHUNK] += dot(normed_t, grad_pre)
        acc_ref[holder, cut + 2 * CHUNK : cut + 3 * CHUNK] += dot(grad_t, hidden)
        small_ref[4 + j : 5 + j] += jnp.sum(grad_pre.astype(F32), 0, keepdims=True)
    out_ref[0] = (mask * total).astype(BF16)
    grad_mid = grad_result + norm_back(grad_normed, unit, inverse, gain_ref[...])
    gmid_ref[0] = grad_mid
    small_ref[0:1] += jnp.sum(grad_normed * unit, 0, keepdims=True)
    small_ref[1:2] += jnp.sum(grad_normed, 0, keepdims=True)
    small_ref[2:3] += jnp.sum(grad_mid, 0, keepdims=True)
    small_ref[3:4] += jnp.sum(grad_result, 0, keepdims=True)
    mid_low = grad_mid.astype(BF16)
    grad_proj = dot_tn(mixed, mid_low)
    for b in range(2):
        at = 4 * CHUNK + b * half
        acc_ref[0, at : at + half] += grad_proj[b * BR : b * BR + half]
        acc_ref[1, at : at + half] += grad_proj[b * BR + half : (b + 1) * BR]
    grad_mixed = dot_nt(mid_low, pw_ref[...])
    gh_ref[0] = grad_mixed[:WIN, :BR].astype(BF16)
    gh_ref[1] = grad_mixed[WIN:, :BR].astype(BF16)
    whole[...] = grad_mixed[:, BR:]
    split_columns(whole, left, right)
    gk_ref[0] = jnp.where(first_half, left[...], right[...]).astype(BF16)
    gs_ref[0] = pltpu.roll(jnp.where(first_half, right[...], left[...]), half, 1).astype(BF16)

    @pl.when(step == 2 * images - 1)
    def _():
        for s in range(2):
            for j in range(2, 4):
                cut = slice(j * CHUNK, (j + 1) * CHUNK)
                acc_ref[s, cut] = acc_ref[s, cut].T
        core, along = core_place(info), along_place(info)
        rows = GRAD_ROWS // 4
        for s in range(2):
            for near in range(2):
                side = along if near == 0 else 1 - along
                mine = pl.multiple_of((2 * core + side) * rows, 8)
                theirs = pl.multiple_of((2 * (1 - core) + side) * rows, 8)
                kept_ref[s, near] = acc_ref[s, pl.ds(mine, rows)].astype(BF16)
                sent_ref[s, near] = acc_ref[s, pl.ds(theirs, rows)].astype(BF16)


def backward_sums(rows, unit, acc_ref, sum_ref):
    acc_ref[...] += dot_tn(unit, rows)
    sum_ref[0:1] += jnp.sum(rows.astype(F32), 0, keepdims=True)


def columns_backward_kernel(
    image, heights, info, gk_ref, gr_ref, p_ref, q_ref, k_ref, v_ref, o_ref, rl_ref, n_ref, wt_ref,
    taps_ref, acc_ref, sum_ref, lepe_ref, keep_ref, send_ref,
    grad_ref, out_ref, kb_ref, vb_ref, ds_ref, pad_ref,
):
    step = pl.program_id(0)
    place = tensor_place(info)
    height, width = sides(image, heights, info)

    @pl.when(step == 0)
    def _():
        set_indicator(vb_ref)
        pad_ref[...] = jnp.zeros_like(pad_ref)
        acc_ref[...] = jnp.zeros_like(acc_ref)
        sum_ref[...] = jnp.zeros_like(sum_ref)
        lepe_ref[...] = jnp.zeros_like(lepe_ref)
        for source, side in ((gk_ref, place), (gr_ref, 1 - place)):
            for s in range(2):
                start = pl.multiple_of(side * PAIR + s * WIN, 8)
                grad_ref[pl.ds(start, WIN)] = source[s].astype(F32)

    refs = (p_ref, q_ref, k_ref, v_ref, o_ref, rl_ref, kb_ref, vb_ref, ds_ref, pad_ref)
    first = 2 * step
    columns = [(first + k) * STRIPE for k in range(2)]
    grads = [
        jnp.concatenate([grad_ref[pl.ds(column + q, PH, stride=HALF)] for q in range(STRIPE)], axis=0)
        for column in columns
    ]
    products = window_pair_back(grads, first, refs)
    for k in range(2):
        column = columns[k]
        rows, tap_rows = window_rows_back(
            grads[k], products[k], place * HALF + column, width, height, taps_ref[1, :9], first, k, refs
        )
        for index, item in enumerate(tap_rows):
            lepe_ref[index : index + 1] += item
        backward_sums(rows, n_ref[2 * step + k], acc_ref, sum_ref)
        back = dot(rows, wt_ref[1])
        for q in range(STRIPE):
            cut = slice(q * PH, (q + 1) * PH)
            out_ref[0, pl.ds(column + q, PH, stride=HALF)] = back[cut, :BR]
            out_ref[1, pl.ds(column + q, PH, stride=HALF)] = back[cut, BR:]

    @pl.when(step == 1)
    def _():
        for s in range(2):
            keep = pl.multiple_of(place * PAIR + s * WIN, 8)
            send = pl.multiple_of((1 - place) * PAIR + s * WIN, 8)
            for j in range(2):
                lanes = slice(j * BR, (j + 1) * BR)
                keep_ref[s, :, lanes] = out_ref[j, pl.ds(keep, WIN)].astype(BF16)
                send_ref[s, :, lanes] = out_ref[j, pl.ds(send, WIN)].astype(BF16)


def direction_grads(acc, sums, gain, bias, weight_t):
    moved = acc.T
    shift = sums[0:1]
    high = shift.astype(BF16)
    low = (shift - high.astype(F32)).astype(BF16)
    wide = dot(high, weight_t) + dot(low, weight_t)
    column = sums.T[:, 0:1]
    grad_qkv = moved * gain + column * bias
    grad_gain = jnp.sum(weight_t.astype(F32) * moved, 0, keepdims=True)
    return grad_qkv, grad_gain, wide


def rows_backward_kernel(image, start, count, last, others, *refs):
    (
        heights, info, x_ref, gm_ref, p_ref, q_ref, k_ref, v_ref, o_ref, rl_ref, wt_ref, taps_ref,
    ) = refs[:12]
    refs = refs[12:]
    if last:
        gain_ref, bias_ref, small2_ref = refs[:3]
        other_refs = refs[3 : 3 + 3 * sum(others)]
        refs = refs[3 + 3 * sum(others) :]
        gp_ref, kept_ref, sent_ref = refs[:3]
        acc_ref, sum_ref, lepe_ref, pack_ref, kb_ref, vb_ref, ds_ref, pad_ref = refs[3:]
    else:
        gp_ref, acc_ref, sum_ref, lepe_ref, kb_ref, vb_ref, ds_ref, pad_ref = refs
    step = pl.program_id(0)
    pair = start + step
    height, width = sides(image, heights, info)
    row_base = tensor_place(info) * HALF + pair * 2 * STRIPE

    @pl.when(step == 0)
    def _():
        set_indicator(vb_ref)
        pad_ref[...] = jnp.zeros_like(pad_ref)
        acc_ref[...] = jnp.zeros_like(acc_ref)
        sum_ref[...] = jnp.zeros_like(sum_ref)
        lepe_ref[...] = jnp.zeros_like(lepe_ref)

    mask = twice(as_float(inside(split_index(PAIR, PW, BR), row_base, 0, height, width)))
    unit, _ = norm_parts(x_ref[0].astype(F32) * mask)
    refs = (p_ref, q_ref, k_ref, v_ref, o_ref, rl_ref, kb_ref, vb_ref, ds_ref, pad_ref)
    first_window = 2 * pair
    grads = [gm_ref[k].astype(F32) for k in range(2)]
    products = window_pair_back(grads, first_window, refs)
    for k in range(2):
        base = row_base + k * STRIPE
        rows, tap_rows = window_rows_back(
            grads[k], products[k], base, height, width, taps_ref[0, :9], first_window, k, refs
        )
        for index, item in enumerate(tap_rows):
            lepe_ref[index : index + 1] += item
        gp_ref[k] = rows
        backward_sums(rows, unit[k * WIN : (k + 1) * WIN].astype(BF16), acc_ref, sum_ref)
    if last:

        @pl.when(step == count - 1)
        def _():
            row_items = [acc_ref[...], sum_ref[...], lepe_ref[...]]
            column_items = [0.0, 0.0, 0.0]
            for at in range(sum(others)):
                kind = other_refs[3 * at : 3 * at + 3]
                if at < others[0]:
                    row_items = [old + ref[...] for old, ref in zip(row_items, kind)]
                else:
                    column_items = [old + ref[...] for old, ref in zip(column_items, kind)]
            gain, bias = gain_ref[...], bias_ref[...]
            grad_gain = grad_bias = 0.0
            half = BR // 2
            for direction, items in enumerate((row_items, column_items)):
                grad_qkv, gain_row, bias_row = direction_grads(
                    items[0], items[1], gain, bias, wt_ref[direction]
                )
                grad_gain = grad_gain + gain_row
                grad_bias = grad_bias + bias_row
                for s in range(2):
                    for item in range(3):
                        at = direction * 3 * half + item * half
                        take = item * BR + s * half
                        pack_ref[s, at : at + half] = grad_qkv[take : take + half]
            small2 = small2_ref[...]
            for s in range(2):
                cut = slice(s * half, (s + 1) * half)
                lepe = jnp.concatenate(
                    [row_items[2][:, cut], column_items[2][:, cut], jnp.zeros((16, BR), F32)], axis=1
                )
                head = jnp.concatenate(
                    [grad_gain, grad_bias, small2[:4], small2[4 + 2 * s : 6 + 2 * s]], axis=0
                )
                pack_ref[s, SMALL_AT : SMALL_AT + 8] = head
                pack_ref[s, SMALL_AT + 8 : SMALL_AT + 24] = lepe
                pack_ref[s, SMALL_AT + 24 :] = jnp.zeros((LAST_ROWS - SMALL_AT - 24, 2 * BR), F32)
            core = core_place(info)
            rows = LAST_ROWS // 2
            for s in range(2):
                mine = pl.multiple_of(core * rows, 8)
                theirs = pl.multiple_of((1 - core) * rows, 8)
                kept_ref[s] = pack_ref[s, pl.ds(mine, rows)].astype(BF16)
                sent_ref[s] = pack_ref[s, pl.ds(theirs, rows)].astype(BF16)


def input_kernel(image, start, first, *refs):
    heights, info, x_ref, gp_ref, gmid_ref, vk_ref, vr_ref, wt_ref, gain_ref = refs[:9]
    refs = refs[9:] if first else refs[10:]
    out_ref, mark_ref, whole, left, right = refs
    mark_ref[...] = jnp.zeros_like(mark_ref)
    pair = start + pl.program_id(0)
    place = tensor_place(info)
    height, width = sides(image, heights, info)
    row_base = place * HALF + pair * 2 * STRIPE
    mask = twice(as_float(inside(split_index(PAIR, PW, BR), row_base, 0, height, width)))
    unit, inverse = norm_parts(x_ref[0].astype(F32) * mask)
    first_half = place == 0
    own = vk_ref[0].astype(F32)
    other = vr_ref[0].astype(F32)
    left[...] = jnp.where(first_half, own, other)
    right[...] = jnp.where(first_half, other, own)
    merge_columns(left, right, whole)
    parts = [dot(gp_ref[k], wt_ref[0]) for k in range(2)]
    grad_normed = jnp.concatenate(parts, axis=0) + whole[...]
    back = norm_back(grad_normed, unit, inverse, gain_ref[...])
    out_ref[0] = (mask * (gmid_ref[0] + back)).astype(BF16)


def unpack_first_kernel(info, a_ref, ax_ref, b_ref, bx_ref, fc1_ref, fc2_ref, proj_ref, mark_ref):
    mark_ref[...] = jnp.zeros_like(mark_ref)
    core, along = core_place(info) == 0, along_place(info) == 0
    quarters = []
    for c in range(2):
        for side in range(2):
            here = core if c == 0 else jnp.logical_not(core)
            near = along if side == 0 else jnp.logical_not(along)
            mine = jnp.where(near, a_ref[...].astype(F32), ax_ref[...].astype(F32))
            theirs = jnp.where(near, b_ref[...].astype(F32), bx_ref[...].astype(F32))
            quarters.append(jnp.where(here, mine, theirs))
    total = jnp.concatenate(quarters, axis=0)
    fc1_ref[:, :CHUNK] = total[:CHUNK]
    fc1_ref[:, CHUNK:] = total[CHUNK : 2 * CHUNK]
    fc2_ref[...] = total[2 * CHUNK : 4 * CHUNK]
    proj_ref[...] = total[4 * CHUNK :]


def unpack_last_kernel(
    info, c_ref, cx_ref, qkv_ref, lepe_ref, shift_ref, b1_ref,
    gain1_ref, bias1_ref, gain2_ref, bias2_ref, projb_ref, b2_ref,
):
    core = core_place(info) == 0
    mine, theirs = c_ref[...].astype(F32), cx_ref[...].astype(F32)
    last = jnp.concatenate([jnp.where(core, mine, theirs), jnp.where(core, theirs, mine)], axis=0)
    half = BR // 2
    for direction in range(2):
        for item in range(3):
            at = direction * 3 * half + item * half
            qkv_ref[item, direction] = last[at : at + half]
    small = last[SMALL_AT : SMALL_AT + 24]
    for row, ref in enumerate((gain1_ref, bias1_ref, gain2_ref, bias2_ref, projb_ref, b2_ref)):
        ref[...] = small[row : row + 1]
    for part in range(4):
        b1_ref[part : part + 1] = small[6 + part // 2 : 7 + part // 2, part % 2 * BR : (part % 2 + 1) * BR]
    for tap in range(9):
        turned = 8 + 3 * (tap % 3) + tap // 3
        lepe_ref[tap, 0:1] = small[8 + tap : 9 + tap, :half]
        lepe_ref[tap, 1:2] = small[turned : turned + 1, half : 2 * half]
    shift_ref[0:1] = small[17:18, :half]
    shift_ref[1:2] = small[17:18, half : 2 * half]


def spec(shape, index=None):
    if index is None:
        return pl.BlockSpec(shape, lambda i: (0,) * len(shape))
    return pl.BlockSpec(shape, index)


def shaped(shape, dtype):
    return jax.ShapeDtypeStruct(shape, dtype)


SCALARS = pl.BlockSpec(memory_space=pltpu.SMEM)
RESIDENT = pl.BlockSpec(memory_space=pltpu.VMEM)


def call(
    kernel, name, grid, in_specs, out_specs, out_shape, scratch, micros, limit, aliases=None, marks=0
):
    known = len(in_specs)

    def body(*refs):
        kernel(*refs[:known], *refs[known + marks :])

    in_specs = list(in_specs) + [pl.BlockSpec(memory_space=pl.ANY)] * marks
    return pl.pallas_call(
        body,
        name=name,
        grid=(grid,),
        in_specs=in_specs,
        out_specs=out_specs,
        out_shape=out_shape,
        scratch_shapes=scratch,
        input_output_aliases=aliases or {},
        cost_estimate=pl.CostEstimate(
            flops=int(micros * FLOPS_PER_MICRO), bytes_accessed=0, transcendentals=0
        ),
        compiler_params=pltpu.CompilerParams(
            vmem_limit_bytes=limit * MIB, dimension_semantics=("arbitrary",)
        ),
    )


def kept_shapes(count):
    return [pltpu.VMEM((count, WIN, WIDE), BF16)] + [
        pltpu.VMEM((count, WIN, BR), BF16) for _ in range(3)
    ] + [pltpu.VMEM((count, WIN, BR), F32) for _ in range(2)]


def resident(arrays):
    return [pltpu.with_memory_space_constraint(item, pltpu.VMEM) for item in arrays]


def in_hbm(arrays):
    return [pltpu.with_memory_space_constraint(item, pltpu.HBM) for item in arrays]


def forward_scratch():
    return [
        pltpu.VMEM((2, WIDE, BR), BF16),
        pltpu.VMEM((2, WIDE, 2 * BR), BF16),
        pltpu.VMEM((2, WIN, BR), F32),
        pltpu.VMEM((2, WIN, BR), F32),
        pltpu.VMEM((WIN, WIDE), F32),
        pltpu.VMEM((2, PAD_ROWS, BR), F32),
    ]


def backward_scratch():
    return [
        pltpu.VMEM((2, WIDE, BR), BF16),
        pltpu.VMEM((2, WIDE, 2 * BR), BF16),
        pltpu.VMEM((2, WIN, WIDE), BF16),
        pltpu.VMEM((4, PAD_ROWS, BR), F32),
    ]


FLOPS_PER_MICRO = 1.15e9
ATTENTION_LIMIT = 15
MLP_LIMIT = 18


def pack_first(qkv, lepe, shift):
    width = qkv.shape[-1]
    return call(
        pack_kernel, "pack", 1, [spec(qkv.shape), spec(lepe.shape), spec(shift.shape)],
        [spec((2 * FIRST_HALF, width)), spec((FIRST_HALF, width))],
        [shaped((2 * FIRST_HALF, width), BF16), shaped((FIRST_HALF, width), BF16)], [], 1, 8,
    )(*in_hbm([qkv, lepe, shift]))


def pack_late(info, w1, w2, proj, vectors):
    width = w2.shape[1]
    rows = 4 * LATE
    return call(
        late_pack_kernel, "pack_late", 1,
        [SCALARS, spec(w1.shape), spec(w2.shape), spec(proj.shape)] + [spec(v.shape) for v in vectors],
        [spec((rows, width)), spec((LATE, width))],
        [shaped((rows, width), BF16), shaped((LATE, width), BF16)], [], 1, 8,
    )(info, w1, w2, proj, *vectors)


def split_quadrants(info, x_pairs):
    count, _, width = x_pairs.shape
    images = count // 2
    block = (1, WIN, width)

    def clamp(image):
        return lambda i: (jnp.clip(i - 2 * image, 0, 1), 0, 0)

    return call(
        partial(quadrant_kernel, images), "quadrants", count,
        [SCALARS, spec((1, PAIR, width), lambda i: (i, 0, 0))],
        [spec(block, lambda i: (i, 0, 0))] + [spec(block, clamp(image)) for image in range(images)],
        [shaped((count, WIN, width), BF16)] + [shaped((2, WIN, width), BF16)] * images,
        [pltpu.VMEM((PAIR, width), F32), pltpu.VMEM((WIN, width), F32), pltpu.VMEM((WIN, width), F32)],
        2, 16,
    )(info, x_pairs)


def rows_forward(image, heights, info, x_pairs, gain, bias, packs, known):
    count, _, width = x_pairs.shape
    pair = spec((1, PAIR, width), lambda i: (2 * image + i, 0, 0))
    in_specs = [SCALARS, SCALARS, pair, spec((1, width)), spec((1, width))]
    operands = [heights, info, x_pairs, gain, bias]
    out_shapes = kept_shapes(4) + [pltpu.VMEM((4, WIN, BR), BF16)]
    scratch = forward_scratch()
    if known is None:
        in_specs += [spec(item.shape) for item in packs]
        operands += list(packs)
        scratch = [pltpu.VMEM((2 * FIRST_HALF, width), BF16)] + scratch
        out_shapes += [
            pltpu.VMEM((2, width, 3 * BR), BF16), pltpu.VMEM((2, 3 * BR, width), BF16),
            pltpu.VMEM((2, 16, BR), F32),
        ]
    else:
        in_specs += [RESIDENT] * 2
        operands += resident(known)
    return call(
        partial(rows_forward_kernel, image, known is None), "rows_forward", 2, in_specs,
        [RESIDENT] * len(out_shapes), out_shapes, scratch,
        6.5, ATTENTION_LIMIT,
    )(*operands)


def columns_forward(image, heights, info, own, other, gain, bias, weight, taps):
    width = own.shape[2]
    fixed = spec((2, WIN, BR), lambda i: (0, 0, 0))
    return call(
        partial(columns_forward_kernel, image), "columns_forward", 2,
        [
            SCALARS, SCALARS, spec((2, WIN, width), lambda i: (image, 0, 0)), spec((2, WIN, width)),
            spec((1, width)), spec((1, width)), RESIDENT, RESIDENT,
        ],
        [RESIDENT] * 7 + [fixed, fixed],
        kept_shapes(4) + [pltpu.VMEM((4, WIN, width), BF16)] + [shaped((2, WIN, BR), BF16)] * 2,
        [pltpu.VMEM((2, 2 * PAIR, BR), F32), pltpu.VMEM((2 * PAIR, BR), F32)] + forward_scratch(),
        6.5, ATTENTION_LIMIT,
    )(heights, info, own, other, gain, bias, *resident([weight, taps]))


def mlp(heights, info, x_pairs, cot_pairs, mixed_rows, mixed_own, mixed_other, gain, bias, late):
    count, _, width = x_pairs.shape
    images = count // 2
    pair = spec((1, PAIR, width), lambda i: (i, 0, 0))
    part = spec((1, WIN, BR), lambda i: (i, 0, 0))
    row = spec((1, width))
    quarter = (2, 2, GRAD_ROWS // 4, width)
    return call(
        partial(mlp_kernel, images), "feed_forward", count,
        [SCALARS, SCALARS, pair, pair] + [RESIDENT] * (3 * images) + [row, row] + [RESIDENT] * 5,
        [
            pair, pair, spec((2, WIN, BR), lambda i: (i, 0, 0)), part, part, spec((8, width)),
            spec(quarter), spec(quarter),
        ],
        [
            shaped(x_pairs.shape, BF16), shaped(x_pairs.shape, F32), shaped((2 * count, WIN, BR), BF16),
            shaped((count, WIN, BR), BF16), shaped((count, WIN, BR), BF16), shaped((8, width), F32),
            shaped(quarter, BF16), shaped(quarter, BF16),
        ],
        [
            pltpu.VMEM((2, GRAD_ROWS, width), F32),
            pltpu.VMEM((2 * BR, width), BF16), pltpu.VMEM((8 * LATE, width), BF16),
            pltpu.VMEM((PAIR, BR), F32), pltpu.VMEM((WIN, BR), F32), pltpu.VMEM((WIN, BR), F32),
        ],
        24, MLP_LIMIT,
    )(
        heights, info, x_pairs, cot_pairs, *resident([*mixed_rows, *mixed_own, *mixed_other]), gain, bias,
        *resident(late),
    )


def columns_backward(image, heights, info, grad_own, grad_other, kept, unit, weight_t, taps):
    width = weight_t.shape[2]
    fixed = spec((2, WIN, width))
    grads = spec((2, WIN, BR), lambda i: (image, 0, 0))
    return call(
        partial(columns_backward_kernel, image), "columns_backward", 2,
        [SCALARS, SCALARS, grads, grads] + [RESIDENT] * 9,
        [spec((width, 3 * BR)), spec((8, 3 * BR)), spec((16, BR)), fixed, fixed],
        [shaped((width, 3 * BR), F32), shaped((8, 3 * BR), F32), shaped((16, BR), F32)]
        + [shaped((2, WIN, width), BF16)] * 2,
        [pltpu.VMEM((2 * PAIR, BR), F32), pltpu.VMEM((2, 2 * PAIR, BR), F32)] + backward_scratch(),
        9.7, ATTENTION_LIMIT,
    )(heights, info, grad_own, grad_other, *resident([*kept, unit, weight_t, taps]))


def rows_backward(image, start, count, heights, info, x_pairs, grad_mixed, kept, weight_t, taps, final):
    width = weight_t.shape[2]
    at = 2 * image + start
    pair = spec((1, PAIR, width), lambda i: (at + i, 0, 0))
    in_specs = [SCALARS, SCALARS, pair, spec((2, WIN, BR), lambda i: (at + i, 0, 0))] + [RESIDENT] * 8
    operands = [heights, info, x_pairs, grad_mixed, *resident([*kept, weight_t, taps])]
    sum_shapes = [(width, 3 * BR), (8, 3 * BR), (16, BR)]
    out_specs = [spec((2, WIN, 3 * BR), lambda i: (i, 0, 0))]
    out_shapes = [shaped((2 * count, WIN, 3 * BR), BF16)]
    scratch = backward_scratch()
    others = (0, 0)
    if final is None:
        out_specs += [spec(shape) for shape in sum_shapes]
        out_shapes += [shaped(shape, F32) for shape in sum_shapes]
    else:
        gain, bias, small2, row_items, column_items = final
        others = (len(row_items), len(column_items))
        in_specs += [spec((1, width)), spec((1, width)), spec((8, width))]
        operands += [gain, bias, small2]
        for item in [*row_items, *column_items]:
            in_specs += [spec(shape) for shape in sum_shapes]
            operands += list(item)
        half = (2, LAST_ROWS // 2, width)
        out_specs += [spec(half), spec(half)]
        out_shapes += [shaped(half, BF16), shaped(half, BF16)]
        scratch = (
            [pltpu.VMEM(shape, F32) for shape in sum_shapes]
            + [pltpu.VMEM((2, LAST_ROWS, width), F32)]
            + scratch
        )
    return call(
        partial(rows_backward_kernel, image, start, count, final is not None, others), "rows_backward",
        count, in_specs, out_specs, out_shapes, scratch, 4.8 * count, ATTENTION_LIMIT,
    )(*operands)


def input_rows(
    image, start, count, heights, info, x_pairs, rows, grad_mid, back_own, back_other, weight_t, gain,
    previous,
):
    width = weight_t.shape[2]
    pair = spec((1, PAIR, width), lambda i: (2 * image + start + i, 0, 0))
    part = spec((1, WIN, width), lambda i: (start + i, 0, 0))
    in_specs = [
        SCALARS, SCALARS, pair, spec((2, WIN, 3 * BR), lambda i: (start + i, 0, 0)), pair, part, part,
        RESIDENT, spec((1, width)),
    ]
    operands = [
        heights, info, x_pairs, rows, grad_mid, back_own, back_other, *resident([weight_t]), gain,
    ]
    aliases = {}
    if previous is not None:
        in_specs.append(pl.BlockSpec(memory_space=pl.ANY))
        operands.append(previous)
        aliases = {len(operands) - 1: 0}
    return call(
        partial(input_kernel, image, start, previous is None), "input_rows", count, in_specs,
        [pair, spec((8, 128))], [shaped(x_pairs.shape, BF16), shaped((8, 128), F32)],
        [pltpu.VMEM((PAIR, width), F32), pltpu.VMEM((WIN, width), F32), pltpu.VMEM((WIN, width), F32)],
        1.6 * count, 20, aliases,
    )(*operands)


def unpack_first(info, a, ax, b, bx, hidden, width):
    return call(
        unpack_first_kernel, "unpack_first", 1, [SCALARS] + [spec(a.shape)] * 4,
        [spec((width, hidden)), spec((hidden, width)), spec((BR, width)), spec((8, 128))],
        [
            shaped((width, hidden), F32), shaped((hidden, width), F32), shaped((BR, width), F32),
            shaped((8, 128), F32),
        ],
        [], 1, 16,
    )(info, a, ax, b, bx)


def unpack_last(info, c, cx, width):
    row = spec((1, width))
    return call(
        unpack_last_kernel, "unpack_last", 1, [SCALARS] + [spec(c.shape)] * 2,
        [
            spec((3, 2, BR // 2, width)), spec((9, 2, BR // 2)), spec((2, BR // 2)), spec((4, BR)),
            row, row, row, row, row, row,
        ],
        [
            shaped((3, 2, BR // 2, width), F32), shaped((9, 2, BR // 2), F32), shaped((2, BR // 2), F32),
            shaped((4, BR), F32),
        ] + [shaped((1, width), F32)] * 6,
        [], 1, 16,
    )(info, c, cx)


def after(value, *marks):
    return lax.optimization_barrier((value,) + marks)[0]


def swap_tensor(values):
    return lax.ppermute(values, "tensor", [(0, 1), (1, 0)])


def swap_dp(values, size, mask):
    return lax.ppermute(values, "dp", [(i, i ^ mask) for i in range(size)])


def swap_both(values, size, mask):
    pairs = [(2 * i + t, 2 * (i ^ mask) + 1 - t) for i in range(size) for t in range(2)]
    return lax.ppermute(values, ("dp", "tensor"), pairs)


def add_kernel(count, *refs):
    refs, outs = refs[:count], refs[count:]
    items = [ref[...].astype(F32) for ref in refs]
    while len(items) > 1:
        items = [items[i] + items[i + 1] for i in range(0, len(items), 2)]
    whole = items[0].astype(BF16)
    whole = whole.reshape((len(outs),) + outs[0].shape)
    for at, out in enumerate(outs):
        out[...] = whole[at]


def added(*items, parts=1, marks=()):
    shape = items[0].shape
    last = shape[-2:]
    outs = call(
        partial(add_kernel, len(items)), "add", 1, [spec(shape)] * len(items), [spec(last)] * parts,
        [shaped(last, BF16)] * parts, [], 0.5, 8, marks=len(marks),
    )(*items, *marks)
    return outs[0] if parts == 1 else outs


def partner_groups(size):
    bits = list(range(1, size.bit_length() - 1))
    groups = []
    while bits:
        pair, bits = bits[:2], bits[2:]
        low = 1 << pair[0]
        groups.append([low] if len(pair) == 1 else [low, 1 << pair[1], low | (1 << pair[1])])
    return groups


def per_device(
    size, block_input, heights, widths, norm1_gain, norm1_bias, qkv_weight, lepe_weight, lepe_bias,
    proj_weight, proj_bias, norm2_gain, norm2_bias, fc1_weight, fc1_bias, fc2_weight, fc2_bias,
    cotangent,
):
    images, local_cells, width = block_input.shape
    hidden = fc1_weight.shape[1]
    x_pairs = block_input.reshape(2 * images, PAIR, width)
    cot_pairs = cotangent.reshape(2 * images, PAIR, width)
    gain1, bias1 = norm1_gain[None], norm1_bias[None]
    pairs = range(images)
    index = lax.axis_index("dp")
    places = jnp.stack([lax.axis_index("tensor"), index % 2, index // 2 % 2]).astype(jnp.int32)
    info = jnp.concatenate([widths, places])

    own, own_half = pack_first(
        qkv_weight.transpose(1, 2, 3, 0), lepe_weight.transpose(1, 0, 2), lepe_bias
    )
    near = swap_tensor(own_half)
    far = swap_dp(near, size, 1)
    quad_own, *quad_send = split_quadrants(info, after(x_pairs, own))
    vectors = (fc1_bias, proj_bias, fc2_bias)
    late_own, late_send = pack_late(info, *after((fc1_weight, fc2_weight, proj_weight, vectors), quad_own))
    quad_other = [swap_tensor(quad_send[0])]

    late_near = swap_tensor(late_send)

    def forward_rows(image, mark, known):
        return rows_forward(
            image, after(heights, mark), info, x_pairs, gain1, bias1, (own, near, far), known
        )

    *kept, mixed, weight, weight_t, taps = forward_rows(0, late_own, None)
    row_kept, mixed_rows = [kept], [mixed]
    quad_other += [swap_tensor(after(item, taps)) for item in quad_send[1:]]
    columns = []
    for image in pairs:
        *kept, unit, keep, send = columns_forward(
            image, heights, info, quad_own, quad_other[image], gain1, bias1, weight, taps
        )
        columns.append((kept, unit, keep, swap_tensor(send)))
        if image == 0:
            ready = after(late_near, keep)
            late_parts = [ready] + [swap_dp(ready, size, mask) for mask in (2, 1, 3)]
    for image in range(1, images):
        *kept, mixed = forward_rows(image, columns[-1][2], (weight, taps))
        row_kept.append(kept)
        mixed_rows.append(mixed)
    output, grad_mid, grad_rows, grad_keep, grad_send, small2, kept1, sent1 = mlp(
        heights, info, x_pairs, cot_pairs, mixed_rows, [item[2] for item in columns],
        [item[3] for item in columns], norm2_gain[None], norm2_bias[None], (late_own, *late_parts),
    )
    grad_other = swap_tensor(grad_send)

    arrived = swap_dp(sent1, size, 1)
    bits = size.bit_length() - 1
    row_pairs, row_sums = [], []

    def backward_rows(image, start, count, mark, final=None):
        rows, *rest = rows_backward(
            image, start, count, after(heights, mark), info, x_pairs, grad_rows, row_kept[image],
            weight_t, taps, final,
        )
        row_pairs.append(rows)
        return rest

    for image in range(images - 1):
        row_sums.append(backward_rows(image, 0, 2, small2))
    mark = row_sums[-1][2] if row_sums else small2
    first, toward_x, toward_y, toward_xy = added(kept1, after(arrived, mark), parts=4)
    crossed = [swap_dp(toward_x, size, 2), swap_tensor(toward_y), swap_both(toward_xy, size, 2)]
    mark = first
    column_back = []
    for image in pairs:
        kept, unit, _, _ = columns[image]
        *column_sums, back_keep, back_send = columns_backward(
            image, after(heights, mark), info, grad_keep, grad_other, kept, unit, weight_t, taps
        )
        column_back.append((column_sums, back_keep, swap_tensor(back_send)))
        mark = column_sums[2]
        if image == 0:
            first = added(first, *[after(item, mark) for item in crossed])
        else:
            first = added(first, after(arrived, mark))
        bit = 2 + image
        arrived = swap_dp(first, size, 1 << bit) if bit < bits else jnp.zeros_like(first)
        mark = first
    final = (gain1, bias1, small2, row_sums, [item[0] for item in column_back])
    kept2, sent2 = backward_rows(images - 1, 0, 2, mark, final)

    input_grad = None

    def meanwhile(image, start, count, mark):
        nonlocal input_grad
        _, back_keep, back_other = column_back[image]
        input_grad, mark = input_rows(
            image, start, count, after(heights, mark), info, x_pairs, row_pairs[image], grad_mid,
            back_keep, back_other, weight_t, gain1, input_grad,
        )
        return mark

    first = added(first, arrived, marks=[kept2])
    core_part = swap_dp(after(sent2, first), size, 1)
    last, toward_y = added(kept2, core_part, parts=2, marks=[item[2] for item in column_back])
    for bit in range(2 + images, bits):
        first = added(first, swap_dp(first, size, 1 << bit))
    first_x = swap_dp(first, size, 2)
    across = swap_tensor(toward_y)
    for image in range(images - 1):
        mark = meanwhile(image, 0, 2, last)
    last = added(last, across, marks=[mark])
    for at, group in enumerate(partner_groups(size)):
        arrived = [swap_dp(last, size, mask) for mask in group]
        marks = []
        if at == 0:
            marks = [meanwhile(images - 1, 0, 1, last), first_x]
        if at == 1:
            first_core = [swap_dp(after(item, last), size, 1) for item in (first, first_x)]
            grad_fc1, grad_fc2, grad_proj, mark = unpack_first(
                after(info, last), first, first_x, first_core[0], first_core[1], hidden, width
            )
            marks = [meanwhile(images - 1, 1, 1, last), mark]
        last = added(last, *arrived, marks=marks)
    last_other = swap_dp(last, size, 1)
    (
        grad_qkv, grad_lepe, grad_shift, grad_b1,
        grad_gain1, grad_bias1, grad_gain2, grad_bias2, grad_projb, grad_b2,
    ) = unpack_last(info, last, last_other, width)
    return (
        output.reshape(block_input.shape), input_grad.reshape(block_input.shape),
        grad_gain1[0], grad_bias1[0], grad_qkv.transpose(3, 0, 1, 2), grad_lepe.transpose(1, 0, 2),
        grad_shift, grad_proj.reshape(2, BR // 2, width), grad_projb[0], grad_gain2[0], grad_bias2[0],
        grad_fc1, grad_b1.reshape(-1), grad_fc2, grad_b2[0],
    )


def solution(mesh):
    placed = (
        P("dp", "tensor", None),
        P("dp"),
        P("dp"),
        P(),
        P(),
        P(None, None, None, "tensor"),
        P(None, None, "tensor"),
        P(None, "tensor"),
        P(None, "tensor", None),
        P(),
        P(),
        P(),
        P(None, "tensor"),
        P("tensor"),
        P("tensor", None),
        P(),
        P("dp", "tensor", None),
    )
    return jax.shard_map(
        partial(per_device, mesh.shape["dp"]),
        mesh=mesh,
        in_specs=placed,
        out_specs=(
            P("dp", "tensor", None),
            P("dp", "tensor", None),
            P(),
            P(),
            P(None, None, None, "tensor"),
            P(None, None, "tensor"),
            P(None, "tensor"),
            P(None, "tensor", None),
            P(),
            P(),
            P(),
            P(None, "tensor"),
            P("tensor"),
            P("tensor", None),
            P(),
        ),
        check_vma=False,
    )
```

```python
from functools import partial

import jax
import jax.numpy as jnp
from jax import lax
from jax.experimental import pallas as pl
from jax.experimental.pallas import tpu as pltpu
from jax.sharding import PartitionSpec as P

HEAD_DIM = 32
STRIPE = 7
PH = 56
PW = 56
HEADS = 4
BR = HEADS * HEAD_DIM
WIN = STRIPE * PW
WIDE = HEADS * WIN
MAIN = WIN // 128 * 128
REST = WIN - MAIN
GAP = 64
PAD_ROWS = STRIPE * GAP + 16
HALF = 28
PAIR = 2 * WIN
CHUNK = 256
CHUNKS = [(lo, min(lo + CHUNK, WIDE)) for lo in range(0, WIDE, CHUNK)]

MASKED_WEIGHT = 9.357622968840175e-14
EPSILON = 1e-05
LOG2E = 1.4426950408889634
ROOT_HALF = 0.7071067811865476
DENSITY = 0.3989422804014327
DEN_LOW = 2.0**-60
DEN_HIGH = 2.0**100

F32 = jnp.float32
BF16 = jnp.bfloat16
MIB = 2**20
GRAD_ROWS = 1152
LAST_ROWS = 416
SMALL_AT = 3 * BR
FIRST_HALF = 208
LATE = 304


def dot(a, b):
    return jnp.dot(a, b, preferred_element_type=F32)


def dot_nt(a, b):
    return lax.dot_general(a, b, (((1,), (1,)), ((), ())), preferred_element_type=F32)


def dot_tn(a, b):
    return lax.dot_general(a, b, (((0,), (0,)), ((), ())), preferred_element_type=F32)


def split_index(count, width, lanes, axis=0):
    shape = (count, lanes) if axis == 0 else (lanes, count)
    index = lax.broadcasted_iota(jnp.int32, shape, axis)
    step = -(-65536 // width)
    major = lax.shift_right_logical(index * step, 16)
    return major, index - major * width


def inside(parts, base_major, base_minor, lim_major, lim_minor):
    major, minor = parts
    return (major < lim_major - base_major) & (minor < lim_minor - base_minor)


def as_float(flag):
    return jnp.where(flag, 1.0, 0.0).astype(F32)


def twice(values):
    return jnp.concatenate([values, values], axis=1)


def head_lane(head):
    lane = lax.broadcasted_iota(jnp.int32, (1, BR), 1)
    return as_float((lane >= head * HEAD_DIM) & (lane < (head + 1) * HEAD_DIM))


def head_blocks(values):
    lanes = [head_lane(head) for head in range(HEADS)]
    top = [values[:MAIN] * lane for lane in lanes]
    rest = [values[MAIN:] * lane for lane in lanes]
    return jnp.concatenate(top + rest, axis=0)


def from_wide(values):
    rows = []
    for head in range(HEADS):
        own = values[head * HEAD_DIM : (head + 1) * HEAD_DIM]
        rest = HEADS * MAIN + head * REST
        rows.append(
            jnp.concatenate(
                [own[:, head * MAIN : (head + 1) * MAIN], own[:, rest : rest + REST]], axis=1
            )
        )
    return jnp.concatenate(rows, axis=0)


def norm_parts(values):
    centred = values - jnp.mean(values, -1, keepdims=True)
    inverse = lax.rsqrt(jnp.mean(centred * centred, -1, keepdims=True) + EPSILON)
    return centred * inverse, inverse


def norm_back(grad_rows, unit_rows, inverse, gain):
    scaled = grad_rows * gain
    return inverse * (
        scaled
        - jnp.mean(scaled, -1, keepdims=True)
        - unit_rows * jnp.mean(scaled * unit_rows, -1, keepdims=True)
    )


def spread(pad_ref, values):
    for row in range(STRIPE):
        pad_ref[8 + GAP * row : 8 + GAP * row + PW] = values[row * PW : (row + 1) * PW]


def neighbours(pad_ref):
    return [
        [pad_ref[8 + GAP * row + shift : 8 + GAP * row + shift + PW] for shift in (-1, 0, 1)]
        for row in range(STRIPE)
    ]


def filtered(rows, taps, flip):
    order = [8 - tap if flip else tap for tap in range(9)]
    taps = [taps[tap : tap + 1] for tap in order]
    out = []
    for row in range(STRIPE):
        total = None
        for a in range(3):
            if 0 <= row + a - 1 < STRIPE:
                for e in range(3):
                    term = taps[3 * a + e] * rows[row + a - 1][e]
                    total = term if total is None else total + term
        out.append(total)
    return jnp.concatenate(out, axis=0)


def tap_sums(grad_rows, value_rows):
    sums = []
    for a in range(3):
        for e in range(3):
            total = None
            for row in range(STRIPE):
                if 0 <= row + a - 1 < STRIPE:
                    term = grad_rows[row][1] * value_rows[row + a - 1][e]
                    total = term if total is None else total + term
            sums.append(jnp.sum(total, 0, keepdims=True))
    total = grad_rows[0][1]
    for row in range(1, STRIPE):
        total = total + grad_rows[row][1]
    sums.append(jnp.sum(total, 0, keepdims=True))
    return sums


def window_valid(window_base, lim_major, lim_minor):
    return inside(split_index(WIN, PW, BR), window_base, 0, lim_major, lim_minor)


def window_scores(projected, valid, first, k, refs):
    p_ref, q_ref, k_ref, v_ref, o_ref, rl_ref, kb_ref, vb_ref, lepe_ref, mixed_ref, pad_ref = refs
    queries = (projected[:, :BR] * HEAD_DIM**-0.5).astype(BF16)
    key_rows = projected[:, BR : 2 * BR]
    values = projected[:, 2 * BR :].astype(BF16).astype(F32)
    valid_float = as_float(valid)
    weight = jnp.where(valid, 1.0, MASKED_WEIGHT)
    q_ref[first + k] = queries
    k_ref[first + k] = (key_rows * valid_float).astype(BF16)
    v_ref[first + k] = values.astype(BF16)
    kb_ref[k] = head_blocks(key_rows * valid_float).astype(BF16)
    vb_ref[k, :, :BR] = head_blocks(values * weight).astype(BF16)
    vb_ref[k, :, BR:] = head_blocks(weight).astype(BF16)
    for lo, hi in CHUNKS:
        p_ref[first + k, :, lo:hi] = jnp.exp2(dot_nt(queries, kb_ref[k, lo:hi]) * LOG2E).astype(BF16)
    return values


def window_mixed(values, taps, shift, first, k, refs):
    p_ref, q_ref, k_ref, v_ref, o_ref, rl_ref, kb_ref, vb_ref, lepe_ref, mixed_ref, pad_ref = refs
    sums = dot(p_ref[first + k], vb_ref[k])
    totals = sums[:, BR:]
    inverse = 1.0 / totals
    attended = sums[:, :BR] * inverse
    o_ref[first + k] = attended
    rl_ref[first + k] = inverse.astype(BF16)
    spread(pad_ref.at[k], values)
    lepe = filtered(neighbours(pad_ref.at[k]), taps, False) + shift
    lepe_ref[k] = lepe
    mixed_ref[k] = attended + lepe
    safe = (totals > DEN_LOW) & (totals < DEN_HIGH)
    return jnp.max(jnp.where(safe, 0.0, 1.0))


def window_forward_safe(first, k, refs, s_ref):
    p_ref, q_ref, k_ref, v_ref, o_ref, rl_ref, kb_ref, vb_ref, lepe_ref, mixed_ref, _ = refs
    s_ref[...] = dot_nt(q_ref[first + k], kb_ref[k]) * LOG2E
    for head in range(HEADS):
        cut = slice(head * MAIN, (head + 1) * MAIN)
        rest = HEADS * MAIN + head * REST
        left = s_ref[:, cut]
        right = s_ref[:, rest : rest + REST]
        peak = jnp.maximum(jnp.max(left, -1, keepdims=True), jnp.max(right, -1, keepdims=True))
        s_ref[:, cut] = left - peak
        s_ref[:, rest : rest + REST] = right - peak
    for lo, hi in CHUNKS:
        p_ref[first + k, :, lo:hi] = jnp.exp2(s_ref[:, lo:hi]).astype(BF16)
    sums = dot(p_ref[first + k], vb_ref[k])
    inverse = 1.0 / sums[:, BR:]
    attended = sums[:, :BR] * inverse
    o_ref[first + k] = attended
    rl_ref[first + k] = inverse.astype(BF16)
    mixed_ref[k] = attended + lepe_ref[k]


def window_scores_back(grads, first, k, refs):
    p_ref, q_ref, k_ref, v_ref, o_ref, rl_ref, kb_ref, vb_ref, ds_ref, pad_ref = refs
    lane = lax.broadcasted_iota(jnp.int32, (WIN, BR), 1)
    scaled = (grads * rl_ref[first + k].astype(F32)).astype(BF16)
    product = scaled.astype(F32) * o_ref[first + k]
    high = product.astype(BF16)
    low = (product - high.astype(F32)).astype(BF16)
    row = lax.broadcasted_iota(jnp.int32, (2 * BR, BR), 0)
    col = lax.broadcasted_iota(jnp.int32, (2 * BR, BR), 1)
    head_of = lax.shift_right_logical(row & (BR - 1), 5)
    picks = as_float((col < 2 * HEADS) & (head_of == (col & (HEADS - 1)))).astype(BF16)
    inner = dot(jnp.concatenate([high, low], axis=1), picks)
    inner_high = inner.astype(BF16).astype(F32)
    extra = jnp.where(lane < HEADS, inner_high, inner - inner_high).astype(BF16)
    left = jnp.concatenate([scaled, extra], axis=1)
    values = v_ref[first + k].astype(F32)
    vb_ref[k, :, :BR] = head_blocks(values).astype(BF16)
    kb_ref[k] = head_blocks(k_ref[first + k].astype(F32)).astype(BF16)
    for lo, hi in CHUNKS:
        grad_probs = dot_nt(left, vb_ref[k, lo:hi])
        ds_ref[k, :, lo:hi] = grad_probs.astype(BF16) * p_ref[first + k, :, lo:hi]
    scaled_t = scaled.astype(F32).T.astype(BF16)
    return dot(scaled_t, p_ref[first + k])


def window_products_back(scaled, first, k, refs):
    p_ref, q_ref, k_ref, v_ref, o_ref, rl_ref, kb_ref, vb_ref, ds_ref, pad_ref = refs
    grad_query = dot(ds_ref[k], kb_ref[k]) * (HEAD_DIM**-0.5)
    query_t = q_ref[first + k].astype(F32).T.astype(BF16)
    return grad_query, dot(query_t, ds_ref[k]), scaled


def window_rows_back(grads, products, base, lim_major, lim_minor, taps, first, k, refs):
    v_ref, pad_ref = refs[3], refs[9]
    grad_query, wide_key, wide_value = products
    values = v_ref[first + k].astype(F32)
    valid_t = inside(split_index(WIN, PW, BR, 1), base, 0, lim_major, lim_minor)
    weight_t = jnp.where(valid_t, 1.0, MASKED_WEIGHT)
    grad_key = (from_wide(wide_key) * jnp.where(valid_t, 1.0, 0.0)).T
    grad_value = (from_wide(wide_value) * weight_t).T
    spread(pad_ref.at[2 * k], grads)
    spread(pad_ref.at[2 * k + 1], values)
    grad_rows, value_rows = neighbours(pad_ref.at[2 * k]), neighbours(pad_ref.at[2 * k + 1])
    back, tap_rows = filtered(grad_rows, taps, True), tap_sums(grad_rows, value_rows)
    out = jnp.concatenate([grad_query, grad_key, grad_value + back], axis=1)
    return out.astype(BF16), tap_rows


def window_pair_back(grads, first, refs):
    scaled = [window_scores_back(grads[k], first, k, refs) for k in range(2)]
    return [window_products_back(scaled[k], first, k, refs) for k in range(2)]


def set_indicator(vb_ref):
    row = lax.broadcasted_iota(jnp.int32, (WIDE, BR), 0)
    col = lax.broadcasted_iota(jnp.int32, (WIDE, BR), 1)
    head = jnp.zeros((WIDE, BR), jnp.int32)
    for cut in range(1, HEADS):
        head = head + jnp.where(row >= cut * MAIN, 1, 0)
    tail = lax.shift_right_logical(row - HEADS * MAIN, 3)
    head = jnp.where(row >= HEADS * MAIN, tail, head)
    hit = (col < 2 * HEADS) & ((col & (HEADS - 1)) == head)
    for k in range(2):
        vb_ref[k, :, BR:] = jnp.where(hit, -1.0, 0.0).astype(BF16)


def split_columns(source, left, right):
    for row in range(STRIPE * 2):
        left[row * HALF : (row + 1) * HALF] = source[row * PW : row * PW + HALF]
        right[row * HALF : (row + 1) * HALF] = source[row * PW + HALF : (row + 1) * PW]


def merge_columns(left, right, target):
    for row in range(STRIPE * 2):
        target[row * PW : row * PW + HALF] = left[row * HALF : (row + 1) * HALF]
        target[row * PW + HALF : (row + 1) * PW] = right[row * HALF : (row + 1) * HALF]


def sides(image, heights, info):
    return heights[image], info[image]


def tensor_place(info):
    return info[info.shape[0] - 3]


def core_place(info):
    return info[info.shape[0] - 2]


def along_place(info):
    return info[info.shape[0] - 1]


def pack_kernel(qkv_ref, lepe_ref, shift_ref, out_ref, send_ref):
    for item in range(3):
        for direction in range(2):
            row = (2 * item + direction) * BR // 2
            out_ref[row : row + BR // 2] = qkv_ref[item, direction]
    rows = [
        jnp.concatenate([lepe_ref[tap, 0:1], lepe_ref[tap, 1:2]], axis=1).astype(F32)
        for tap in range(9)
    ]
    rows.append(jnp.concatenate([shift_ref[0:1], shift_ref[1:2]], axis=1).astype(F32))
    rows.append(jnp.zeros((2 * FIRST_HALF - SMALL_AT - 10, BR), F32))
    small = jnp.concatenate(rows, axis=0)
    out_ref[SMALL_AT:] = jnp.concatenate([small, jnp.zeros_like(small)], axis=1).astype(BF16)
    core = lax.axis_index("dp") % 2
    send_ref[...] = out_ref[pl.ds(pl.multiple_of(core * FIRST_HALF, 16), FIRST_HALF)]


def late_pack_kernel(info, w1_ref, w2_ref, proj_ref, b1_ref, pb_ref, b2_ref, out_ref, send_ref):
    for j in range(2):
        out_ref[j * CHUNK : (j + 1) * CHUNK] = w1_ref[:, j * CHUNK : (j + 1) * CHUNK]
    out_ref[2 * CHUNK : 4 * CHUNK] = w2_ref[...]
    for b in range(2):
        at = 4 * CHUNK + b * BR // 2
        out_ref[at : at + BR // 2] = proj_ref[b]
    first = b1_ref[...].astype(F32).reshape(1, 2 * CHUNK)
    vectors = [first[:, :CHUNK], first[:, CHUNK:]]
    vectors += [ref[...].astype(F32).reshape(1, 2 * BR) for ref in (pb_ref, b2_ref)]
    tail = jnp.concatenate(vectors + [jnp.zeros((4 * LATE - GRAD_ROWS - 4, 2 * BR), F32)], axis=0)
    out_ref[GRAD_ROWS:] = tail.astype(BF16)
    part = 2 * core_place(info) + along_place(info)
    send_ref[...] = out_ref[pl.ds(pl.multiple_of(part * LATE, 16), LATE)]


def quadrant_kernel(images, info, x_ref, own_ref, *rest):
    sends, (whole, left, right) = rest[:images], rest[images:]
    step = pl.program_id(0)
    whole[...] = x_ref[0].astype(F32)
    split_columns(whole, left, right)
    first = tensor_place(info) == 0
    own_ref[0] = jnp.where(first, left[...], right[...]).astype(BF16)
    other = jnp.where(first, right[...], left[...]).astype(BF16)
    for image in range(images):

        @pl.when(step // 2 == image)
        def _():
            sends[image][0] = other


def rows_forward_kernel(image, first, *refs):
    heights, info, x_ref, gain_ref, bias_ref = refs[:5]
    if first:
        own_ref, near_ref, far_ref, p_ref, q_ref, k_ref, v_ref, o_ref, rl_ref, m_ref, w_ref, wt_ref, taps_ref = refs[5:18]
        other_ref = refs[-7]
    else:
        w_ref, taps_ref, p_ref, q_ref, k_ref, v_ref, o_ref, rl_ref, m_ref = refs[5:14]
    kb_ref, vb_ref, lepe_ref, mixed_ref, s_ref, pad_ref = refs[-6:]
    step = pl.program_id(0)
    height, width = sides(image, heights, info)
    row_base = tensor_place(info) * HALF + step * 2 * STRIPE

    def unpack_weights():
        core = core_place(info)
        for part, piece in ((core, near_ref), (1 - core, far_ref)):
            other_ref[pl.ds(pl.multiple_of(part * FIRST_HALF, 16), FIRST_HALF)] = piece[...]
        for direction in range(2):
            for item in range(3):
                row = (2 * item + direction) * BR // 2
                at = item * BR
                wt_ref[direction, at : at + BR // 2] = own_ref[row : row + BR // 2]
                wt_ref[direction, at + BR // 2 : at + BR] = other_ref[row : row + BR // 2]
            w_ref[direction] = wt_ref[direction].astype(F32).T.astype(BF16)
        own = own_ref[SMALL_AT : SMALL_AT + 16].astype(F32)
        other = other_ref[SMALL_AT : SMALL_AT + 16].astype(F32)
        half = BR // 2
        for direction in range(2):
            cut = slice(direction * half, (direction + 1) * half)
            both = jnp.concatenate([own[:, cut], other[:, cut]], axis=1)
            if direction == 1:
                order = [3 * (tap % 3) + tap // 3 for tap in range(9)] + list(range(9, 16))
                both = jnp.concatenate([both[tap : tap + 1] for tap in order], axis=0)
            taps_ref[direction] = both

    if first:
        pl.when(step == 0)(unpack_weights)

    @pl.when(step == 0)
    def _():
        pad_ref[...] = jnp.zeros_like(pad_ref)

    mask = as_float(inside(split_index(PAIR, PW, BR), row_base, 0, height, width))
    unit, _ = norm_parts(x_ref[0].astype(F32) * twice(mask))
    normed = (unit * gain_ref[...] + bias_ref[...]).astype(BF16)
    projected = dot(normed, w_ref[0])
    refs = (
        p_ref, q_ref, k_ref, v_ref, o_ref, rl_ref, kb_ref, vb_ref, lepe_ref, mixed_ref, pad_ref
    )
    bad = jnp.float32(0)
    values = []
    for k in range(2):
        valid = window_valid(row_base + k * STRIPE, height, width)
        rows = projected[k * WIN : (k + 1) * WIN]
        values.append(window_scores(rows, valid, 2 * step, k, refs))
    for k in range(2):
        bad = jnp.maximum(
            bad, window_mixed(values[k], taps_ref[0, :9], taps_ref[0, 9:10], 2 * step, k, refs)
        )

    @pl.when(bad > 0.0)
    def _():
        def one(k, carry):
            window_forward_safe(2 * step, k, refs, s_ref)
            return carry

        lax.fori_loop(0, 2, one, 0)

    for k in range(2):
        m_ref[2 * step + k] = mixed_ref[k].astype(BF16)


def columns_forward_kernel(
    image, heights, info, own_ref, other_ref, gain_ref, bias_ref, w_ref, taps_ref,
    p_ref, q_ref, k_ref, v_ref, o_ref, rl_ref, n_ref, keep_ref, send_ref,
    unit_ref, out_ref, kb_ref, vb_ref, lepe_ref, mixed_ref, s_ref, pad_ref,
):
    step = pl.program_id(0)
    place = tensor_place(info)
    height, width = sides(image, heights, info)
    column_base = place * HALF

    @pl.when(step == 0)
    def _():
        pad_ref[...] = jnp.zeros_like(pad_ref)
        for source, side in ((own_ref, place), (other_ref, 1 - place)):
            for s in range(2):
                flag = inside(
                    split_index(WIN, HALF, BR), side * HALF + s * 2 * STRIPE, column_base,
                    height, width,
                )
                unit, _ = norm_parts(source[s].astype(F32) * twice(as_float(flag)))
                start = pl.multiple_of(side * PAIR + s * WIN, 8)
                unit_ref[0, pl.ds(start, WIN)] = unit[:, :BR]
                unit_ref[1, pl.ds(start, WIN)] = unit[:, BR:]

    refs = (
        p_ref, q_ref, k_ref, v_ref, o_ref, rl_ref, kb_ref, vb_ref, lepe_ref, mixed_ref, pad_ref
    )
    bad = jnp.float32(0)
    values = []
    for k in range(2):
        column = (2 * step + k) * STRIPE
        halves = [
            jnp.concatenate(
                [unit_ref[j, pl.ds(column + q, PH, stride=HALF)] for q in range(STRIPE)], axis=0
            )
            for j in range(2)
        ]
        unit = jnp.concatenate(halves, axis=1)
        n_ref[2 * step + k] = unit.astype(BF16)
        normed = (unit * gain_ref[...] + bias_ref[...]).astype(BF16)
        valid = window_valid(column_base + column, width, height)
        values.append(window_scores(dot(normed, w_ref[1]), valid, 2 * step, k, refs))
    for k in range(2):
        bad = jnp.maximum(
            bad, window_mixed(values[k], taps_ref[1, :9], taps_ref[1, 9:10], 2 * step, k, refs)
        )

    @pl.when(bad > 0.0)
    def _():
        def one(k, carry):
            window_forward_safe(2 * step, k, refs, s_ref)
            return carry

        lax.fori_loop(0, 2, one, 0)

    for k in range(2):
        column = (2 * step + k) * STRIPE
        mixed = mixed_ref[k]
        for q in range(STRIPE):
            out_ref[pl.ds(column + q, PH, stride=HALF)] = mixed[q * PH : (q + 1) * PH]

    @pl.when(step == 1)
    def _():
        for s in range(2):
            keep = pl.multiple_of(place * PAIR + s * WIN, 8)
            send = pl.multiple_of((1 - place) * PAIR + s * WIN, 8)
            keep_ref[s] = out_ref[pl.ds(keep, WIN)].astype(BF16)
            send_ref[s] = pltpu.roll(out_ref[pl.ds(send, WIN)], BR // 2, 1).astype(BF16)


def mlp_kernel(images, *refs):
    heights, info, x_ref, cot_ref = refs[:4]
    mh_refs, mo_refs, mr_refs = (refs[4 + i * images : 4 + (i + 1) * images] for i in range(3))
    refs = refs[4 + 3 * images :]
    gain_ref, bias_ref, late_own, *late_parts = refs[:7]
    out_ref, gmid_ref, gh_ref, gk_ref, gs_ref, small_ref, kept_ref, sent_ref = refs[7:15]
    acc_ref, pw_ref, late_ref, whole, left, right = refs[15:]
    step = pl.program_id(0)
    image, pair = step // 2, step % 2
    place = tensor_place(info)
    height, width = sides(image, heights, info)
    row_base = place * HALF + pair * 2 * STRIPE
    half = BR // 2

    def of_image(items, at):
        value = items[0][at].astype(F32)
        for index in range(1, images):
            value = jnp.where(image == index, items[index][at].astype(F32), value)
        return value

    @pl.when(step == 0)
    def _():
        far = 4 * LATE
        late_ref[:far] = late_own[...]
        core, along = core_place(info), along_place(info)
        for at, piece in enumerate(late_parts):
            part = 2 * (core if at < 2 else 1 - core) + (along if at % 2 == 0 else 1 - along)
            late_ref[pl.ds(pl.multiple_of(far + part * LATE, 16), LATE)] = piece[...]
        for b in range(2):
            at = 4 * CHUNK + b * half
            pw_ref[b * BR : b * BR + half] = late_ref[at : at + half]
            pw_ref[b * BR + half : (b + 1) * BR] = late_ref[far + at : far + at + half]
        acc_ref[...] = jnp.zeros_like(acc_ref)
        small_ref[...] = jnp.zeros_like(small_ref)

    vectors = late_own[GRAD_ROWS : GRAD_ROWS + 16].astype(F32)
    mask = twice(as_float(inside(split_index(PAIR, PW, BR), row_base, 0, height, width)))
    first_half = place == 0
    own = of_image(mo_refs, pair)
    other = of_image(mr_refs, pair)
    left[...] = jnp.where(first_half, own, other)
    right[...] = jnp.where(first_half, other, own)
    merge_columns(left, right, whole)
    rows_part = jnp.concatenate([of_image(mh_refs, 2 * pair + k) for k in range(2)], axis=0)
    mixed = jnp.concatenate([rows_part, whole[...]], axis=1).astype(BF16)
    x_in = x_ref[0].astype(F32) * mask
    x_mid = x_in + dot(mixed, pw_ref[...]) + vectors[2:3]
    unit, inverse = norm_parts(x_mid)
    normed = (unit * gain_ref[...] + bias_ref[...]).astype(BF16)
    grad_result = cot_ref[0].astype(F32) * mask
    grad_low = grad_result.astype(BF16)
    normed_t = normed.T
    grad_t = grad_low.T

    total = x_mid + vectors[3:4]
    grad_normed = jnp.zeros_like(x_mid)

    def chunk_start(j):
        base = (j // 2) * 4 * LATE
        at = base + (j % 2) * CHUNK
        w1, w2 = late_ref[at : at + CHUNK], late_ref[at + 2 * CHUNK : at + 3 * CHUNK]
        rows = late_ref[base + GRAD_ROWS : base + GRAD_ROWS + 16].astype(F32)
        pre = dot(normed, w1) + rows[j % 2 : j % 2 + 1]
        return w1, w2, pre, dot_nt(grad_low, w2)

    ahead = chunk_start(0)
    for j in range(4):
        w1, w2, pre, grad_hidden = ahead
        if j < 3:
            ahead = chunk_start(j + 1)
        holder, cut = j // 2, (j % 2) * CHUNK
        bell = jnp.exp2(pre * pre * (-0.5 * LOG2E))
        below = 0.5 + 0.5 * lax.erf(pre * ROOT_HALF)
        hidden = (pre * below).astype(BF16)
        slope = below + pre * bell * DENSITY
        grad_pre = (grad_hidden * slope).astype(BF16)
        total = total + dot(hidden, w2)
        grad_normed = grad_normed + dot_nt(grad_pre, w1)
        acc_ref[holder, cut : cut + CHUNK] += dot(normed_t, grad_pre)
        acc_ref[holder, cut + 2 * CHUNK : cut + 3 * CHUNK] += dot(grad_t, hidden)
        small_ref[4 + j : 5 + j] += jnp.sum(grad_pre.astype(F32), 0, keepdims=True)
    out_ref[0] = (mask * total).astype(BF16)
    grad_mid = grad_result + norm_back(grad_normed, unit, inverse, gain_ref[...])
    gmid_ref[0] = grad_mid
    small_ref[0:1] += jnp.sum(grad_normed * unit, 0, keepdims=True)
    small_ref[1:2] += jnp.sum(grad_normed, 0, keepdims=True)
    small_ref[2:3] += jnp.sum(grad_mid, 0, keepdims=True)
    small_ref[3:4] += jnp.sum(grad_result, 0, keepdims=True)
    mid_low = grad_mid.astype(BF16)
    grad_proj = dot_tn(mixed, mid_low)
    for b in range(2):
        at = 4 * CHUNK + b * half
        acc_ref[0, at : at + half] += grad_proj[b * BR : b * BR + half]
        acc_ref[1, at : at + half] += grad_proj[b * BR + half : (b + 1) * BR]
    grad_mixed = dot_nt(mid_low, pw_ref[...])
    gh_ref[0] = grad_mixed[:WIN, :BR].astype(BF16)
    gh_ref[1] = grad_mixed[WIN:, :BR].astype(BF16)
    whole[...] = grad_mixed[:, BR:]
    split_columns(whole, left, right)
    gk_ref[0] = jnp.where(first_half, left[...], right[...]).astype(BF16)
    gs_ref[0] = pltpu.roll(jnp.where(first_half, right[...], left[...]), half, 1).astype(BF16)

    @pl.when(step == 2 * images - 1)
    def _():
        for s in range(2):
            for j in range(2, 4):
                cut = slice(j * CHUNK, (j + 1) * CHUNK)
                acc_ref[s, cut] = acc_ref[s, cut].T
        core, along = core_place(info), along_place(info)
        rows = GRAD_ROWS // 4
        for s in range(2):
            for near in range(2):
                side = along if near == 0 else 1 - along
                mine = pl.multiple_of((2 * core + side) * rows, 8)
                theirs = pl.multiple_of((2 * (1 - core) + side) * rows, 8)
                kept_ref[s, near] = acc_ref[s, pl.ds(mine, rows)].astype(BF16)
                sent_ref[s, near] = acc_ref[s, pl.ds(theirs, rows)].astype(BF16)


def backward_sums(rows, unit, acc_ref, sum_ref):
    acc_ref[...] += dot_tn(unit, rows)
    sum_ref[0:1] += jnp.sum(rows.astype(F32), 0, keepdims=True)


def columns_backward_kernel(
    image, heights, info, gk_ref, gr_ref, p_ref, q_ref, k_ref, v_ref, o_ref, rl_ref, n_ref, wt_ref,
    taps_ref, acc_ref, sum_ref, lepe_ref, keep_ref, send_ref,
    grad_ref, out_ref, kb_ref, vb_ref, ds_ref, pad_ref,
):
    step = pl.program_id(0)
    place = tensor_place(info)
    height, width = sides(image, heights, info)

    @pl.when(step == 0)
    def _():
        set_indicator(vb_ref)
        pad_ref[...] = jnp.zeros_like(pad_ref)
        acc_ref[...] = jnp.zeros_like(acc_ref)
        sum_ref[...] = jnp.zeros_like(sum_ref)
        lepe_ref[...] = jnp.zeros_like(lepe_ref)
        for source, side in ((gk_ref, place), (gr_ref, 1 - place)):
            for s in range(2):
                start = pl.multiple_of(side * PAIR + s * WIN, 8)
                grad_ref[pl.ds(start, WIN)] = source[s].astype(F32)

    refs = (p_ref, q_ref, k_ref, v_ref, o_ref, rl_ref, kb_ref, vb_ref, ds_ref, pad_ref)
    first = 2 * step
    columns = [(first + k) * STRIPE for k in range(2)]
    grads = [
        jnp.concatenate([grad_ref[pl.ds(column + q, PH, stride=HALF)] for q in range(STRIPE)], axis=0)
        for column in columns
    ]
    products = window_pair_back(grads, first, refs)
    for k in range(2):
        column = columns[k]
        rows, tap_rows = window_rows_back(
            grads[k], products[k], place * HALF + column, width, height, taps_ref[1, :9], first, k, refs
        )
        for index, item in enumerate(tap_rows):
            lepe_ref[index : index + 1] += item
        backward_sums(rows, n_ref[2 * step + k], acc_ref, sum_ref)
        back = dot(rows, wt_ref[1])
        for q in range(STRIPE):
            cut = slice(q * PH, (q + 1) * PH)
            out_ref[0, pl.ds(column + q, PH, stride=HALF)] = back[cut, :BR]
            out_ref[1, pl.ds(column + q, PH, stride=HALF)] = back[cut, BR:]

    @pl.when(step == 1)
    def _():
        for s in range(2):
            keep = pl.multiple_of(place * PAIR + s * WIN, 8)
            send = pl.multiple_of((1 - place) * PAIR + s * WIN, 8)
            for j in range(2):
                lanes = slice(j * BR, (j + 1) * BR)
                keep_ref[s, :, lanes] = out_ref[j, pl.ds(keep, WIN)].astype(BF16)
                send_ref[s, :, lanes] = out_ref[j, pl.ds(send, WIN)].astype(BF16)


def direction_grads(acc, sums, gain, bias, weight_t):
    moved = acc.T
    shift = sums[0:1]
    high = shift.astype(BF16)
    low = (shift - high.astype(F32)).astype(BF16)
    wide = dot(high, weight_t) + dot(low, weight_t)
    column = sums.T[:, 0:1]
    grad_qkv = moved * gain + column * bias
    grad_gain = jnp.sum(weight_t.astype(F32) * moved, 0, keepdims=True)
    return grad_qkv, grad_gain, wide


def rows_backward_kernel(image, start, count, last, others, *refs):
    (
        heights, info, x_ref, gm_ref, p_ref, q_ref, k_ref, v_ref, o_ref, rl_ref, wt_ref, taps_ref,
    ) = refs[:12]
    refs = refs[12:]
    if last:
        gain_ref, bias_ref, small2_ref = refs[:3]
        other_refs = refs[3 : 3 + 3 * sum(others)]
        refs = refs[3 + 3 * sum(others) :]
        gp_ref, kept_ref, sent_ref = refs[:3]
        acc_ref, sum_ref, lepe_ref, pack_ref, kb_ref, vb_ref, ds_ref, pad_ref = refs[3:]
    else:
        gp_ref, acc_ref, sum_ref, lepe_ref, kb_ref, vb_ref, ds_ref, pad_ref = refs
    step = pl.program_id(0)
    pair = start + step
    height, width = sides(image, heights, info)
    row_base = tensor_place(info) * HALF + pair * 2 * STRIPE

    @pl.when(step == 0)
    def _():
        set_indicator(vb_ref)
        pad_ref[...] = jnp.zeros_like(pad_ref)
        acc_ref[...] = jnp.zeros_like(acc_ref)
        sum_ref[...] = jnp.zeros_like(sum_ref)
        lepe_ref[...] = jnp.zeros_like(lepe_ref)

    mask = twice(as_float(inside(split_index(PAIR, PW, BR), row_base, 0, height, width)))
    unit, _ = norm_parts(x_ref[0].astype(F32) * mask)
    refs = (p_ref, q_ref, k_ref, v_ref, o_ref, rl_ref, kb_ref, vb_ref, ds_ref, pad_ref)
    first_window = 2 * pair
    grads = [gm_ref[k].astype(F32) for k in range(2)]
    products = window_pair_back(grads, first_window, refs)
    for k in range(2):
        base = row_base + k * STRIPE
        rows, tap_rows = window_rows_back(
            grads[k], products[k], base, height, width, taps_ref[0, :9], first_window, k, refs
        )
        for index, item in enumerate(tap_rows):
            lepe_ref[index : index + 1] += item
        gp_ref[k] = rows
        backward_sums(rows, unit[k * WIN : (k + 1) * WIN].astype(BF16), acc_ref, sum_ref)
    if last:

        @pl.when(step == count - 1)
        def _():
            row_items = [acc_ref[...], sum_ref[...], lepe_ref[...]]
            column_items = [0.0, 0.0, 0.0]
            for at in range(sum(others)):
                kind = other_refs[3 * at : 3 * at + 3]
                if at < others[0]:
                    row_items = [old + ref[...] for old, ref in zip(row_items, kind)]
                else:
                    column_items = [old + ref[...] for old, ref in zip(column_items, kind)]
            gain, bias = gain_ref[...], bias_ref[...]
            grad_gain = grad_bias = 0.0
            half = BR // 2
            for direction, items in enumerate((row_items, column_items)):
                grad_qkv, gain_row, bias_row = direction_grads(
                    items[0], items[1], gain, bias, wt_ref[direction]
                )
                grad_gain = grad_gain + gain_row
                grad_bias = grad_bias + bias_row
                for s in range(2):
                    for item in range(3):
                        at = direction * 3 * half + item * half
                        take = item * BR + s * half
                        pack_ref[s, at : at + half] = grad_qkv[take : take + half]
            small2 = small2_ref[...]
            for s in range(2):
                cut = slice(s * half, (s + 1) * half)
                lepe = jnp.concatenate(
                    [row_items[2][:, cut], column_items[2][:, cut], jnp.zeros((16, BR), F32)], axis=1
                )
                head = jnp.concatenate(
                    [grad_gain, grad_bias, small2[:4], small2[4 + 2 * s : 6 + 2 * s]], axis=0
                )
                pack_ref[s, SMALL_AT : SMALL_AT + 8] = head
                pack_ref[s, SMALL_AT + 8 : SMALL_AT + 24] = lepe
                pack_ref[s, SMALL_AT + 24 :] = jnp.zeros((LAST_ROWS - SMALL_AT - 24, 2 * BR), F32)
            core = core_place(info)
            rows = LAST_ROWS // 2
            for s in range(2):
                mine = pl.multiple_of(core * rows, 8)
                theirs = pl.multiple_of((1 - core) * rows, 8)
                kept_ref[s] = pack_ref[s, pl.ds(mine, rows)].astype(BF16)
                sent_ref[s] = pack_ref[s, pl.ds(theirs, rows)].astype(BF16)


def input_kernel(image, start, first, *refs):
    heights, info, x_ref, gp_ref, gmid_ref, vk_ref, vr_ref, wt_ref, gain_ref = refs[:9]
    refs = refs[9:] if first else refs[10:]
    out_ref, mark_ref, whole, left, right = refs
    mark_ref[...] = jnp.zeros_like(mark_ref)
    pair = start + pl.program_id(0)
    place = tensor_place(info)
    height, width = sides(image, heights, info)
    row_base = place * HALF + pair * 2 * STRIPE
    mask = twice(as_float(inside(split_index(PAIR, PW, BR), row_base, 0, height, width)))
    unit, inverse = norm_parts(x_ref[0].astype(F32) * mask)
    first_half = place == 0
    own = vk_ref[0].astype(F32)
    other = vr_ref[0].astype(F32)
    left[...] = jnp.where(first_half, own, other)
    right[...] = jnp.where(first_half, other, own)
    merge_columns(left, right, whole)
    parts = [dot(gp_ref[k], wt_ref[0]) for k in range(2)]
    grad_normed = jnp.concatenate(parts, axis=0) + whole[...]
    back = norm_back(grad_normed, unit, inverse, gain_ref[...])
    out_ref[0] = (mask * (gmid_ref[0] + back)).astype(BF16)


def unpack_first_kernel(info, a_ref, ax_ref, b_ref, bx_ref, fc1_ref, fc2_ref, proj_ref, mark_ref):
    mark_ref[...] = jnp.zeros_like(mark_ref)
    core, along = core_place(info) == 0, along_place(info) == 0
    quarters = []
    for c in range(2):
        for side in range(2):
            here = core if c == 0 else jnp.logical_not(core)
            near = along if side == 0 else jnp.logical_not(along)
            mine = jnp.where(near, a_ref[...].astype(F32), ax_ref[...].astype(F32))
            theirs = jnp.where(near, b_ref[...].astype(F32), bx_ref[...].astype(F32))
            quarters.append(jnp.where(here, mine, theirs))
    total = jnp.concatenate(quarters, axis=0)
    fc1_ref[:, :CHUNK] = total[:CHUNK]
    fc1_ref[:, CHUNK:] = total[CHUNK : 2 * CHUNK]
    fc2_ref[...] = total[2 * CHUNK : 4 * CHUNK]
    proj_ref[...] = total[4 * CHUNK :]


def unpack_last_kernel(
    info, c_ref, cx_ref, qkv_ref, lepe_ref, shift_ref, b1_ref,
    gain1_ref, bias1_ref, gain2_ref, bias2_ref, projb_ref, b2_ref,
):
    core = core_place(info) == 0
    mine, theirs = c_ref[...].astype(F32), cx_ref[...].astype(F32)
    last = jnp.concatenate([jnp.where(core, mine, theirs), jnp.where(core, theirs, mine)], axis=0)
    half = BR // 2
    for direction in range(2):
        for item in range(3):
            at = direction * 3 * half + item * half
            qkv_ref[item, direction] = last[at : at + half]
    small = last[SMALL_AT : SMALL_AT + 24]
    for row, ref in enumerate((gain1_ref, bias1_ref, gain2_ref, bias2_ref, projb_ref, b2_ref)):
        ref[...] = small[row : row + 1]
    for part in range(4):
        b1_ref[part : part + 1] = small[6 + part // 2 : 7 + part // 2, part % 2 * BR : (part % 2 + 1) * BR]
    for tap in range(9):
        turned = 8 + 3 * (tap % 3) + tap // 3
        lepe_ref[tap, 0:1] = small[8 + tap : 9 + tap, :half]
        lepe_ref[tap, 1:2] = small[turned : turned + 1, half : 2 * half]
    shift_ref[0:1] = small[17:18, :half]
    shift_ref[1:2] = small[17:18, half : 2 * half]


def spec(shape, index=None):
    if index is None:
        return pl.BlockSpec(shape, lambda i: (0,) * len(shape))
    return pl.BlockSpec(shape, index)


def shaped(shape, dtype):
    return jax.ShapeDtypeStruct(shape, dtype)


SCALARS = pl.BlockSpec(memory_space=pltpu.SMEM)
RESIDENT = pl.BlockSpec(memory_space=pltpu.VMEM)


def call(
    kernel, name, grid, in_specs, out_specs, out_shape, scratch, micros, limit, aliases=None, marks=0
):
    known = len(in_specs)

    def body(*refs):
        kernel(*refs[:known], *refs[known + marks :])

    in_specs = list(in_specs) + [pl.BlockSpec(memory_space=pl.ANY)] * marks
    return pl.pallas_call(
        body,
        name=name,
        grid=(grid,),
        in_specs=in_specs,
        out_specs=out_specs,
        out_shape=out_shape,
        scratch_shapes=scratch,
        input_output_aliases=aliases or {},
        cost_estimate=pl.CostEstimate(
            flops=int(micros * FLOPS_PER_MICRO), bytes_accessed=0, transcendentals=0
        ),
        compiler_params=pltpu.CompilerParams(
            vmem_limit_bytes=limit * MIB, dimension_semantics=("arbitrary",)
        ),
    )


def kept_shapes(count):
    return [pltpu.VMEM((count, WIN, WIDE), BF16)] + [
        pltpu.VMEM((count, WIN, BR), BF16) for _ in range(3)
    ] + [pltpu.VMEM((count, WIN, BR), kind) for kind in (F32, BF16)]


def resident(arrays):
    return [pltpu.with_memory_space_constraint(item, pltpu.VMEM) for item in arrays]


def in_hbm(arrays):
    return [pltpu.with_memory_space_constraint(item, pltpu.HBM) for item in arrays]


def forward_scratch():
    return [
        pltpu.VMEM((2, WIDE, BR), BF16),
        pltpu.VMEM((2, WIDE, 2 * BR), BF16),
        pltpu.VMEM((2, WIN, BR), F32),
        pltpu.VMEM((2, WIN, BR), F32),
        pltpu.VMEM((WIN, WIDE), F32),
        pltpu.VMEM((2, PAD_ROWS, BR), F32),
    ]


def backward_scratch():
    return [
        pltpu.VMEM((2, WIDE, BR), BF16),
        pltpu.VMEM((2, WIDE, 2 * BR), BF16),
        pltpu.VMEM((2, WIN, WIDE), BF16),
        pltpu.VMEM((4, PAD_ROWS, BR), F32),
    ]


FLOPS_PER_MICRO = 1.15e9
ATTENTION_LIMIT = 15
MLP_LIMIT = 18


def pack_first(qkv, lepe, shift):
    width = qkv.shape[-1]
    return call(
        pack_kernel, "pack", 1, [spec(qkv.shape), spec(lepe.shape), spec(shift.shape)],
        [spec((2 * FIRST_HALF, width)), spec((FIRST_HALF, width))],
        [shaped((2 * FIRST_HALF, width), BF16), shaped((FIRST_HALF, width), BF16)], [], 1, 8,
    )(*in_hbm([qkv, lepe, shift]))


def pack_late(info, w1, w2, proj, vectors):
    width = w2.shape[1]
    rows = 4 * LATE
    return call(
        late_pack_kernel, "pack_late", 1,
        [SCALARS, spec(w1.shape), spec(w2.shape), spec(proj.shape)] + [spec(v.shape) for v in vectors],
        [spec((rows, width)), spec((LATE, width))],
        [shaped((rows, width), BF16), shaped((LATE, width), BF16)], [], 1, 8,
    )(info, w1, w2, proj, *vectors)


def split_quadrants(info, x_pairs):
    count, _, width = x_pairs.shape
    images = count // 2
    block = (1, WIN, width)

    def clamp(image):
        return lambda i: (jnp.clip(i - 2 * image, 0, 1), 0, 0)

    return call(
        partial(quadrant_kernel, images), "quadrants", count,
        [SCALARS, spec((1, PAIR, width), lambda i: (i, 0, 0))],
        [spec(block, lambda i: (i, 0, 0))] + [spec(block, clamp(image)) for image in range(images)],
        [shaped((count, WIN, width), BF16)] + [shaped((2, WIN, width), BF16)] * images,
        [pltpu.VMEM((PAIR, width), F32), pltpu.VMEM((WIN, width), F32), pltpu.VMEM((WIN, width), F32)],
        2, 16,
    )(info, x_pairs)


def rows_forward(image, heights, info, x_pairs, gain, bias, packs, known):
    count, _, width = x_pairs.shape
    pair = spec((1, PAIR, width), lambda i: (2 * image + i, 0, 0))
    in_specs = [SCALARS, SCALARS, pair, spec((1, width)), spec((1, width))]
    operands = [heights, info, x_pairs, gain, bias]
    out_shapes = kept_shapes(4) + [pltpu.VMEM((4, WIN, BR), BF16)]
    scratch = forward_scratch()
    if known is None:
        in_specs += [spec(item.shape) for item in packs]
        operands += list(packs)
        scratch = [pltpu.VMEM((2 * FIRST_HALF, width), BF16)] + scratch
        out_shapes += [
            pltpu.VMEM((2, width, 3 * BR), BF16), pltpu.VMEM((2, 3 * BR, width), BF16),
            pltpu.VMEM((2, 16, BR), F32),
        ]
    else:
        in_specs += [RESIDENT] * 2
        operands += resident(known)
    return call(
        partial(rows_forward_kernel, image, known is None), "rows_forward", 2, in_specs,
        [RESIDENT] * len(out_shapes), out_shapes, scratch,
        6.2, ATTENTION_LIMIT,
    )(*operands)


def columns_forward(image, heights, info, own, other, gain, bias, weight, taps):
    width = own.shape[2]
    fixed = spec((2, WIN, BR), lambda i: (0, 0, 0))
    return call(
        partial(columns_forward_kernel, image), "columns_forward", 2,
        [
            SCALARS, SCALARS, spec((2, WIN, width), lambda i: (image, 0, 0)), spec((2, WIN, width)),
            spec((1, width)), spec((1, width)), RESIDENT, RESIDENT,
        ],
        [RESIDENT] * 7 + [fixed, fixed],
        kept_shapes(4) + [pltpu.VMEM((4, WIN, width), BF16)] + [shaped((2, WIN, BR), BF16)] * 2,
        [pltpu.VMEM((2, 2 * PAIR, BR), F32), pltpu.VMEM((2 * PAIR, BR), F32)] + forward_scratch(),
        6.2, ATTENTION_LIMIT,
    )(heights, info, own, other, gain, bias, *resident([weight, taps]))


def mlp(heights, info, x_pairs, cot_pairs, mixed_rows, mixed_own, mixed_other, gain, bias, late):
    count, _, width = x_pairs.shape
    images = count // 2
    pair = spec((1, PAIR, width), lambda i: (i, 0, 0))
    part = spec((1, WIN, BR), lambda i: (i, 0, 0))
    row = spec((1, width))
    quarter = (2, 2, GRAD_ROWS // 4, width)
    return call(
        partial(mlp_kernel, images), "feed_forward", count,
        [SCALARS, SCALARS, pair, pair] + [RESIDENT] * (3 * images) + [row, row] + [RESIDENT] * 5,
        [
            pair, pair, spec((2, WIN, BR), lambda i: (i, 0, 0)), part, part, spec((8, width)),
            spec(quarter), spec(quarter),
        ],
        [
            shaped(x_pairs.shape, BF16), shaped(x_pairs.shape, F32), shaped((2 * count, WIN, BR), BF16),
            shaped((count, WIN, BR), BF16), shaped((count, WIN, BR), BF16), shaped((8, width), F32),
            shaped(quarter, BF16), shaped(quarter, BF16),
        ],
        [
            pltpu.VMEM((2, GRAD_ROWS, width), F32),
            pltpu.VMEM((2 * BR, width), BF16), pltpu.VMEM((8 * LATE, width), BF16),
            pltpu.VMEM((PAIR, BR), F32), pltpu.VMEM((WIN, BR), F32), pltpu.VMEM((WIN, BR), F32),
        ],
        20.4, MLP_LIMIT,
    )(
        heights, info, x_pairs, cot_pairs, *resident([*mixed_rows, *mixed_own, *mixed_other]), gain, bias,
        *resident(late),
    )


def columns_backward(image, heights, info, grad_own, grad_other, kept, unit, weight_t, taps):
    width = weight_t.shape[2]
    fixed = spec((2, WIN, width))
    grads = spec((2, WIN, BR), lambda i: (image, 0, 0))
    return call(
        partial(columns_backward_kernel, image), "columns_backward", 2,
        [SCALARS, SCALARS, grads, grads] + [RESIDENT] * 9,
        [spec((width, 3 * BR)), spec((8, 3 * BR)), spec((16, BR)), fixed, fixed],
        [shaped((width, 3 * BR), F32), shaped((8, 3 * BR), F32), shaped((16, BR), F32)]
        + [shaped((2, WIN, width), BF16)] * 2,
        [pltpu.VMEM((2 * PAIR, BR), F32), pltpu.VMEM((2, 2 * PAIR, BR), F32)] + backward_scratch(),
        8.5, ATTENTION_LIMIT,
    )(heights, info, grad_own, grad_other, *resident([*kept, unit, weight_t, taps]))


def rows_backward(image, start, count, heights, info, x_pairs, grad_mixed, kept, weight_t, taps, final):
    width = weight_t.shape[2]
    at = 2 * image + start
    pair = spec((1, PAIR, width), lambda i: (at + i, 0, 0))
    in_specs = [SCALARS, SCALARS, pair, spec((2, WIN, BR), lambda i: (at + i, 0, 0))] + [RESIDENT] * 8
    operands = [heights, info, x_pairs, grad_mixed, *resident([*kept, weight_t, taps])]
    sum_shapes = [(width, 3 * BR), (8, 3 * BR), (16, BR)]
    out_specs = [spec((2, WIN, 3 * BR), lambda i: (i, 0, 0))]
    out_shapes = [shaped((2 * count, WIN, 3 * BR), BF16)]
    scratch = backward_scratch()
    others = (0, 0)
    if final is None:
        out_specs += [spec(shape) for shape in sum_shapes]
        out_shapes += [shaped(shape, F32) for shape in sum_shapes]
    else:
        gain, bias, small2, row_items, column_items = final
        others = (len(row_items), len(column_items))
        in_specs += [spec((1, width)), spec((1, width)), spec((8, width))]
        operands += [gain, bias, small2]
        for item in [*row_items, *column_items]:
            in_specs += [spec(shape) for shape in sum_shapes]
            operands += list(item)
        half = (2, LAST_ROWS // 2, width)
        out_specs += [spec(half), spec(half)]
        out_shapes += [shaped(half, BF16), shaped(half, BF16)]
        scratch = (
            [pltpu.VMEM(shape, F32) for shape in sum_shapes]
            + [pltpu.VMEM((2, LAST_ROWS, width), F32)]
            + scratch
        )
    return call(
        partial(rows_backward_kernel, image, start, count, final is not None, others), "rows_backward",
        count, in_specs, out_specs, out_shapes, scratch, 4.3 * count, ATTENTION_LIMIT,
    )(*operands)


def input_rows(
    image, start, count, heights, info, x_pairs, rows, grad_mid, back_own, back_other, weight_t, gain,
    previous,
):
    width = weight_t.shape[2]
    pair = spec((1, PAIR, width), lambda i: (2 * image + start + i, 0, 0))
    part = spec((1, WIN, width), lambda i: (start + i, 0, 0))
    in_specs = [
        SCALARS, SCALARS, pair, spec((2, WIN, 3 * BR), lambda i: (start + i, 0, 0)), pair, part, part,
        RESIDENT, spec((1, width)),
    ]
    operands = [
        heights, info, x_pairs, rows, grad_mid, back_own, back_other, *resident([weight_t]), gain,
    ]
    aliases = {}
    if previous is not None:
        in_specs.append(pl.BlockSpec(memory_space=pl.ANY))
        operands.append(previous)
        aliases = {len(operands) - 1: 0}
    return call(
        partial(input_kernel, image, start, previous is None), "input_rows", count, in_specs,
        [pair, spec((8, 128))], [shaped(x_pairs.shape, BF16), shaped((8, 128), F32)],
        [pltpu.VMEM((PAIR, width), F32), pltpu.VMEM((WIN, width), F32), pltpu.VMEM((WIN, width), F32)],
        1.6 * count, 20, aliases,
    )(*operands)


def unpack_first(info, a, ax, b, bx, hidden, width):
    return call(
        unpack_first_kernel, "unpack_first", 1, [SCALARS] + [spec(a.shape)] * 4,
        [spec((width, hidden)), spec((hidden, width)), spec((BR, width)), spec((8, 128))],
        [
            shaped((width, hidden), F32), shaped((hidden, width), F32), shaped((BR, width), F32),
            shaped((8, 128), F32),
        ],
        [], 1, 16,
    )(info, a, ax, b, bx)


def unpack_last(info, c, cx, width):
    row = spec((1, width))
    return call(
        unpack_last_kernel, "unpack_last", 1, [SCALARS] + [spec(c.shape)] * 2,
        [
            spec((3, 2, BR // 2, width)), spec((9, 2, BR // 2)), spec((2, BR // 2)), spec((4, BR)),
            row, row, row, row, row, row,
        ],
        [
            shaped((3, 2, BR // 2, width), F32), shaped((9, 2, BR // 2), F32), shaped((2, BR // 2), F32),
            shaped((4, BR), F32),
        ] + [shaped((1, width), F32)] * 6,
        [], 1, 16,
    )(info, c, cx)


def after(value, *marks):
    return lax.optimization_barrier((value,) + marks)[0]


def swap_tensor(values):
    return lax.ppermute(values, "tensor", [(0, 1), (1, 0)])


def swap_dp(values, size, mask):
    return lax.ppermute(values, "dp", [(i, i ^ mask) for i in range(size)])


def swap_both(values, size, mask):
    pairs = [(2 * i + t, 2 * (i ^ mask) + 1 - t) for i in range(size) for t in range(2)]
    return lax.ppermute(values, ("dp", "tensor"), pairs)


def add_kernel(count, *refs):
    refs, outs = refs[:count], refs[count:]
    items = [ref[...].astype(F32) for ref in refs]
    while len(items) > 1:
        items = [items[i] + items[i + 1] for i in range(0, len(items), 2)]
    whole = items[0].astype(BF16)
    whole = whole.reshape((len(outs),) + outs[0].shape)
    for at, out in enumerate(outs):
        out[...] = whole[at]


def added(*items, parts=1, marks=()):
    shape = items[0].shape
    last = shape[-2:]
    outs = call(
        partial(add_kernel, len(items)), "add", 1, [spec(shape)] * len(items), [spec(last)] * parts,
        [shaped(last, BF16)] * parts, [], 0.5, 8, marks=len(marks),
    )(*items, *marks)
    return outs[0] if parts == 1 else outs


def partner_groups(size):
    bits = list(range(1, size.bit_length() - 1))
    groups = []
    while bits:
        pair, bits = bits[:2], bits[2:]
        low = 1 << pair[0]
        groups.append([low] if len(pair) == 1 else [low, 1 << pair[1], low | (1 << pair[1])])
    return groups


def per_device(
    size, block_input, heights, widths, norm1_gain, norm1_bias, qkv_weight, lepe_weight, lepe_bias,
    proj_weight, proj_bias, norm2_gain, norm2_bias, fc1_weight, fc1_bias, fc2_weight, fc2_bias,
    cotangent,
):
    images, local_cells, width = block_input.shape
    hidden = fc1_weight.shape[1]
    x_pairs = block_input.reshape(2 * images, PAIR, width)
    cot_pairs = cotangent.reshape(2 * images, PAIR, width)
    gain1, bias1 = norm1_gain[None], norm1_bias[None]
    pairs = range(images)
    index = lax.axis_index("dp")
    places = jnp.stack([lax.axis_index("tensor"), index % 2, index // 2 % 2]).astype(jnp.int32)
    info = jnp.concatenate([widths, places])

    own, own_half = pack_first(
        qkv_weight.transpose(1, 2, 3, 0), lepe_weight.transpose(1, 0, 2), lepe_bias
    )
    near = swap_tensor(own_half)
    far = swap_dp(near, size, 1)
    quad_own, *quad_send = split_quadrants(info, after(x_pairs, own))
    vectors = (fc1_bias, proj_bias, fc2_bias)
    late_own, late_send = pack_late(info, *after((fc1_weight, fc2_weight, proj_weight, vectors), quad_own))
    quad_other = [swap_tensor(quad_send[0])]

    late_near = swap_tensor(late_send)

    def forward_rows(image, mark, known):
        return rows_forward(
            image, after(heights, mark), info, x_pairs, gain1, bias1, (own, near, far), known
        )

    *kept, mixed, weight, weight_t, taps = forward_rows(0, late_own, None)
    row_kept, mixed_rows = [kept], [mixed]
    quad_other += [swap_tensor(after(item, taps)) for item in quad_send[1:]]
    columns = []
    for image in pairs:
        *kept, unit, keep, send = columns_forward(
            image, heights, info, quad_own, quad_other[image], gain1, bias1, weight, taps
        )
        columns.append((kept, unit, keep, swap_tensor(send)))
        if image == 0:
            ready = after(late_near, keep)
            late_parts = [ready] + [swap_dp(ready, size, mask) for mask in (2, 1, 3)]
    for image in range(1, images):
        *kept, mixed = forward_rows(image, columns[-1][2], (weight, taps))
        row_kept.append(kept)
        mixed_rows.append(mixed)
    output, grad_mid, grad_rows, grad_keep, grad_send, small2, kept1, sent1 = mlp(
        heights, info, x_pairs, cot_pairs, mixed_rows, [item[2] for item in columns],
        [item[3] for item in columns], norm2_gain[None], norm2_bias[None], (late_own, *late_parts),
    )
    grad_other = swap_tensor(grad_send)

    arrived = swap_dp(sent1, size, 1)
    bits = size.bit_length() - 1
    row_pairs, row_sums = [], []

    def backward_rows(image, start, count, mark, final=None):
        rows, *rest = rows_backward(
            image, start, count, after(heights, mark), info, x_pairs, grad_rows, row_kept[image],
            weight_t, taps, final,
        )
        row_pairs.append(rows)
        return rest

    for image in range(images - 1):
        row_sums.append(backward_rows(image, 0, 2, small2))
    mark = row_sums[-1][2] if row_sums else small2
    first, toward_x, toward_y, toward_xy = added(kept1, after(arrived, mark), parts=4)
    crossed = [swap_dp(toward_x, size, 2), swap_tensor(toward_y), swap_both(toward_xy, size, 2)]
    mark = first
    column_back = []
    for image in pairs:
        kept, unit, _, _ = columns[image]
        *column_sums, back_keep, back_send = columns_backward(
            image, after(heights, mark), info, grad_keep, grad_other, kept, unit, weight_t, taps
        )
        column_back.append((column_sums, back_keep, swap_tensor(back_send)))
        mark = column_sums[2]
        if image == 0:
            first = added(first, *[after(item, mark) for item in crossed])
        else:
            first = added(first, after(arrived, mark))
        bit = 2 + image
        arrived = swap_dp(first, size, 1 << bit) if bit < bits else jnp.zeros_like(first)
        mark = first
    final = (gain1, bias1, small2, row_sums, [item[0] for item in column_back])
    kept2, sent2 = backward_rows(images - 1, 0, 2, mark, final)

    input_grad = None

    def meanwhile(image, start, count, mark):
        nonlocal input_grad
        _, back_keep, back_other = column_back[image]
        input_grad, mark = input_rows(
            image, start, count, after(heights, mark), info, x_pairs, row_pairs[image], grad_mid,
            back_keep, back_other, weight_t, gain1, input_grad,
        )
        return mark

    first = added(first, arrived, marks=[kept2])
    core_part = swap_dp(after(sent2, first), size, 1)
    last, toward_y = added(kept2, core_part, parts=2, marks=[item[2] for item in column_back])
    for bit in range(2 + images, bits):
        first = added(first, swap_dp(first, size, 1 << bit))
    first_x = swap_dp(first, size, 2)
    across = swap_tensor(toward_y)
    for image in range(images - 1):
        mark = meanwhile(image, 0, 2, last)
    last = added(last, across, marks=[mark])
    for at, group in enumerate(partner_groups(size)):
        arrived = [swap_dp(last, size, mask) for mask in group]
        marks = []
        if at == 0:
            marks = [meanwhile(images - 1, 0, 1, last), first_x]
        if at == 1:
            first_core = [swap_dp(after(item, last), size, 1) for item in (first, first_x)]
            grad_fc1, grad_fc2, grad_proj, mark = unpack_first(
                after(info, last), first, first_x, first_core[0], first_core[1], hidden, width
            )
            marks = [meanwhile(images - 1, 1, 1, last), mark]
        last = added(last, *arrived, marks=marks)
    last_other = swap_dp(last, size, 1)
    (
        grad_qkv, grad_lepe, grad_shift, grad_b1,
        grad_gain1, grad_bias1, grad_gain2, grad_bias2, grad_projb, grad_b2,
    ) = unpack_last(info, last, last_other, width)
    return (
        output.reshape(block_input.shape), input_grad.reshape(block_input.shape),
        grad_gain1[0], grad_bias1[0], grad_qkv.transpose(3, 0, 1, 2), grad_lepe.transpose(1, 0, 2),
        grad_shift, grad_proj.reshape(2, BR // 2, width), grad_projb[0], grad_gain2[0], grad_bias2[0],
        grad_fc1, grad_b1.reshape(-1), grad_fc2, grad_b2[0],
    )


def solution(mesh):
    placed = (
        P("dp", "tensor", None),
        P("dp"),
        P("dp"),
        P(),
        P(),
        P(None, None, None, "tensor"),
        P(None, None, "tensor"),
        P(None, "tensor"),
        P(None, "tensor", None),
        P(),
        P(),
        P(),
        P(None, "tensor"),
        P("tensor"),
        P("tensor", None),
        P(),
        P("dp", "tensor", None),
    )
    return jax.shard_map(
        partial(per_device, mesh.shape["dp"]),
        mesh=mesh,
        in_specs=placed,
        out_specs=(
            P("dp", "tensor", None),
            P("dp", "tensor", None),
            P(),
            P(),
            P(None, None, None, "tensor"),
            P(None, None, "tensor"),
            P(None, "tensor"),
            P(None, "tensor", None),
            P(),
            P(),
            P(),
            P(None, "tensor"),
            P("tensor"),
            P("tensor", None),
            P(),
        ),
        check_vma=False,
    )
```
